32 devices in a mesh: row: 2 (over x), col: 4 (over y, core), depth: 4 (over z).
Axes of the slice: x: 2, y: 2, z: 4, core: 2. Of those that a mesh axis runs over, the one named last changes fastest.
Arguments:
- tokens: bfloat16 [768, 8192], P(('depth', 'col'), 'row'), may hold values from -6 to 6
- gate_weight: bfloat16 [8192, 14336], P('row', ('col', 'depth')), may hold values from -0.0625 to 0.0625
- up_weight: bfloat16 [8192, 14336], P('row', ('col', 'depth')), may hold values from -0.0625 to 0.0625
- down_weight: bfloat16 [14336, 8192], P(('col', 'depth'), 'row'), may hold values from -0.046875 to 0.046875
- cotangent: bfloat16 [768, 8192], P(('depth', 'col'), 'row'), may hold values from -0.86328125 to 0.86328125
Outputs:
- mixed: float32 [768, 8192], P(('depth', 'col'), 'row')
- token_grad: float32 [768, 8192], P(('depth', 'col'), 'row')
- gate_weight_grad: float32 [8192, 14336], P('row', ('col', 'depth'))
- up_weight_grad: float32 [8192, 14336], P('row', ('col', 'depth'))
- down_weight_grad: float32 [14336, 8192], P(('col', 'depth'), 'row')
The draws below stay inside these ranges and needn't reach their ends.
All inputs are finite; a program needn't handle non-finite values.
Results may differ from the reference program's by a relative error of at most 0.012.
Values may be sent and summed in bfloat16 or wider, within the bound.
No kernel may reach another device: no remote copies, remote signals or barrier semaphores. Data moves between devices by JAX's collectives and lax.ppermute only.
A program may use at most 384 MiB of HBM per device.

```python
import jax
import jax.numpy as jnp
from jax import lax

D = 8192
FF = 14336
TOK_L = 192
TOKENS = 768
N_DEPTH = 4


def block_levels(rng, dims, cuts, smallest, high):
    def one(dim, shards_of):
        draws = jax.random.uniform(jax.random.fold_in(jax.random.fold_in(rng, 6), dim), (shards_of,), jnp.float32, smallest / len(cuts), high / len(cuts))
        return jnp.repeat(jnp.exp(draws), dims[dim] // shards_of).reshape((-1,) + (1,) * (len(dims) - dim - 1))

    gain = one(*cuts[0])
    for cut in cuts[1:]:
        gain = gain * one(*cut)
    return gain


def normal_values(key, extent, spread, bound, pieces=(), held_as=jnp.bfloat16):
    factor_of = block_levels(key, extent, pieces, -0.22, 0.18) if pieces else 1.0
    result = jax.random.normal(key, extent, jnp.float32) * spread * factor_of
    return jnp.minimum(jnp.maximum(result, -bound), bound).astype(held_as)


def setup_inputs(seed: int = 0) -> dict:
    seeds = jax.random.split(jax.random.key(seed), 6)
    tokens = normal_values(seeds[0], (TOKENS, D), 1.0, 6.0, ((0, 16), (1, 2)))
    gate_weight = normal_values(seeds[1], (D, FF), D ** -0.5, 0.0625, ((0, 2), (1, 16)))
    up_weight = normal_values(seeds[2], (D, FF), D ** -0.5, 0.0625, ((0, 2), (1, 16)))
    down_weight = normal_values(seeds[3], (FF, D), FF ** -0.5, 0.046875, ((0, 16), (1, 2)))
    cotangent = normal_values(seeds[4], (TOKENS, D), (4.0 / TOKENS ** 0.5), 0.86328125, ((0, 16), (1, 2)))
    return dict(tokens=tokens, gate_weight=gate_weight, up_weight=up_weight, down_weight=down_weight, cotangent=cotangent)


def swish_parts(gate):
    sigma_gate = jax.nn.sigmoid(gate)
    return gate * sigma_gate, sigma_gate


def rounded_sum(total, left_side, right_side):
    partial_term = jnp.dot(left_side.T, right_side, preferred_element_type=jnp.float32).astype(jnp.bfloat16)
    return total + lax.optimization_barrier(partial_term).astype(jnp.float32)


def reference(tokens, gate_weight, up_weight, down_weight, cotangent):
    gate = jnp.dot(tokens, gate_weight, preferred_element_type=jnp.float32)
    up_full = jnp.dot(tokens, up_weight, preferred_element_type=jnp.float32)
    activated, sigma_gate = swish_parts(gate)
    hidden = (activated * up_full).astype(jnp.bfloat16)
    mixed = jnp.dot(hidden, down_weight, preferred_element_type=jnp.float32)
    hidden_grad = jnp.dot(cotangent, down_weight.T, preferred_element_type=jnp.float32)
    gate_grad = (hidden_grad * up_full * sigma_gate * (1.0 + gate * (1.0 - sigma_gate))).astype(jnp.bfloat16)
    up_grad = (hidden_grad * activated).astype(jnp.bfloat16)
    token_grad = (jnp.dot(gate_grad, gate_weight.T, preferred_element_type=jnp.float32)
                  + jnp.dot(up_grad, up_weight.T, preferred_element_type=jnp.float32))
    gate_total = jnp.zeros((D, FF), jnp.float32)
    up_total = jnp.zeros((D, FF), jnp.float32)
    down_total = jnp.zeros((FF, D), jnp.float32)
    for layer_index in range(N_DEPTH):
        first_row = layer_index * TOK_L
        last_row = first_row + TOK_L
        tokens_layer = tokens[first_row:last_row]
        gate_total = rounded_sum(gate_total, tokens_layer, gate_grad[first_row:last_row])
        up_total = rounded_sum(up_total, tokens_layer, up_grad[first_row:last_row])
        down_total = rounded_sum(down_total, hidden[first_row:last_row], cotangent[first_row:last_row])
    return (mixed, token_grad, gate_total, up_total, down_total)
```

```python
import jax
import jax.numpy as jnp
from jax import lax
from jax.sharding import PartitionSpec as P

TOKEN_AXES = ("depth", "col")


def dot(left, right, left_dim, right_dim):
    return lax.dot_general(
        left, right, (((left_dim,), (right_dim,)), ((), ())), preferred_element_type=jnp.float32
    )


def row_sum(partial):
    n = lax.axis_size("row")
    sent = partial.astype(jnp.bfloat16)
    total = partial
    for step in range(1, n):
        moved = lax.ppermute(sent, "row", [(i, (i + step) % n) for i in range(n)])
        total = total + moved.astype(jnp.float32)
    return total


def token_scatter(partial):
    return lax.psum_scatter(
        partial.astype(jnp.bfloat16), TOKEN_AXES, scatter_dimension=0, tiled=True
    ).astype(jnp.float32)


def body(tokens, gate_weight, up_weight, down_weight, cotangent):
    token_all = lax.all_gather(tokens, TOKEN_AXES, axis=0, tiled=True)
    cotangent_all = lax.all_gather(cotangent, TOKEN_AXES, axis=0, tiled=True)
    gate = row_sum(dot(token_all, gate_weight, 1, 0))
    up = row_sum(dot(token_all, up_weight, 1, 0))
    hidden_grad = row_sum(dot(cotangent_all, down_weight, 1, 1))
    sigma = jax.nn.sigmoid(gate)
    activated = gate * sigma
    hidden = (activated * up).astype(jnp.bfloat16)
    mixed = token_scatter(dot(hidden, down_weight, 1, 0))
    gate_grad = (hidden_grad * up * sigma * (1.0 + gate * (1.0 - sigma))).astype(jnp.bfloat16)
    up_grad = (hidden_grad * activated).astype(jnp.bfloat16)
    token_grad = token_scatter(
        dot(gate_grad, gate_weight, 1, 1) + dot(up_grad, up_weight, 1, 1)
    )
    gate_total = dot(token_all, gate_grad, 0, 0)
    up_total = dot(token_all, up_grad, 0, 0)
    down_total = dot(hidden, cotangent_all, 0, 0)
    return (mixed, token_grad, gate_total, up_total, down_total)


def solution(mesh):
    activations = P(("depth", "col"), "row")
    wide = P("row", ("col", "depth"))
    tall = P(("col", "depth"), "row")
    return jax.shard_map(
        body,
        mesh=mesh,
        in_specs=(activations, wide, wide, tall, activations),
        out_specs=(activations, activations, wide, wide, tall),
        check_vma=False,
    )
```

```python
import jax
import jax.numpy as jnp
from jax import lax
from jax.sharding import PartitionSpec as P

CORE, CHIP = 1, 2


def dot(left, right, left_dim, right_dim):
    return lax.dot_general(
        left, right, (((left_dim,), (right_dim,)), ((), ())), preferred_element_type=jnp.float32
    )


def after(array, *others):
    return lax.optimization_barrier((array, *others))[0]


def shift(block, step):
    n = lax.axis_size("depth")
    return lax.ppermute(block, "depth", [(i, (i + step) % n) for i in range(n)])


def swap(block, bit):
    n = lax.axis_size("col")
    return lax.ppermute(block, "col", [(i, i ^ bit) for i in range(n)])


def row_sum(partial):
    n = lax.axis_size("row")
    sent = partial.astype(jnp.bfloat16)
    total = partial
    for step in range(1, n):
        moved = lax.ppermute(sent, "row", [(i, (i + step) % n) for i in range(n)])
        total = total + moved.astype(jnp.float32)
    return total


def gather(shard, hold=None):
    near = [shard] + [shift(shard, k) for k in range(1, lax.axis_size("depth"))]
    mine = jnp.concatenate(near, axis=0)
    first = jnp.concatenate([mine, swap(mine, CORE)], axis=0)
    passed = near if hold is None else [near[0]] + hold(near[1:], first)
    mine = jnp.concatenate([swap(block, CHIP) for block in passed], axis=0)
    second = jnp.concatenate([mine, swap(mine, CORE)], axis=0)
    return first, second, near


def scatter(near, far):
    n = lax.axis_size("depth")
    half = near.shape[0] // 2
    size = half // n

    def wide(block):
        return block.astype(jnp.float32)

    far_core = swap(far[half:], CORE)
    near_core = swap(near[half:], CORE)
    total, to_chip, to_depth = None, [], []
    for k in reversed(range(n)):
        rows = slice(k * size, (k + 1) * size)
        far_sum = (wide(far[rows]) + wide(far_core[rows])).astype(jnp.bfloat16)
        to_chip.append(far_sum)
        block = wide(near[rows]) + wide(near_core[rows]) + wide(swap(far_sum, CHIP))
        if k:
            sent = block.astype(jnp.bfloat16)
            to_depth.append(sent)
            block = wide(shift(sent, -k))
        total = block if total is None else total + block
    return total, to_chip, to_depth


def body(tokens, gate_weight, up_weight, down_weight, cotangent):
    token_first, token_second, token_near = gather(tokens)
    gate_first = dot(token_first, gate_weight, 1, 0)
    up_first = dot(token_first, up_weight, 1, 0)
    gates, ups = [row_sum(gate_first)], [row_sum(up_first)]

    def hold(blocks, first):
        return list(lax.optimization_barrier((*blocks, gate_first, up_first))[: len(blocks)])

    cotangent_first, cotangent_second, _ = gather(after(cotangent, *token_near), hold)
    gates.append(row_sum(dot(token_second, gate_weight, 1, 0)))
    ups.append(row_sum(dot(token_second, up_weight, 1, 0)))
    hidden_grads = [
        row_sum(dot(group, down_weight, 1, 1)) for group in (cotangent_first, cotangent_second)
    ]
    hiddens, mixes = [], []
    for gate, up in zip(gates, ups):
        hidden = (gate * jax.nn.sigmoid(gate) * up).astype(jnp.bfloat16)
        hiddens.append(hidden)
        mixes.append(dot(hidden, down_weight, 1, 0).astype(jnp.bfloat16))
    mixed, to_chip, _ = scatter(*mixes)
    cotangent_all = jnp.concatenate([cotangent_first, cotangent_second], axis=0)
    hidden_all = after(jnp.concatenate(hiddens, axis=0), *to_chip)
    down_total = dot(hidden_all, cotangent_all, 0, 0)
    gate_grads, up_grads, token_grads = [], [], []
    for gate, up, hidden_grad in zip(gates, ups, hidden_grads):
        sigma = jax.nn.sigmoid(gate)
        gate_grad = (hidden_grad * up * sigma * (1.0 + gate * (1.0 - sigma))).astype(jnp.bfloat16)
        up_grad = (hidden_grad * (gate * sigma)).astype(jnp.bfloat16)
        gate_grads.append(gate_grad)
        up_grads.append(up_grad)
        token_grads.append(
            (dot(gate_grad, gate_weight, 1, 1) + dot(up_grad, up_weight, 1, 1)).astype(jnp.bfloat16)
        )
    token_grad, to_chip, to_depth = scatter(*token_grads)
    token_all = jnp.concatenate([token_first, token_second], axis=0)
    gate_total = dot(token_all, after(jnp.concatenate(gate_grads, axis=0), *to_chip), 0, 0)
    up_total = dot(token_all, after(jnp.concatenate(up_grads, axis=0), *to_depth), 0, 0)
    return (mixed, token_grad, gate_total, up_total, down_total)


def solution(mesh):
    activations = P(("depth", "col"), "row")
    wide = P("row", ("col", "depth"))
    tall = P(("col", "depth"), "row")
    return jax.shard_map(
        body,
        mesh=mesh,
        in_specs=(activations, wide, wide, tall, activations),
        out_specs=(activations, activations, wide, wide, tall),
        check_vma=False,
    )
```

```python
import functools

import jax
import jax.numpy as jnp
from jax import lax
from jax.experimental import pallas as pl
from jax.experimental.pallas import tpu as pltpu
from jax.sharding import PartitionSpec as P

CORE, CHIP = 1, 2
PARTS = 3
VMEM_BYTES = 56 * 1024 * 1024


def dot(left, right, left_dim, right_dim):
    return lax.dot_general(
        left, right, (((left_dim,), (right_dim,)), ((), ())), preferred_element_type=jnp.float32
    )


def after(array, *others):
    return lax.optimization_barrier((array, *others))[0]


def wide(block):
    return block.astype(jnp.float32)


def narrow(block):
    return block.astype(jnp.bfloat16)


def contract_kernel(n_pieces, n_weights, right_dim, *refs):
    pieces, weights = refs[:n_pieces], refs[n_pieces : n_pieces + n_weights]
    outs, total = refs[n_pieces + n_weights : -1], refs[-1]
    step = pl.program_id(0)

    @pl.when(step == 0)
    def _():
        total[...] = jnp.zeros_like(total)

    rows = jnp.concatenate([piece[...] for piece in pieces], axis=0)
    for i, weight in enumerate(weights):
        total[i] += dot(rows, weight[...], 1, right_dim)

    @pl.when(step == pl.num_programs(0) - 1)
    def _():
        size = outs[0].shape[0]
        for i, out in enumerate(outs):
            group, weight = divmod(i, n_weights)
            out[...] = narrow(total[weight, group * size : (group + 1) * size])


def contract(groups, weights, right_dim):
    pieces = sum(groups, [])
    arrays = [array for array, _ in pieces]
    size, width = arrays[0].shape[1:]
    units = weights[0].shape[1 - right_dim]
    block = min(1024, width)
    if right_dim == 0:
        weight_spec = pl.BlockSpec((block, units), lambda k: (k, 0))
    else:
        weight_spec = pl.BlockSpec((units, block), lambda k: (0, k))
    shape = (size * len(groups[0]), units)
    n_outs = len(groups) * len(weights)
    return pl.pallas_call(
        functools.partial(contract_kernel, len(pieces), len(weights), right_dim),
        grid=(width // block,),
        in_specs=[
            pl.BlockSpec((None, size, block), lambda k, index=index: (index, 0, k))
            for _, index in pieces
        ]
        + [weight_spec] * len(weights),
        out_specs=[pl.BlockSpec(shape, lambda k: (0, 0))] * n_outs,
        out_shape=[jax.ShapeDtypeStruct(shape, jnp.bfloat16)] * n_outs,
        scratch_shapes=[pltpu.VMEM((len(weights), size * len(pieces), units), jnp.float32)],
        compiler_params=pltpu.CompilerParams(vmem_limit_bytes=VMEM_BYTES),
        cost_estimate=pl.CostEstimate(flops=1000, bytes_accessed=1000, transcendentals=0),
    )(*arrays, *weights)


def expand_kernel(n, right_dim, *refs):
    lefts, weights, outs = refs[:n], refs[n : 2 * n], refs[2 * n :]
    total = sum(dot(left[...], weight[...], 1, right_dim) for left, weight in zip(lefts, weights))
    half = total.shape[0] // 2
    outs[0][...] = narrow(total[:half])
    outs[1][...] = narrow(total[half:])


def expand(lefts, weights, right_dim):
    rows, units = lefts[0].shape
    width = weights[0].shape[1 - right_dim]
    block = min(512, width)
    if right_dim == 0:
        weight_spec = pl.BlockSpec((units, block), lambda j: (0, j))
    else:
        weight_spec = pl.BlockSpec((block, units), lambda j: (j, 0))
    out = jax.ShapeDtypeStruct((rows // 2, width), jnp.bfloat16)
    halves = pl.pallas_call(
        functools.partial(expand_kernel, len(lefts), right_dim),
        grid=(width // block,),
        in_specs=[pl.BlockSpec((rows, units), lambda j: (0, 0))] * len(lefts)
        + [weight_spec] * len(weights),
        out_specs=[pl.BlockSpec((rows // 2, block), lambda j: (0, j))] * 2,
        out_shape=[out, out],
        compiler_params=pltpu.CompilerParams(vmem_limit_bytes=VMEM_BYTES),
        cost_estimate=pl.CostEstimate(flops=1000, bytes_accessed=1000, transcendentals=0),
    )(*lefts, *weights)
    return list(halves)


def swap(block, bit):
    n = lax.axis_size("col")
    return lax.ppermute(block, "col", [(i, i ^ bit) for i in range(n)])


def row_moves(partial):
    n = lax.axis_size("row")
    return [
        lax.ppermute(partial, "row", [(i, (i + step) % n) for i in range(n)])
        for step in range(1, n)
    ]


def row_sum(partial, moved, *others):
    return sum([wide(after(block, *others)) for block in moved], wide(partial))


def line_gather(*shards):
    return lax.all_gather(jnp.stack(shards), "depth", axis=1, tiled=True)


def line_scatter(line):
    return wide(lax.psum_scatter(line, "depth", scatter_dimension=0, tiled=True))


def cut(array, part):
    tiles = array.shape[1] // 128
    first, last = (128 * (tiles * i // PARTS) for i in (part, part + 1))
    return array[:, first:last]


def add(*blocks):
    return narrow(sum(wide(block) for block in blocks))


def grads_of(gate, up, hidden_grad):
    sigma = jax.nn.sigmoid(gate)
    gate_grad = narrow(hidden_grad * up * sigma * (1.0 + gate * (1.0 - sigma)))
    return gate_grad, narrow(hidden_grad * (gate * sigma))


def hidden_of(gate, up):
    return narrow(gate * jax.nn.sigmoid(gate) * up)


def body(tokens, gate_weight, up_weight, down_weight, cotangent):
    cotangent_next = swap(cotangent, CHIP)
    token_near = after(line_gather(tokens), cotangent_next)
    cotangents = line_gather(after(cotangent, token_near), after(cotangent_next, token_near))
    token_far = swap(token_near, CHIP)
    token_near = [token_near, swap(token_near, CORE)]

    pieces = [(array, 0) for array in token_near]
    (gate_near,) = contract([pieces], [gate_weight], 0)
    gate_moved = row_moves(gate_near)
    pieces[0] = (after(token_near[0], gate_near), 0)
    (up_near,) = contract([pieces], [up_weight], 0)
    up_moved = row_moves(after(up_near, *gate_moved))

    token_far = after(token_far, *up_moved)
    token_far = [token_far, swap(token_far, CORE)]
    gate_near, up_near = row_sum(gate_near, gate_moved), row_sum(up_near, up_moved)
    hidden_near = hidden_of(gate_near, up_near)
    pieces = [(after(token_far[0], hidden_near), 0), (token_far[1], 0)]
    gate_far, up_far = contract([pieces], [gate_weight, up_weight], 0)
    gate_moved = row_moves(gate_far)

    mixed_near = expand([after(hidden_near, up_far)], [down_weight], 0)
    mixed_near[1] = swap(mixed_near[1], CORE)
    cotangents = after(cotangents, up_far)
    cotangents = [cotangents, swap(cotangents, CORE)]
    first = after(cotangents[0], *gate_moved, *mixed_near[:1])
    up_moved = row_moves(after(up_far, *gate_moved))
    groups = [[(first, i), (cotangents[1], i)] for i in (1, 0)]
    grad_far, grad_near = contract(groups, [down_weight], 1)
    mixed_near = add(mixed_near[0], after(mixed_near[1], grad_far))

    gate_far = row_sum(gate_far, gate_moved)
    up_far = row_sum(up_far, up_moved, grad_far, mixed_near)
    mixed_near = line_scatter(mixed_near)
    grad_far_moved = row_moves(after(grad_far, *up_moved))
    hidden_far = hidden_of(gate_far, up_far)
    mixed_far = expand([hidden_far], [down_weight], 0)
    mixed_far[1] = swap(mixed_far[1], CORE)
    grad_far = row_sum(grad_far, grad_far_moved, mixed_far[0])
    grad_near_moved = row_moves(after(grad_near, *grad_far_moved))
    far_grads = grads_of(gate_far, up_far, grad_far)
    mine, other = expand(far_grads, [gate_weight, up_weight], 1)
    mixed_far = add(mixed_far[0], after(mixed_far[1], mine))
    other = swap(after(other, mixed_far, *grad_near_moved), CORE)
    mixed_far = line_scatter(mixed_far)

    far_sums = [add(cut(mine, 0), cut(other, 0))]
    grad_near = row_sum(grad_near, grad_near_moved, *far_sums)
    near_grads = grads_of(gate_near, up_near, grad_near)
    for part in range(1, PARTS):
        far_sums.append(add(cut(mine, part), cut(after(other, *near_grads), part)))
    token_all = jnp.concatenate([array[0] for array in token_near + token_far], axis=0)
    cotangent_all = jnp.concatenate([array[i] for i in (0, 1) for array in cotangents], axis=0)
    gate_grad, up_grad = (jnp.concatenate(pair, axis=0) for pair in zip(near_grads, far_grads))
    hidden = jnp.concatenate([hidden_near, hidden_far], axis=0)

    moved = swap(far_sums[0], CHIP)
    mine, other = expand(near_grads, [gate_weight, up_weight], 1)
    other = swap(other, CORE)
    lines = [add(cut(mine, 0), cut(other, 0), after(moved, mine))]
    moved = swap(after(far_sums[1], moved), CHIP)
    gate_total = dot(token_all, after(gate_grad, *lines), 0, 0)
    lines.append(add(cut(mine, 1), cut(other, 1), after(moved, gate_total)))
    moved = swap(after(far_sums[2], moved, gate_total), CHIP)
    up_total = dot(token_all, after(up_grad, *lines), 0, 0)
    lines.append(add(cut(mine, 2), cut(other, 2), after(moved, up_total)))
    down_total = dot(after(hidden, *lines), cotangent_all, 0, 0)
    mixed = mixed_near + wide(swap(after(narrow(mixed_far), *lines), CHIP))
    token_grad = jnp.concatenate([line_scatter(line) for line in lines], axis=1)
    return (mixed, token_grad, gate_total, up_total, down_total)


def solution(mesh):
    activations = P(("depth", "col"), "row")
    wide_weight = P("row", ("col", "depth"))
    tall_weight = P(("col", "depth"), "row")
    return jax.shard_map(
        body,
        mesh=mesh,
        in_specs=(activations, wide_weight, wide_weight, tall_weight, activations),
        out_specs=(activations, activations, wide_weight, wide_weight, tall_weight),
        check_vma=False,
    )
```

```python
import functools

import jax
import jax.numpy as jnp
from jax import lax
from jax.experimental import pallas as pl
from jax.experimental.pallas import tpu as pltpu
from jax.sharding import PartitionSpec as P

CORE, CHIP = 1, 2
VMEM_BYTES = 56 * 1024 * 1024


def dot(left, right, left_dim, right_dim):
    return lax.dot_general(
        left, right, (((left_dim,), (right_dim,)), ((), ())), preferred_element_type=jnp.float32
    )


def after(array, *others):
    return lax.optimization_barrier((array, *others))[0]


def wide(block):
    return block.astype(jnp.float32)


def narrow(block):
    return block.astype(jnp.bfloat16)


def cost(flops, *arrays):
    moved = sum(array.size * array.dtype.itemsize for array in arrays)
    return pl.CostEstimate(flops=flops, bytes_accessed=moved, transcendentals=0)


def contract_kernel(n_pieces, n_weights, right_dim, *refs):
    pieces, weights = refs[:n_pieces], refs[n_pieces : n_pieces + n_weights]
    outs, total = refs[n_pieces + n_weights : -1], refs[-1]
    step = pl.program_id(0)

    @pl.when(step == 0)
    def _():
        total[...] = jnp.zeros_like(total)

    rows = jnp.concatenate([piece[...] for piece in pieces], axis=0)
    for i, weight in enumerate(weights):
        total[i] += dot(rows, weight[...], 1, right_dim)

    @pl.when(step == pl.num_programs(0) - 1)
    def _():
        size = outs[0].shape[0]
        for i, out in enumerate(outs):
            part, weight = divmod(i, n_weights)
            out[...] = narrow(total[weight, part * size : (part + 1) * size])


def contract(pieces, weights, right_dim, parts=1):
    width = pieces[0].shape[1]
    units = weights[0].shape[1 - right_dim]
    block = min(1024, width)
    if right_dim == 0:
        weight_spec = pl.BlockSpec((block, units), lambda k: (k, 0))
    else:
        weight_spec = pl.BlockSpec((units, block), lambda k: (0, k))
    rows = sum(piece.shape[0] for piece in pieces)
    out = jax.ShapeDtypeStruct((rows // parts, units), jnp.bfloat16)
    n_outs = parts * len(weights)
    return pl.pallas_call(
        functools.partial(contract_kernel, len(pieces), len(weights), right_dim),
        grid=(width // block,),
        in_specs=[pl.BlockSpec((piece.shape[0], block), lambda k: (0, k)) for piece in pieces]
        + [weight_spec] * len(weights),
        out_specs=[pl.BlockSpec(out.shape, lambda k: (0, 0))] * n_outs,
        out_shape=[out] * n_outs,
        scratch_shapes=[pltpu.VMEM((len(weights), rows, units), jnp.float32)],
        compiler_params=pltpu.CompilerParams(vmem_limit_bytes=VMEM_BYTES),
        cost_estimate=cost(2 * len(weights) * rows * width * units, *pieces, *weights),
    )(*pieces, *weights)


def expand_kernel(n, right_dim, *refs):
    lefts, weights, outs = refs[:n], refs[n : 2 * n], refs[2 * n :]
    total = sum(dot(left[...], weight[...], 1, right_dim) for left, weight in zip(lefts, weights))
    half = total.shape[0] // 2
    outs[0][...] = narrow(total[:half])
    outs[1][...] = narrow(total[half:])


def expand(lefts, weights, right_dim):
    rows, units = lefts[0].shape
    width = weights[0].shape[1 - right_dim]
    block = min(512, width)
    if right_dim == 0:
        weight_spec = pl.BlockSpec((units, block), lambda j: (0, j))
    else:
        weight_spec = pl.BlockSpec((block, units), lambda j: (j, 0))
    out = jax.ShapeDtypeStruct((rows // 2, width), jnp.bfloat16)
    return pl.pallas_call(
        functools.partial(expand_kernel, len(lefts), right_dim),
        grid=(width // block,),
        in_specs=[pl.BlockSpec((rows, units), lambda j: (0, 0))] * len(lefts)
        + [weight_spec] * len(weights),
        out_specs=[pl.BlockSpec((rows // 2, block), lambda j: (0, j))] * 2,
        out_shape=[out, out],
        compiler_params=pltpu.CompilerParams(vmem_limit_bytes=VMEM_BYTES),
        cost_estimate=cost(2 * len(lefts) * rows * width * units, *lefts, *weights, out, out),
    )(*lefts, *weights)


def wide_grad_kernel(n_pieces, *refs):
    pieces, grads, outs = refs[:n_pieces], refs[n_pieces:-2], refs[-2:]
    rows = jnp.concatenate([piece[...] for piece in pieces], axis=0)
    half = len(grads) // 2
    for i, out in enumerate(outs):
        grad = jnp.concatenate([grad[...] for grad in grads[i * half : (i + 1) * half]], axis=0)
        out[...] = dot(rows, grad, 0, 0)


def wide_grads(pieces, gate_grads, up_grads):
    grads = [*gate_grads, *up_grads]
    width, units = pieces[0].shape[1], grads[0].shape[1]
    block = min(512, width)
    rows = sum(piece.shape[0] for piece in pieces)
    out = jax.ShapeDtypeStruct((width, units), jnp.float32)
    return pl.pallas_call(
        functools.partial(wide_grad_kernel, len(pieces)),
        grid=(width // block,),
        in_specs=[pl.BlockSpec((piece.shape[0], block), lambda j: (0, j)) for piece in pieces]
        + [pl.BlockSpec(grad.shape, lambda j: (0, 0)) for grad in grads],
        out_specs=[pl.BlockSpec((block, units), lambda j: (j, 0))] * 2,
        out_shape=[out, out],
        compiler_params=pltpu.CompilerParams(vmem_limit_bytes=VMEM_BYTES),
        cost_estimate=cost(4 * rows * width * units, *pieces, *grads, out, out),
    )(*pieces, *grads)


def tall_grad_kernel(n_pieces, *refs):
    pieces, hiddens, out = refs[:n_pieces], refs[n_pieces:-1], refs[-1]
    rows = jnp.concatenate([piece[...] for piece in pieces], axis=0)
    hidden = jnp.concatenate([hidden[...] for hidden in hiddens], axis=0)
    out[...] = dot(hidden, rows, 0, 0)


def tall_grad(pieces, hiddens):
    width, units = pieces[0].shape[1], hiddens[0].shape[1]
    block = min(512, width)
    rows = sum(piece.shape[0] for piece in pieces)
    out = jax.ShapeDtypeStruct((units, width), jnp.float32)
    return pl.pallas_call(
        functools.partial(tall_grad_kernel, len(pieces)),
        grid=(width // block,),
        in_specs=[pl.BlockSpec((piece.shape[0], block), lambda j: (0, j)) for piece in pieces]
        + [pl.BlockSpec(hidden.shape, lambda j: (0, 0)) for hidden in hiddens],
        out_specs=pl.BlockSpec((units, block), lambda j: (0, j)),
        out_shape=out,
        compiler_params=pltpu.CompilerParams(vmem_limit_bytes=VMEM_BYTES),
        cost_estimate=cost(2 * rows * width * units, *pieces, *hiddens, out),
    )(*pieces, *hiddens)


def shift(block, step):
    n = lax.axis_size("depth")
    return lax.ppermute(block, "depth", [(i, (i + step) % n) for i in range(n)])


def swap(block, bit):
    n = lax.axis_size("col")
    return lax.ppermute(block, "col", [(i, i ^ bit) for i in range(n)])


def row_moves(partial):
    n = lax.axis_size("row")
    return [
        lax.ppermute(partial, "row", [(i, (i + step) % n) for i in range(n)])
        for step in range(1, n)
    ]


def row_sum(partial, moved, *others):
    return sum([wide(after(block, *others)) for block in moved], wide(partial))


def add(*blocks):
    return narrow(sum(wide(block) for block in blocks))


def grads_of(gate, up, hidden_grad):
    sigma = jax.nn.sigmoid(gate)
    gate_grad = narrow(hidden_grad * up * sigma * (1.0 + gate * (1.0 - sigma)))
    return gate_grad, narrow(hidden_grad * (gate * sigma))


def hidden_of(gate, up):
    return narrow(gate * jax.nn.sigmoid(gate) * up)


def sync(*arrays):
    return lax.optimization_barrier(arrays)


def other_cores(blocks):
    return [swap(block, CORE) for block in blocks]


def chip_part(mine, moved):
    half = mine.shape[0] // 2
    return add(mine[half:], moved[half:]), (mine[:half], moved[:half])


def owner_parts(kept, moved):
    size = moved.shape[0] // 2
    rows = [slice(0, size), slice(size, 2 * size)]
    return [sum(wide(block[at]) for block in (*kept, moved)) for at in rows]


def body(tokens, gate_weight, up_weight, down_weight, cotangent):
    near1, far0, core0 = sync(shift(tokens, 1), swap(tokens, CHIP), swap(tokens, CORE))

    near3, far1, *moved = sync(
        shift(after(tokens, near1), 3), swap(near1, CHIP), *other_cores([near1, far0])
    )
    token_a = [tokens, near1, far0, far1, core0, *moved, swap(far1, CORE)]

    near2, far3 = shift(after(near1, near3), 1), swap(near3, CHIP)
    (gate_a,) = contract(token_a, [gate_weight], 0)
    near2, far3, gate_a = sync(near2, far3, gate_a)

    gate_moved = row_moves(gate_a)
    far2, cot_near1 = swap(near2, CHIP), shift(after(cotangent, near2), 1)
    (up_a,) = contract([after(tokens, gate_a), *token_a[1:]], [up_weight], 0)
    far2, cot_near1, up_a, *gate_moved = sync(far2, cot_near1, up_a, *gate_moved)
    gate_a = row_sum(gate_a, gate_moved)

    up_moved = row_moves(up_a)
    token_b = [near3, near2, far3, far2]
    token_b += other_cores(after(block, up_a) for block in token_b)
    cot = after(cotangent, cot_near1)
    cot_far0, cot_far1, cot_near3 = swap(cot, CHIP), swap(cot_near1, CHIP), shift(cot, 3)
    gate_b, up_b = contract(token_b, [gate_weight, up_weight], 0)
    cot_far0, cot_far1, cot_near3, gate_b, up_b, *up_moved = sync(
        cot_far0, cot_far1, cot_near3, gate_b, up_b, *up_moved
    )
    up_a = row_sum(up_a, up_moved)
    hidden_a = hidden_of(gate_a, up_a)

    gate_moved = row_moves(gate_b)
    cot_near2, cot_far3 = shift(after(cot_near1, cot_near3), 1), swap(cot_near3, CHIP)
    mine, other = expand([hidden_a], [down_weight], 0)
    cot_near2, cot_far3, mine, other, *gate_moved = sync(
        cot_near2, cot_far3, mine, other, *gate_moved
    )
    gate_b = row_sum(gate_b, gate_moved)

    up_moved = row_moves(after(up_b, mine))
    cot_far2 = swap(cot_near2, CHIP)
    other = swap(other, CORE)
    cots = [after(cotangent, mine), cot_near1, cot_far0, cot_far1]
    cots += other_cores(after(block, mine) for block in cots)
    cots += [cot_near3, cot_near2, cot_far3, cot_far2]
    cots += other_cores(after(block, mine) for block in cots[8:])
    grad_a, grad_b = contract(cots, [down_weight], 1, parts=2)
    other, grad_a, grad_b, *up_moved = sync(other, grad_a, grad_b, *up_moved)
    up_b = row_sum(up_b, up_moved)
    hidden_b = hidden_of(gate_b, up_b)

    grad_b_moved = row_moves(grad_b)
    sent, mixed_a = chip_part(mine, other)
    mixed_a_moved = swap(sent, CHIP)
    mine, other = expand([hidden_b], [down_weight], 0)
    mixed_a_moved, mine, other, *grad_b_moved = sync(mixed_a_moved, mine, other, *grad_b_moved)
    grad_b = row_sum(grad_b, grad_b_moved)

    grad_a_moved = row_moves(after(grad_a, mine))
    sent, mixed_b = chip_part(mine, swap(other, CORE))
    mixed_b_moved = swap(sent, CHIP)
    mixed_a = owner_parts(mixed_a, mixed_a_moved)
    part1 = shift(narrow(mixed_a[1]), -1)
    grads_b = grads_of(gate_b, up_b, grad_b)
    mine, other = expand(grads_b, [gate_weight, up_weight], 1)
    mine, other, mixed_b_moved, part1, *grad_a_moved = sync(
        mine, other, mixed_b_moved, part1, *grad_a_moved
    )
    grad_a = row_sum(grad_a, grad_a_moved)

    sent, token_grad_b = chip_part(mine, swap(other, CORE))
    token_b_moved = swap(sent, CHIP)
    mixed_b = owner_parts(mixed_b, mixed_b_moved)
    part3, part2 = (shift(narrow(part), -k) for part, k in zip(mixed_b, (3, 2)))
    grads_a = grads_of(gate_a, up_a, grad_a)
    mine, other = expand(grads_a, [gate_weight, up_weight], 1)
    mine, other, token_b_moved, part2, part3 = sync(mine, other, token_b_moved, part2, part3)
    mixed = sum((wide(part) for part in (part1, part2, part3)), mixed_a[0])

    sent, token_grad_a = chip_part(mine, swap(other, CORE))
    token_a_moved = swap(sent, CHIP)
    token_grad_b = owner_parts(token_grad_b, token_b_moved)
    part3, part2 = (shift(narrow(part), -k) for part, k in zip(token_grad_b, (3, 2)))
    gate_total, up_total = wide_grads(
        [after(token_a[0], sent), *token_a[1:], *token_b],
        [grads_a[0], grads_b[0]],
        [grads_a[1], grads_b[1]],
    )
    token_a_moved, part2, part3, gate_total, up_total = sync(
        token_a_moved, part2, part3, gate_total, up_total
    )

    token_grad_a = owner_parts(token_grad_a, token_a_moved)
    part1 = shift(narrow(token_grad_a[1]), -1)
    down_total = tall_grad(cots, [after(hidden_a, gate_total), hidden_b])
    part1, down_total = sync(part1, down_total)
    token_grad = sum((wide(part) for part in (part1, part2, part3)), token_grad_a[0])
    return (mixed, token_grad, gate_total, up_total, down_total)


def solution(mesh):
    activations = P(("depth", "col"), "row")
    wide_weight = P("row", ("col", "depth"))
    tall_weight = P(("col", "depth"), "row")
    return jax.shard_map(
        body,
        mesh=mesh,
        in_specs=(activations, wide_weight, wide_weight, tall_weight, activations),
        out_specs=(activations, activations, wide_weight, wide_weight, tall_weight),
        check_vma=False,
    )
```

```python
import functools

import jax
import jax.numpy as jnp
from jax import lax
from jax.experimental import pallas as pl
from jax.experimental.pallas import tpu as pltpu
from jax.sharding import PartitionSpec as P

CORE, CHIP = 1, 2
VMEM_BYTES = 56 * 1024 * 1024


def dot(left, right, left_dim, right_dim):
    return lax.dot_general(
        left, right, (((left_dim,), (right_dim,)), ((), ())), preferred_element_type=jnp.float32
    )


def after(array, *others):
    return lax.optimization_barrier((array, *others))[0]


def wide(block):
    return block.astype(jnp.float32)


def narrow(block):
    return block.astype(jnp.bfloat16)


def cost(flops, *arrays):
    moved = sum(array.size * array.dtype.itemsize for array in arrays)
    return pl.CostEstimate(flops=flops, bytes_accessed=moved, transcendentals=0)


def contract_kernel(n_pieces, n_weights, right_dim, *refs):
    pieces, weights = refs[:n_pieces], refs[n_pieces : n_pieces + n_weights]
    out, total = refs[-2:]
    step = pl.program_id(0)

    @pl.when(step == 0)
    def _():
        total[...] = jnp.zeros_like(total)

    rows = jnp.concatenate([piece[...] for piece in pieces], axis=0)
    for i, weight in enumerate(weights):
        total[i * rows.shape[0] : (i + 1) * rows.shape[0]] += dot(rows, weight[...], 1, right_dim)

    @pl.when(step == pl.num_programs(0) - 1)
    def _():
        out[...] = narrow(total[...])


def contract(pieces, weights, right_dim):
    width = pieces[0].shape[1]
    units = weights[0].shape[1 - right_dim]
    block = min(1024, width)
    if right_dim == 0:
        weight_spec = pl.BlockSpec((block, units), lambda k: (k, 0))
    else:
        weight_spec = pl.BlockSpec((units, block), lambda k: (0, k))
    rows = sum(piece.shape[0] for piece in pieces)
    shape = (rows * len(weights), units)
    return pl.pallas_call(
        functools.partial(contract_kernel, len(pieces), len(weights), right_dim),
        grid=(width // block,),
        in_specs=[pl.BlockSpec((piece.shape[0], block), lambda k: (0, k)) for piece in pieces]
        + [weight_spec] * len(weights),
        out_specs=pl.BlockSpec(shape, lambda k: (0, 0)),
        out_shape=jax.ShapeDtypeStruct(shape, jnp.bfloat16),
        scratch_shapes=[pltpu.VMEM(shape, jnp.float32)],
        compiler_params=pltpu.CompilerParams(vmem_limit_bytes=VMEM_BYTES),
        cost_estimate=cost(2 * len(weights) * rows * width * units, *pieces, *weights),
    )(*pieces, *weights)


def store_halves(total, outs):
    size = total.shape[0] // 8
    for i, out in enumerate(outs):
        for at, (half, block) in enumerate(((0, 0), (0, 1), (1, 0), (1, 1))):
            first = (4 * block + 2 * i + half) * size
            out[at * size : (at + 1) * size] = narrow(total[first : first + size])


def expand_kernel(n, *refs):
    lefts, weights, outs = refs[: 2 * n], refs[2 * n : 3 * n], refs[3 * n :]
    total = 0.0
    for i, weight in enumerate(weights):
        left = jnp.concatenate([block[...] for block in lefts[2 * i : 2 * i + 2]], axis=0)
        total = total + dot(left, weight[...], 1, 1)
    store_halves(total, outs)


def expand(lefts, weights):
    blocks = sum(lefts, [])
    rows, units = blocks[0].shape
    width = weights[0].shape[0]
    block = min(512, width)
    out = jax.ShapeDtypeStruct((rows, width), jnp.bfloat16)
    return pl.pallas_call(
        functools.partial(expand_kernel, len(lefts)),
        grid=(width // block,),
        in_specs=[pl.BlockSpec((rows, units), lambda j: (0, 0))] * len(blocks)
        + [pl.BlockSpec((block, units), lambda j: (j, 0))] * len(weights),
        out_specs=[pl.BlockSpec((rows, block), lambda j: (0, j))] * 2,
        out_shape=[out, out],
        compiler_params=pltpu.CompilerParams(vmem_limit_bytes=VMEM_BYTES),
        cost_estimate=cost(4 * len(lefts) * rows * width * units, *blocks, *weights, out, out),
    )(*blocks, *weights)


def down_kernel(n_pieces, *refs):
    pieces, (first, second, weight, grad, mine, other, total) = refs[:n_pieces], refs[n_pieces:]
    step = pl.program_id(0)

    @pl.when(step == 0)
    def _():
        total[...] = jnp.zeros_like(total)

    rows = jnp.concatenate([piece[...] for piece in pieces], axis=0)
    total[...] += dot(rows, weight[...], 1, 1)
    hidden = jnp.concatenate([first[...], second[...]], axis=0)
    store_halves(dot(hidden, weight[...], 1, 0), (mine, other))

    @pl.when(step == pl.num_programs(0) - 1)
    def _():
        grad[...] = narrow(total[...])


def down_products(pieces, hiddens, weight):
    units, width = weight.shape
    block = min(512, width)
    rows = sum(piece.shape[0] for piece in pieces)
    half = hiddens[0].shape[0]
    grad = jax.ShapeDtypeStruct((rows, units), jnp.bfloat16)
    out = jax.ShapeDtypeStruct((half, width), jnp.bfloat16)
    return pl.pallas_call(
        functools.partial(down_kernel, len(pieces)),
        grid=(width // block,),
        in_specs=[pl.BlockSpec((piece.shape[0], block), lambda j: (0, j)) for piece in pieces]
        + [pl.BlockSpec((half, units), lambda j: (0, 0))] * 2
        + [pl.BlockSpec((units, block), lambda j: (0, j))],
        out_specs=[pl.BlockSpec(grad.shape, lambda j: (0, 0))]
        + [pl.BlockSpec((half, block), lambda j: (0, j))] * 2,
        out_shape=[grad, out, out],
        scratch_shapes=[pltpu.VMEM(grad.shape, jnp.float32)],
        compiler_params=pltpu.CompilerParams(vmem_limit_bytes=VMEM_BYTES),
        cost_estimate=cost(4 * rows * width * units, *pieces, *hiddens, weight, out, out),
    )(*pieces, *hiddens, weight)


def wide_grad_kernel(n_pieces, *refs):
    pieces, grads, outs = refs[:n_pieces], refs[n_pieces:-2], refs[-2:]
    rows = jnp.concatenate([piece[...] for piece in pieces], axis=0)
    half = len(grads) // 2
    for i, out in enumerate(outs):
        grad = jnp.concatenate([grad[...] for grad in grads[i * half : (i + 1) * half]], axis=0)
        out[...] = dot(rows, grad, 0, 0)


def wide_grads(pieces, gate_grads, up_grads):
    grads = [*gate_grads, *up_grads]
    width, units = pieces[0].shape[1], grads[0].shape[1]
    block = min(512, width)
    rows = sum(piece.shape[0] for piece in pieces)
    out = jax.ShapeDtypeStruct((width, units), jnp.float32)
    return pl.pallas_call(
        functools.partial(wide_grad_kernel, len(pieces)),
        grid=(width // block,),
        in_specs=[pl.BlockSpec((piece.shape[0], block), lambda j: (0, j)) for piece in pieces]
        + [pl.BlockSpec(grad.shape, lambda j: (0, 0)) for grad in grads],
        out_specs=[pl.BlockSpec((block, units), lambda j: (j, 0))] * 2,
        out_shape=[out, out],
        compiler_params=pltpu.CompilerParams(vmem_limit_bytes=VMEM_BYTES),
        cost_estimate=cost(4 * rows * width * units, *pieces, *grads, out, out),
    )(*pieces, *grads)


def tall_grad_kernel(n_pieces, *refs):
    pieces, hiddens, out = refs[:n_pieces], refs[n_pieces:-1], refs[-1]
    rows = jnp.concatenate([piece[...] for piece in pieces], axis=0)
    hidden = jnp.concatenate([hidden[...] for hidden in hiddens], axis=0)
    out[...] = dot(hidden, rows, 0, 0)


def tall_grad(pieces, hiddens):
    width, units = pieces[0].shape[1], hiddens[0].shape[1]
    block = min(512, width)
    rows = sum(piece.shape[0] for piece in pieces)
    out = jax.ShapeDtypeStruct((units, width), jnp.float32)
    return pl.pallas_call(
        functools.partial(tall_grad_kernel, len(pieces)),
        grid=(width // block,),
        in_specs=[pl.BlockSpec((piece.shape[0], block), lambda j: (0, j)) for piece in pieces]
        + [pl.BlockSpec(hidden.shape, lambda j: (0, 0)) for hidden in hiddens],
        out_specs=pl.BlockSpec((units, block), lambda j: (0, j)),
        out_shape=out,
        compiler_params=pltpu.CompilerParams(vmem_limit_bytes=VMEM_BYTES),
        cost_estimate=cost(2 * rows * width * units, *pieces, *hiddens, out),
    )(*pieces, *hiddens)


def shift(block, step):
    n = lax.axis_size("depth")
    return lax.ppermute(block, "depth", [(i, (i + step) % n) for i in range(n)])


def swap(block, bit):
    n = lax.axis_size("col")
    return lax.ppermute(block, "col", [(i, i ^ bit) for i in range(n)])


def row_moves(partial):
    n = lax.axis_size("row")
    return [
        lax.ppermute(partial, "row", [(i, (i + step) % n) for i in range(n)])
        for step in range(1, n)
    ]


def row_sum(partial, moved, *others):
    return sum([wide(after(block, *others)) for block in moved], wide(partial))


def add(*blocks):
    return narrow(sum(wide(block) for block in blocks))


def grads_of(gate, up, hidden_grad):
    sigma = jax.nn.sigmoid(gate)
    gate_grad = narrow(hidden_grad * up * sigma * (1.0 + gate * (1.0 - sigma)))
    return gate_grad, narrow(hidden_grad * (gate * sigma))


def hidden_of(gate, up):
    return narrow(gate * jax.nn.sigmoid(gate) * up)


def sync(*arrays):
    return lax.optimization_barrier(arrays)


def other_cores(blocks):
    return [swap(block, CORE) for block in blocks]


def chip_part(mine, moved):
    half = mine.shape[0] // 2
    return add(mine[half:], moved[half:]), (mine[:half], moved[:half])


def owner_parts(kept, moved):
    size = moved.shape[0] // 2
    rows = [slice(0, size), slice(size, 2 * size)]
    return [sum(wide(block[at]) for block in (*kept, moved)) for at in rows]


def quad(near, far, moved):
    return [near, far, *moved]


def body(tokens, gate_weight, up_weight, down_weight, cotangent):
    pair = [gate_weight, up_weight]

    def pair_sums(partial, moved):
        half = partial.shape[0] // 2
        total = row_sum(partial, moved)
        return total[:half], total[half:]

    near1, far0, core0 = sync(shift(tokens, 1), swap(tokens, CHIP), swap(tokens, CORE))

    near3, far1 = shift(after(tokens, near1), 3), swap(near1, CHIP)
    core1, far_core0 = other_cores([near1, far0])
    token0 = quad(tokens, far0, [core0, far_core0])
    pair0 = contract(token0, pair, 0)
    near3, far1, core1, pair0 = sync(near3, far1, core1, pair0)

    pair0_moved = row_moves(pair0)
    cot = after(cotangent, pair0)
    near2, cot_near3 = shift(near1, 1), shift(cot, 3)
    far3, cot_far0 = swap(near3, CHIP), swap(cot, CHIP)
    token1 = quad(near1, far1, [core1, swap(far1, CORE)])
    pair1 = contract(token1, pair, 0)
    near2, cot_near3, far3, cot_far0, pair1, *pair0_moved = sync(
        near2, cot_near3, far3, cot_far0, pair1, *pair0_moved
    )

    gate0, up0 = pair_sums(pair0, pair0_moved)
    hidden0 = hidden_of(gate0, up0)
    pair1_moved = row_moves(pair1)
    cot = after(cotangent, pair1)
    cot_near2 = shift(cot, 2)
    far2, cot_far3 = swap(near2, CHIP), swap(cot_near3, CHIP)
    token3 = quad(near3, far3, other_cores([after(near3, pair1), far3]))
    pair3 = contract(token3, pair, 0)
    cot_near2, far2, cot_far3, pair3, *pair1_moved = sync(
        cot_near2, far2, cot_far3, pair3, *pair1_moved
    )

    gate1, up1 = pair_sums(pair1, pair1_moved)
    hidden1 = hidden_of(gate1, up1)
    pair3_moved = row_moves(pair3)
    cot = after(cotangent, pair3)
    cot_near1, cot_far2 = shift(cot, 1), swap(cot_near2, CHIP)
    token2 = quad(near2, far2, other_cores([after(near2, pair3), far2]))
    pair2 = contract(token2, pair, 0)
    cot_near1, cot_far2, pair2, *pair3_moved = sync(cot_near1, cot_far2, pair2, *pair3_moved)

    gate3, up3 = pair_sums(pair3, pair3_moved)
    hidden3 = hidden_of(gate3, up3)
    pair2_moved = row_moves(pair2)
    cot_far1 = swap(cot_near1, CHIP)
    cot3 = quad(cot_near3, cot_far3, other_cores(after(x, pair2) for x in (cot_near3, cot_far3)))
    cot2 = quad(cot_near2, cot_far2, other_cores(after(x, pair2) for x in (cot_near2, cot_far2)))
    grad_b, mine, other = down_products(cot3 + cot2, [hidden0, hidden1], down_weight)
    cot_far1, grad_b, mine, other, *pair2_moved = sync(
        cot_far1, grad_b, mine, other, *pair2_moved
    )

    gate2, up2 = pair_sums(pair2, pair2_moved)
    hidden2 = hidden_of(gate2, up2)
    grad_b_moved = row_moves(grad_b)
    sent, mixed_a = chip_part(mine, swap(other, CORE))
    mixed_a_moved = swap(sent, CHIP)
    cot = after(cotangent, grad_b)
    cot0 = quad(cot, cot_far0, other_cores([cot, after(cot_far0, grad_b)]))
    cot1 = quad(cot_near1, cot_far1, other_cores([after(cot_near1, grad_b), cot_far1]))
    grad_a, mine, other = down_products(cot0 + cot1, [hidden3, hidden2], down_weight)
    mixed_a_moved, grad_a, mine, other, *grad_b_moved = sync(
        mixed_a_moved, grad_a, mine, other, *grad_b_moved
    )

    grad_b = row_sum(grad_b, grad_b_moved)
    grad_a_moved = row_moves(grad_a)
    sent, mixed_b = chip_part(mine, swap(other, CORE))
    mixed_b_moved = swap(sent, CHIP)
    half = grad_b.shape[0] // 2
    grads3 = grads_of(gate3, up3, grad_b[:half])
    grads2 = grads_of(gate2, up2, grad_b[half:])
    mine, other = expand([[x, y] for x, y in zip(grads3, grads2)], pair)
    mixed_b_moved, mine, other, *grad_a_moved = sync(mixed_b_moved, mine, other, *grad_a_moved)

    grad_a = row_sum(grad_a, grad_a_moved)
    sent, token_grad_b = chip_part(mine, swap(other, CORE))
    token_b_moved = swap(sent, CHIP)
    mixed_b = owner_parts(mixed_b, mixed_b_moved)
    part3, part2 = shift(narrow(mixed_b[0]), 1), shift(narrow(mixed_b[1]), -1)
    grads0 = grads_of(gate0, up0, grad_a[:half])
    grads1 = grads_of(gate1, up1, grad_a[half:])
    mine, other = expand([[x, y] for x, y in zip(grads0, grads1)], pair)
    token_b_moved, mine, other, part3, part2 = sync(token_b_moved, mine, other, part3, part2)

    sent, token_grad_a = chip_part(mine, swap(other, CORE))
    token_a_moved = swap(sent, CHIP)
    mixed_a = owner_parts(mixed_a, mixed_a_moved)
    part1 = shift(narrow(mixed_a[1] + wide(part2)), -1)
    mixed = mixed_a[0] + wide(part3)
    token_grad_b = owner_parts(token_grad_b, token_b_moved)
    part3, part2 = shift(narrow(token_grad_b[0]), 1), shift(narrow(token_grad_b[1]), -1)
    gate_total, up_total = wide_grads(
        [after(tokens, sent), *token0[1:], *token1, *token3, *token2],
        [grads0[0], grads1[0], grads3[0], grads2[0]],
        [grads0[1], grads1[1], grads3[1], grads2[1]],
    )
    token_a_moved, part1, part2, part3, gate_total, up_total = sync(
        token_a_moved, part1, part2, part3, gate_total, up_total
    )
    mixed = mixed + wide(part1)

    token_grad_a = owner_parts(token_grad_a, token_a_moved)
    part1 = shift(narrow(token_grad_a[1] + wide(part2)), -1)
    down_total = tall_grad(
        cot0 + cot1 + cot3 + cot2, [after(hidden0, gate_total), hidden1, hidden3, hidden2]
    )
    token_grad = token_grad_a[0] + wide(part3) + wide(part1)
    return (mixed, token_grad, gate_total, up_total, down_total)


def solution(mesh):
    activations = P(("depth", "col"), "row")
    wide_weight = P("row", ("col", "depth"))
    tall_weight = P(("col", "depth"), "row")
    return jax.shard_map(
        body,
        mesh=mesh,
        in_specs=(activations, wide_weight, wide_weight, tall_weight, activations),
        out_specs=(activations, activations, wide_weight, wide_weight, tall_weight),
        check_vma=False,
    )
```

```python
import functools

import jax
import jax.numpy as jnp
from jax import lax
from jax.experimental import pallas as pl
from jax.experimental.pallas import tpu as pltpu
from jax.sharding import PartitionSpec as P

CORE, CHIP = 1, 2
VMEM_BYTES = 56 * 1024 * 1024
DEEP = pl.Buffered(4)


def dot(left, right, left_dim, right_dim):
    return lax.dot_general(
        left, right, (((left_dim,), (right_dim,)), ((), ())), preferred_element_type=jnp.float32
    )


def after(array, *others):
    return lax.optimization_barrier((array, *others))[0]


def wide(block):
    return block.astype(jnp.float32)


def narrow(block):
    return block.astype(jnp.bfloat16)


def cost(flops, *arrays):
    moved = sum(array.size * array.dtype.itemsize for array in arrays)
    return pl.CostEstimate(flops=flops, bytes_accessed=moved, transcendentals=0)


def streamed(kernel, steps, in_specs, out_specs, out_shape, total, flops):
    def outer(*refs):
        kept = refs[len(in_specs) + len(out_specs) :]
        pipeline = pltpu.emit_pipeline(
            lambda *blocks: kernel(*blocks, *kept),
            grid=(steps,),
            in_specs=in_specs,
            out_specs=out_specs,
        )
        pipeline(*refs[: len(in_specs) + len(out_specs)])

    def call(*operands):
        return pl.pallas_call(
            outer,
            in_specs=[pl.BlockSpec(memory_space=pl.ANY)] * len(in_specs),
            out_specs=[pl.BlockSpec(memory_space=pl.ANY)] * len(out_specs),
            out_shape=out_shape,
            scratch_shapes=[pltpu.VMEM(shape, jnp.float32) for shape in total],
            compiler_params=pltpu.CompilerParams(vmem_limit_bytes=VMEM_BYTES),
            cost_estimate=cost(flops, *operands, *out_shape),
        )(*operands)

    return call


def piece_specs(pieces, block):
    return [
        pl.BlockSpec((piece.shape[0], block), lambda j: (0, j), pipeline_mode=DEEP)
        for piece in pieces
    ]


def contract_kernel(n_pieces, n_weights, right_dim, *refs):
    pieces, weights = refs[:n_pieces], refs[n_pieces : n_pieces + n_weights]
    out, total = refs[-2:]
    step = pl.program_id(0)

    @pl.when(step == 0)
    def _():
        total[...] = jnp.zeros_like(total)

    rows = jnp.concatenate([piece[...] for piece in pieces], axis=0)
    for i, weight in enumerate(weights):
        total[i * rows.shape[0] : (i + 1) * rows.shape[0]] += dot(rows, weight[...], 1, right_dim)

    @pl.when(step == pl.num_programs(0) - 1)
    def _():
        out[...] = narrow(total[...])


def contract(pieces, weights, right_dim):
    width = pieces[0].shape[1]
    units = weights[0].shape[1 - right_dim]
    block = min(512, width)
    if right_dim == 0:
        weight_spec = pl.BlockSpec((block, units), lambda k: (k, 0), pipeline_mode=DEEP)
    else:
        weight_spec = pl.BlockSpec((units, block), lambda k: (0, k), pipeline_mode=DEEP)
    rows = sum(piece.shape[0] for piece in pieces)
    shape = (rows * len(weights), units)
    (out,) = streamed(
        functools.partial(contract_kernel, len(pieces), len(weights), right_dim),
        width // block,
        piece_specs(pieces, block) + [weight_spec] * len(weights),
        [pl.BlockSpec(shape, lambda k: (0, 0))],
        [jax.ShapeDtypeStruct(shape, jnp.bfloat16)],
        [shape],
        2 * len(weights) * rows * width * units,
    )(*pieces, *weights)
    return out


def store_halves(total, outs):
    size = total.shape[0] // 8
    for i, out in enumerate(outs):
        for at, (half, block) in enumerate(((0, 0), (0, 1), (1, 0), (1, 1))):
            first = (4 * block + 2 * i + half) * size
            out[at * size : (at + 1) * size] = narrow(total[first : first + size])


def expand_kernel(n, *refs):
    lefts, weights, outs = refs[: 2 * n], refs[2 * n : 3 * n], refs[3 * n :]
    total = 0.0
    for i, weight in enumerate(weights):
        left = jnp.concatenate([block[...] for block in lefts[2 * i : 2 * i + 2]], axis=0)
        total = total + dot(left, weight[...], 1, 1)
    store_halves(total, outs)


def expand(lefts, weights):
    blocks = sum(lefts, [])
    rows, units = blocks[0].shape
    width = weights[0].shape[0]
    block = min(512, width)
    out = jax.ShapeDtypeStruct((rows, width), jnp.bfloat16)
    return streamed(
        functools.partial(expand_kernel, len(lefts)),
        width // block,
        [pl.BlockSpec((rows, units), lambda j: (0, 0))] * len(blocks)
        + [pl.BlockSpec((block, units), lambda j: (j, 0), pipeline_mode=DEEP)] * len(weights),
        [pl.BlockSpec((rows, block), lambda j: (0, j))] * 2,
        [out, out],
        [],
        4 * len(lefts) * rows * width * units,
    )(*blocks, *weights)


def down_kernel(n_pieces, *refs):
    pieces, (first, second, weight, grad, mine, other, total) = refs[:n_pieces], refs[n_pieces:]
    step = pl.program_id(0)

    @pl.when(step == 0)
    def _():
        total[...] = jnp.zeros_like(total)

    rows = jnp.concatenate([piece[...] for piece in pieces], axis=0)
    total[...] += dot(rows, weight[...], 1, 1)
    hidden = jnp.concatenate([first[...], second[...]], axis=0)
    store_halves(dot(hidden, weight[...], 1, 0), (mine, other))

    @pl.when(step == pl.num_programs(0) - 1)
    def _():
        grad[...] = narrow(total[...])


def down_products(pieces, hiddens, weight):
    units, width = weight.shape
    block = min(512, width)
    rows = sum(piece.shape[0] for piece in pieces)
    half = hiddens[0].shape[0]
    grad = jax.ShapeDtypeStruct((rows, units), jnp.bfloat16)
    out = jax.ShapeDtypeStruct((half, width), jnp.bfloat16)
    return streamed(
        functools.partial(down_kernel, len(pieces)),
        width // block,
        piece_specs(pieces, block)
        + [pl.BlockSpec((half, units), lambda j: (0, 0))] * 2
        + [pl.BlockSpec((units, block), lambda j: (0, j), pipeline_mode=DEEP)],
        [pl.BlockSpec(grad.shape, lambda j: (0, 0))]
        + [pl.BlockSpec((half, block), lambda j: (0, j))] * 2,
        [grad, out, out],
        [grad.shape],
        4 * rows * width * units,
    )(*pieces, *hiddens, weight)


def wide_grad_kernel(n_pieces, *refs):
    pieces, grads, outs = refs[:n_pieces], refs[n_pieces:-2], refs[-2:]
    rows = jnp.concatenate([piece[...] for piece in pieces], axis=0)
    half = len(grads) // 2
    for i, out in enumerate(outs):
        grad = jnp.concatenate([grad[...] for grad in grads[i * half : (i + 1) * half]], axis=0)
        out[...] = dot(rows, grad, 0, 0)


def wide_grads(pieces, gate_grads, up_grads):
    grads = [*gate_grads, *up_grads]
    width, units = pieces[0].shape[1], grads[0].shape[1]
    block = min(512, width)
    rows = sum(piece.shape[0] for piece in pieces)
    out = jax.ShapeDtypeStruct((width, units), jnp.float32)
    return streamed(
        functools.partial(wide_grad_kernel, len(pieces)),
        width // block,
        piece_specs(pieces, block)
        + [pl.BlockSpec(grad.shape, lambda j: (0, 0)) for grad in grads],
        [pl.BlockSpec((block, units), lambda j: (j, 0))] * 2,
        [out, out],
        [],
        4 * rows * width * units,
    )(*pieces, *grads)


def tall_grad_kernel(n_pieces, *refs):
    pieces, hiddens, out = refs[:n_pieces], refs[n_pieces:-1], refs[-1]
    rows = jnp.concatenate([piece[...] for piece in pieces], axis=0)
    hidden = jnp.concatenate([hidden[...] for hidden in hiddens], axis=0)
    out[...] = dot(hidden, rows, 0, 0)


def tall_grad(pieces, hiddens):
    width, units = pieces[0].shape[1], hiddens[0].shape[1]
    block = min(512, width)
    rows = sum(piece.shape[0] for piece in pieces)
    out = jax.ShapeDtypeStruct((units, width), jnp.float32)
    (out,) = streamed(
        functools.partial(tall_grad_kernel, len(pieces)),
        width // block,
        piece_specs(pieces, block)
        + [pl.BlockSpec(hidden.shape, lambda j: (0, 0)) for hidden in hiddens],
        [pl.BlockSpec((units, block), lambda j: (0, j))],
        [out],
        [],
        2 * rows * width * units,
    )(*pieces, *hiddens)
    return out


def shift(block, step):
    n = lax.axis_size("depth")
    return lax.ppermute(block, "depth", [(i, (i + step) % n) for i in range(n)])


def swap(block, bit):
    n = lax.axis_size("col")
    return lax.ppermute(block, "col", [(i, i ^ bit) for i in range(n)])


def row_moves(partial):
    n = lax.axis_size("row")
    return [
        lax.ppermute(partial, "row", [(i, (i + step) % n) for i in range(n)])
        for step in range(1, n)
    ]


def row_sum(partial, moved, *others):
    return sum([wide(after(block, *others)) for block in moved], wide(partial))


def add(*blocks):
    return narrow(sum(wide(block) for block in blocks))


def grads_of(gate, up, hidden_grad):
    sigma = jax.nn.sigmoid(gate)
    gate_grad = narrow(hidden_grad * up * sigma * (1.0 + gate * (1.0 - sigma)))
    return gate_grad, narrow(hidden_grad * (gate * sigma))


def hidden_of(gate, up):
    return narrow(gate * jax.nn.sigmoid(gate) * up)


def sync(*arrays):
    return lax.optimization_barrier(arrays)


def other_cores(blocks):
    return [swap(block, CORE) for block in blocks]


def chip_part(mine, moved):
    half = mine.shape[0] // 2
    return add(mine[half:], moved[half:]), (mine[:half], moved[:half])


def owner_parts(kept, moved):
    size = moved.shape[0] // 2
    rows = [slice(0, size), slice(size, 2 * size)]
    return [sum(wide(block[at]) for block in (*kept, moved)) for at in rows]


def quad(near, far, moved):
    return [near, far, *moved]


def body(tokens, gate_weight, up_weight, down_weight, cotangent):
    pair = [gate_weight, up_weight]

    def pair_sums(partial, moved):
        half = partial.shape[0] // 2
        total = row_sum(partial, moved)
        return total[:half], total[half:]

    near1, far0, core0 = sync(shift(tokens, 1), swap(tokens, CHIP), swap(tokens, CORE))

    near3, far1 = shift(after(tokens, near1), 3), swap(near1, CHIP)
    core1, far_core0 = other_cores([near1, far0])
    token0 = quad(tokens, far0, [core0, far_core0])
    pair0 = contract(token0, pair, 0)
    near3, far1, core1, pair0 = sync(near3, far1, core1, pair0)

    pair0_moved = row_moves(pair0)
    cot = after(cotangent, pair0)
    near2, cot_near3 = shift(near1, 1), shift(cot, 3)
    far3, cot_far0 = swap(near3, CHIP), swap(cot, CHIP)
    token1 = quad(near1, far1, [core1, swap(far1, CORE)])
    pair1 = contract(token1, pair, 0)
    near2, cot_near3, far3, cot_far0, pair1, *pair0_moved = sync(
        near2, cot_near3, far3, cot_far0, pair1, *pair0_moved
    )

    gate0, up0 = pair_sums(pair0, pair0_moved)
    hidden0 = hidden_of(gate0, up0)
    pair1_moved = row_moves(pair1)
    cot = after(cotangent, pair1)
    cot_near2 = shift(cot, 2)
    far2, cot_far3 = swap(near2, CHIP), swap(cot_near3, CHIP)
    token3 = quad(near3, far3, other_cores([after(near3, pair1), far3]))
    pair3 = contract(token3, pair, 0)
    cot_near2, far2, cot_far3, pair3, *pair1_moved = sync(
        cot_near2, far2, cot_far3, pair3, *pair1_moved
    )

    gate1, up1 = pair_sums(pair1, pair1_moved)
    hidden1 = hidden_of(gate1, up1)
    pair3_moved = row_moves(pair3)
    cot = after(cotangent, pair3)
    cot_near1, cot_far2 = shift(cot, 1), swap(cot_near2, CHIP)
    token2 = quad(near2, far2, other_cores([after(near2, pair3), far2]))
    pair2 = contract(token2, pair, 0)
    cot0 = quad(cot, cot_far0, other_cores([cot, after(cot_far0, pair3)]))
    cot_near1, cot_far2, pair2, cot0[2], cot0[3], *pair3_moved = sync(
        cot_near1, cot_far2, pair2, cot0[2], cot0[3], *pair3_moved
    )

    gate3, up3 = pair_sums(pair3, pair3_moved)
    hidden3 = hidden_of(gate3, up3)
    pair2_moved = row_moves(pair2)
    cot_far1 = swap(cot_near1, CHIP)
    cot3 = quad(cot_near3, cot_far3, other_cores(after(x, pair2) for x in (cot_near3, cot_far3)))
    cot2 = quad(cot_near2, cot_far2, other_cores(after(x, pair2) for x in (cot_near2, cot_far2)))
    grad_b, mine, other = down_products(cot3 + cot2, [hidden0, hidden1], down_weight)
    cot_far1, grad_b, mine, other, *pair2_moved = sync(
        cot_far1, grad_b, mine, other, *pair2_moved
    )

    gate2, up2 = pair_sums(pair2, pair2_moved)
    hidden2 = hidden_of(gate2, up2)
    grad_b_moved = row_moves(grad_b)
    sent, mixed_a = chip_part(mine, swap(other, CORE))
    mixed_a_moved = swap(sent, CHIP)
    cot1 = quad(cot_near1, cot_far1, other_cores([after(cot_near1, grad_b), cot_far1]))
    grad_a, mine, other = down_products(cot0 + cot1, [hidden3, hidden2], down_weight)
    mixed_a_moved, grad_a, mine, other, *grad_b_moved = sync(
        mixed_a_moved, grad_a, mine, other, *grad_b_moved
    )

    grad_a_moved = row_moves(grad_a)
    sent, mixed_b = chip_part(mine, swap(other, CORE))
    grad_b = row_sum(grad_b, grad_b_moved, sent)
    mixed_b_moved = swap(sent, CHIP)
    half = grad_b.shape[0] // 2
    grads3 = grads_of(gate3, up3, grad_b[:half])
    grads2 = grads_of(gate2, up2, grad_b[half:])
    mine, other = expand([[x, y] for x, y in zip(grads3, grads2)], pair)
    mixed_b_moved, mine, other, *grad_a_moved = sync(mixed_b_moved, mine, other, *grad_a_moved)

    sent, token_grad_b = chip_part(mine, swap(other, CORE))
    token_b_moved = swap(sent, CHIP)
    grad_a = row_sum(grad_a, grad_a_moved, sent)
    mixed_b = owner_parts(mixed_b, after(mixed_b_moved, sent))
    part3, part2 = shift(narrow(mixed_b[0]), 1), shift(narrow(mixed_b[1]), -1)
    grads0 = grads_of(gate0, up0, grad_a[:half])
    grads1 = grads_of(gate1, up1, grad_a[half:])
    mine, other = expand([[x, y] for x, y in zip(grads0, grads1)], pair)
    token_b_moved, mine, other, part3, part2 = sync(token_b_moved, mine, other, part3, part2)

    sent, token_grad_a = chip_part(mine, swap(other, CORE))
    token_a_moved = swap(sent, CHIP)
    mixed_a = owner_parts(mixed_a, after(mixed_a_moved, sent))
    part1 = shift(narrow(mixed_a[1] + wide(part2)), -1)
    mixed = mixed_a[0] + wide(part3)
    token_grad_b = owner_parts(token_grad_b, after(token_b_moved, sent))
    part3, part2 = shift(narrow(token_grad_b[0]), 1), shift(narrow(token_grad_b[1]), -1)
    gate_total, up_total = wide_grads(
        [after(tokens, sent), *token0[1:], *token1, *token3, *token2],
        [grads0[0], grads1[0], grads3[0], grads2[0]],
        [grads0[1], grads1[1], grads3[1], grads2[1]],
    )
    token_a_moved, part1, part2, part3, gate_total, up_total = sync(
        token_a_moved, part1, part2, part3, gate_total, up_total
    )
    mixed = mixed + wide(part1)

    token_grad_a = owner_parts(token_grad_a, token_a_moved)
    part1 = shift(narrow(token_grad_a[1] + wide(part2)), -1)
    down_total = tall_grad(
        cot0 + cot1 + cot3 + cot2, [after(hidden0, gate_total), hidden1, hidden3, hidden2]
    )
    token_grad = token_grad_a[0] + wide(part3) + wide(part1)
    return (mixed, token_grad, gate_total, up_total, down_total)


def solution(mesh):
    activations = P(("depth", "col"), "row")
    wide_weight = P("row", ("col", "depth"))
    tall_weight = P(("col", "depth"), "row")
    return jax.shard_map(
        body,
        mesh=mesh,
        in_specs=(activations, wide_weight, wide_weight, tall_weight, activations),
        out_specs=(activations, activations, wide_weight, wide_weight, tall_weight),
        check_vma=False,
    )
```

```python
import functools

import jax
import jax.numpy as jnp
from jax import lax
from jax.experimental import pallas as pl
from jax.experimental.pallas import tpu as pltpu
from jax.sharding import PartitionSpec as P

CORE, CHIP = 1, 2
VMEM_BYTES = 56 * 1024 * 1024


def dot(left, right, left_dim, right_dim):
    return lax.dot_general(
        left, right, (((left_dim,), (right_dim,)), ((), ())), preferred_element_type=jnp.float32
    )


def after(array, *others):
    return lax.optimization_barrier((array, *others))[0]


def wide(block):
    return block.astype(jnp.float32)


def narrow(block):
    return block.astype(jnp.bfloat16)


def cost(flops, *arrays):
    moved = sum(array.size * array.dtype.itemsize for array in arrays)
    return pl.CostEstimate(flops=flops, bytes_accessed=moved, transcendentals=0)


def contract_kernel(n_pieces, n_weights, *refs):
    pieces, weights = refs[:n_pieces], refs[n_pieces : n_pieces + n_weights]
    out, total = refs[-2:]
    step = pl.program_id(0)

    @pl.when(step == 0)
    def _():
        total[...] = jnp.zeros_like(total)

    rows = jnp.concatenate([piece[...] for piece in pieces], axis=0)
    weight = jnp.concatenate([weight[...] for weight in weights], axis=1)
    total[...] += dot(rows, weight, 1, 0)

    @pl.when(step == pl.num_programs(0) - 1)
    def _():
        size, units = rows.shape[0], total.shape[1] // n_weights
        for i in range(n_weights):
            out[i * size : (i + 1) * size] = narrow(total[:, i * units : (i + 1) * units])


def contract(pieces, weights):
    width = pieces[0].shape[1]
    units = weights[0].shape[1]
    block = min(1024, width)
    weight_spec = pl.BlockSpec((block, units), lambda k: (k, 0))
    rows = sum(piece.shape[0] for piece in pieces)
    shape = (rows * len(weights), units)
    return pl.pallas_call(
        functools.partial(contract_kernel, len(pieces), len(weights)),
        grid=(width // block,),
        in_specs=[pl.BlockSpec((piece.shape[0], block), lambda k: (0, k)) for piece in pieces]
        + [weight_spec] * len(weights),
        out_specs=pl.BlockSpec(shape, lambda k: (0, 0)),
        out_shape=jax.ShapeDtypeStruct(shape, jnp.bfloat16),
        scratch_shapes=[pltpu.VMEM((rows, units * len(weights)), jnp.float32)],
        compiler_params=pltpu.CompilerParams(vmem_limit_bytes=VMEM_BYTES),
        cost_estimate=cost(2 * len(weights) * rows * width * units, *pieces, *weights),
    )(*pieces, *weights)


def store_halves(total, outs):
    size = total.shape[0] // 8
    for i, out in enumerate(outs):
        for at, (half, block) in enumerate(((0, 0), (0, 1), (1, 0), (1, 1))):
            first = (4 * block + 2 * i + half) * size
            out[at * size : (at + 1) * size] = narrow(total[first : first + size])


def expand_kernel(n, *refs):
    lefts, weights, outs = refs[: 2 * n], refs[2 * n : 3 * n], refs[3 * n :]
    left = [
        jnp.concatenate([block[...] for block in lefts[2 * i : 2 * i + 2]], axis=0)
        for i in range(n)
    ]
    weight = jnp.concatenate([weight[...] for weight in weights], axis=1)
    store_halves(dot(jnp.concatenate(left, axis=1), weight, 1, 1), outs)


def expand(lefts, weights):
    blocks = sum(lefts, [])
    rows, units = blocks[0].shape
    width = weights[0].shape[0]
    block = min(512, width)
    out = jax.ShapeDtypeStruct((rows, width), jnp.bfloat16)
    return pl.pallas_call(
        functools.partial(expand_kernel, len(lefts)),
        grid=(width // block,),
        in_specs=[pl.BlockSpec((rows, units), lambda j: (0, 0))] * len(blocks)
        + [pl.BlockSpec((block, units), lambda j: (j, 0))] * len(weights),
        out_specs=[pl.BlockSpec((rows, block), lambda j: (0, j))] * 2,
        out_shape=[out, out],
        compiler_params=pltpu.CompilerParams(vmem_limit_bytes=VMEM_BYTES),
        cost_estimate=cost(4 * len(lefts) * rows * width * units, *blocks, *weights, out, out),
    )(*blocks, *weights)


def down_kernel(n_pieces, *refs):
    pieces, (first, second, weight, grad, mine, other, total) = refs[:n_pieces], refs[n_pieces:]
    step = pl.program_id(0)

    @pl.when(step == 0)
    def _():
        total[...] = jnp.zeros_like(total)

    rows = jnp.concatenate([piece[...] for piece in pieces], axis=0)
    total[...] += dot(rows, weight[...], 1, 1)
    hidden = jnp.concatenate([first[...], second[...]], axis=0)
    store_halves(dot(hidden, weight[...], 1, 0), (mine, other))

    @pl.when(step == pl.num_programs(0) - 1)
    def _():
        grad[...] = narrow(total[...])


def down_products(pieces, hiddens, weight):
    units, width = weight.shape
    block = min(512, width)
    rows = sum(piece.shape[0] for piece in pieces)
    half = hiddens[0].shape[0]
    grad = jax.ShapeDtypeStruct((rows, units), jnp.bfloat16)
    out = jax.ShapeDtypeStruct((half, width), jnp.bfloat16)
    return pl.pallas_call(
        functools.partial(down_kernel, len(pieces)),
        grid=(width // block,),
        in_specs=[pl.BlockSpec((piece.shape[0], block), lambda j: (0, j)) for piece in pieces]
        + [pl.BlockSpec((half, units), lambda j: (0, 0))] * 2
        + [pl.BlockSpec((units, block), lambda j: (0, j))],
        out_specs=[pl.BlockSpec(grad.shape, lambda j: (0, 0))]
        + [pl.BlockSpec((half, block), lambda j: (0, j))] * 2,
        out_shape=[grad, out, out],
        scratch_shapes=[pltpu.VMEM(grad.shape, jnp.float32)],
        compiler_params=pltpu.CompilerParams(vmem_limit_bytes=VMEM_BYTES),
        cost_estimate=cost(4 * rows * width * units, *pieces, *hiddens, weight, out, out),
    )(*pieces, *hiddens, weight)


def wide_grad_kernel(n_pieces, *refs):
    pieces, grads, outs = refs[:n_pieces], refs[n_pieces:-2], refs[-2:]
    rows = jnp.concatenate([piece[...] for piece in pieces], axis=0)
    half = len(grads) // 2
    grad = [
        jnp.concatenate([grad[...] for grad in grads[i * half : (i + 1) * half]], axis=0)
        for i in range(2)
    ]
    both = dot(rows, jnp.concatenate(grad, axis=1), 0, 0)
    units = both.shape[1] // 2
    for i, out in enumerate(outs):
        out[...] = both[:, i * units : (i + 1) * units]


def wide_grads(pieces, gate_grads, up_grads):
    grads = [*gate_grads, *up_grads]
    width, units = pieces[0].shape[1], grads[0].shape[1]
    block = min(512, width)
    rows = sum(piece.shape[0] for piece in pieces)
    out = jax.ShapeDtypeStruct((width, units), jnp.float32)
    return pl.pallas_call(
        functools.partial(wide_grad_kernel, len(pieces)),
        grid=(width // block,),
        in_specs=[pl.BlockSpec((piece.shape[0], block), lambda j: (0, j)) for piece in pieces]
        + [pl.BlockSpec(grad.shape, lambda j: (0, 0)) for grad in grads],
        out_specs=[pl.BlockSpec((block, units), lambda j: (j, 0))] * 2,
        out_shape=[out, out],
        compiler_params=pltpu.CompilerParams(vmem_limit_bytes=VMEM_BYTES),
        cost_estimate=cost(4 * rows * width * units, *pieces, *grads, out, out),
    )(*pieces, *grads)


def tall_grad_kernel(n_pieces, *refs):
    pieces, hiddens, out = refs[:n_pieces], refs[n_pieces:-1], refs[-1]
    rows = jnp.concatenate([piece[...] for piece in pieces], axis=0)
    hidden = jnp.concatenate([hidden[...] for hidden in hiddens], axis=0)
    out[...] = dot(hidden, rows, 0, 0)


def tall_grad(pieces, hiddens):
    width, units = pieces[0].shape[1], hiddens[0].shape[1]
    block = min(512, width)
    rows = sum(piece.shape[0] for piece in pieces)
    out = jax.ShapeDtypeStruct((units, width), jnp.float32)
    return pl.pallas_call(
        functools.partial(tall_grad_kernel, len(pieces)),
        grid=(width // block,),
        in_specs=[pl.BlockSpec((piece.shape[0], block), lambda j: (0, j)) for piece in pieces]
        + [pl.BlockSpec(hidden.shape, lambda j: (0, 0)) for hidden in hiddens],
        out_specs=pl.BlockSpec((units, block), lambda j: (0, j)),
        out_shape=out,
        compiler_params=pltpu.CompilerParams(vmem_limit_bytes=VMEM_BYTES),
        cost_estimate=cost(2 * rows * width * units, *pieces, *hiddens, out),
    )(*pieces, *hiddens)


def shift(block, step):
    n = lax.axis_size("depth")
    return lax.ppermute(block, "depth", [(i, (i + step) % n) for i in range(n)])


def swap(block, bit):
    n = lax.axis_size("col")
    return lax.ppermute(block, "col", [(i, i ^ bit) for i in range(n)])


def row_moves(partial):
    n = lax.axis_size("row")
    return [
        lax.ppermute(partial, "row", [(i, (i + step) % n) for i in range(n)])
        for step in range(1, n)
    ]


def row_sum(partial, moved, *others):
    return sum([wide(after(block, *others)) for block in moved], wide(partial))


def add(*blocks):
    return narrow(sum(wide(block) for block in blocks))


def grads_of(gate, up, hidden_grad):
    sigma = jax.nn.sigmoid(gate)
    gate_grad = narrow(hidden_grad * up * sigma * (1.0 + gate * (1.0 - sigma)))
    return gate_grad, narrow(hidden_grad * (gate * sigma))


def hidden_of(gate, up):
    return narrow(gate * jax.nn.sigmoid(gate) * up)


def sync(*arrays):
    return lax.optimization_barrier(arrays)


def other_cores(blocks):
    return [swap(block, CORE) for block in blocks]


def chip_part(mine, moved):
    half = mine.shape[0] // 2
    return add(mine[half:], moved[half:]), (mine[:half], moved[:half])


def owner_parts(kept, moved):
    size = moved.shape[0] // 2
    rows = [slice(0, size), slice(size, 2 * size)]
    return [sum(wide(block[at]) for block in (*kept, moved)) for at in rows]


def quad(near, far, moved):
    return [near, far, *moved]


def body(tokens, gate_weight, up_weight, down_weight, cotangent):
    pair = [gate_weight, up_weight]

    def pair_sums(partial, moved):
        half = partial.shape[0] // 2
        total = row_sum(partial, moved)
        return total[:half], total[half:]

    near1, far0, core0 = sync(shift(tokens, 1), swap(tokens, CHIP), swap(tokens, CORE))

    near3, far1 = shift(after(tokens, near1), 3), swap(near1, CHIP)
    core1, far_core0 = other_cores([near1, far0])
    token0 = quad(tokens, far0, [core0, far_core0])
    pair0 = contract(token0, pair)
    near3, far1, core1, pair0 = sync(near3, far1, core1, pair0)

    pair0_moved = row_moves(pair0)
    cot = after(cotangent, pair0)
    near2, cot_near3 = shift(near1, 1), shift(cot, 3)
    far3, cot_far0 = swap(near3, CHIP), swap(cot, CHIP)
    token1 = quad(near1, far1, [core1, swap(far1, CORE)])
    pair1 = contract(token1, pair)
    near2, cot_near3, far3, cot_far0, pair1, *pair0_moved = sync(
        near2, cot_near3, far3, cot_far0, pair1, *pair0_moved
    )

    gate0, up0 = pair_sums(pair0, pair0_moved)
    hidden0 = hidden_of(gate0, up0)
    pair1_moved = row_moves(pair1)
    cot = after(cotangent, pair1)
    cot_near2 = shift(cot, 2)
    far2, cot_far3 = swap(near2, CHIP), swap(cot_near3, CHIP)
    token3 = quad(near3, far3, other_cores([after(near3, pair1), far3]))
    pair3 = contract(token3, pair)
    cot_near2, far2, cot_far3, pair3, *pair1_moved = sync(
        cot_near2, far2, cot_far3, pair3, *pair1_moved
    )

    gate1, up1 = pair_sums(pair1, pair1_moved)
    hidden1 = hidden_of(gate1, up1)
    pair3_moved = row_moves(pair3)
    cot = after(cotangent, pair3)
    cot_near1, cot_far2 = shift(cot, 1), swap(cot_near2, CHIP)
    token2 = quad(near2, far2, other_cores([after(near2, pair3), far2]))
    pair2 = contract(token2, pair)
    cot0 = quad(cot, cot_far0, other_cores([cot, after(cot_far0, pair3)]))
    cot_near1, cot_far2, pair2, cot0[2], cot0[3], *pair3_moved = sync(
        cot_near1, cot_far2, pair2, cot0[2], cot0[3], *pair3_moved
    )

    gate3, up3 = pair_sums(pair3, pair3_moved)
    hidden3 = hidden_of(gate3, up3)
    pair2_moved = row_moves(pair2)
    cot_far1 = swap(cot_near1, CHIP)
    cot3 = quad(cot_near3, cot_far3, other_cores(after(x, pair2) for x in (cot_near3, cot_far3)))
    cot2 = quad(cot_near2, cot_far2, other_cores(after(x, pair2) for x in (cot_near2, cot_far2)))
    grad_b, mine, other = down_products(cot3 + cot2, [hidden0, hidden1], down_weight)
    cot_far1, grad_b, mine, other, *pair2_moved = sync(
        cot_far1, grad_b, mine, other, *pair2_moved
    )

    gate2, up2 = pair_sums(pair2, pair2_moved)
    hidden2 = hidden_of(gate2, up2)
    grad_b_moved = row_moves(grad_b)
    sent, mixed_a = chip_part(mine, swap(other, CORE))
    mixed_a_moved = swap(sent, CHIP)
    cot1 = quad(cot_near1, cot_far1, other_cores([after(cot_near1, grad_b), cot_far1]))
    grad_a, mine, other = down_products(cot0 + cot1, [hidden3, hidden2], down_weight)
    mixed_a_moved, grad_a, mine, other, *grad_b_moved = sync(
        mixed_a_moved, grad_a, mine, other, *grad_b_moved
    )

    grad_b = row_sum(grad_b, grad_b_moved)
    grad_a_moved = row_moves(grad_a)
    sent, mixed_b = chip_part(mine, swap(other, CORE))
    mixed_b_moved = swap(sent, CHIP)
    half = grad_b.shape[0] // 2
    grads3 = grads_of(gate3, up3, grad_b[:half])
    grads2 = grads_of(gate2, up2, grad_b[half:])
    mine, other = expand([[x, y] for x, y in zip(grads3, grads2)], pair)
    mixed_b_moved, mine, other, *grad_a_moved = sync(mixed_b_moved, mine, other, *grad_a_moved)

    sent, token_grad_b = chip_part(mine, swap(other, CORE))
    token_b_moved = swap(sent, CHIP)
    grad_a = row_sum(grad_a, grad_a_moved)
    mixed_b = owner_parts(mixed_b, after(mixed_b_moved, sent))
    part3, part2 = shift(narrow(mixed_b[0]), 1), shift(narrow(mixed_b[1]), -1)
    grads0 = grads_of(gate0, up0, grad_a[:half])
    grads1 = grads_of(gate1, up1, grad_a[half:])
    mine, other = expand([[x, y] for x, y in zip(grads0, grads1)], pair)
    token_b_moved, mine, other, part3, part2 = sync(token_b_moved, mine, other, part3, part2)

    sent, token_grad_a = chip_part(mine, swap(other, CORE))
    token_a_moved = swap(sent, CHIP)
    mixed_a = owner_parts(mixed_a, mixed_a_moved)
    token_grad_b = owner_parts(token_grad_b, after(token_b_moved, sent))
    mixed_part3, part3 = part3, shift(narrow(token_grad_b[0]), 1)
    back = [narrow(mixed_a[1] + wide(part2)), narrow(token_grad_b[1])]
    back = shift(jnp.concatenate(back, axis=0), -1)
    gate_total, up_total = wide_grads(
        [after(tokens, sent), *token0[1:], *token1, *token3, *token2],
        [grads0[0], grads1[0], grads3[0], grads2[0]],
        [grads0[1], grads1[1], grads3[1], grads2[1]],
    )
    token_a_moved, back, part3, gate_total, up_total = sync(
        token_a_moved, back, part3, gate_total, up_total
    )

    token_grad_a = owner_parts(token_grad_a, token_a_moved)
    size = back.shape[0] // 2
    part1 = shift(narrow(token_grad_a[1] + wide(back[size:])), -1)
    down_total = tall_grad(
        cot0 + cot1 + cot3 + cot2, [after(hidden0, gate_total), hidden1, hidden3, hidden2]
    )
    part1, mixed_part3, back, part3, down_total = sync(part1, mixed_part3, back, part3, down_total)
    mixed = mixed_a[0] + wide(mixed_part3) + wide(back[:size])
    token_grad = token_grad_a[0] + wide(part3) + wide(part1)
    return (mixed, token_grad, gate_total, up_total, down_total)


def solution(mesh):
    activations = P(("depth", "col"), "row")
    wide_weight = P("row", ("col", "depth"))
    tall_weight = P(("col", "depth"), "row")
    return jax.shard_map(
        body,
        mesh=mesh,
        in_specs=(activations, wide_weight, wide_weight, tall_weight, activations),
        out_specs=(activations, activations, wide_weight, wide_weight, tall_weight),
        check_vma=False,
    )
```

```python
import functools

import jax
import jax.numpy as jnp
from jax import lax
from jax.experimental import pallas as pl
from jax.experimental.pallas import tpu as pltpu
from jax.sharding import PartitionSpec as P

CORE, CHIP = 1, 2
VMEM_BYTES = 56 * 1024 * 1024


def dot(left, right, left_dim, right_dim):
    return lax.dot_general(
        left, right, (((left_dim,), (right_dim,)), ((), ())), preferred_element_type=jnp.float32
    )


def after(array, *others):
    return lax.optimization_barrier((array, *others))[0]


def wide(block):
    return block.astype(jnp.float32)


def narrow(block):
    return block.astype(jnp.bfloat16)


def cost(flops, *arrays):
    moved = sum(array.size * array.dtype.itemsize for array in arrays)
    return pl.CostEstimate(flops=flops, bytes_accessed=moved, transcendentals=0)


def contract_kernel(n_pieces, n_weights, *refs):
    pieces, weights = refs[:n_pieces], refs[n_pieces : n_pieces + n_weights]
    out, total = refs[-2:]
    step = pl.program_id(0)

    @pl.when(step == 0)
    def _():
        total[...] = jnp.zeros_like(total)

    rows = jnp.concatenate([piece[...] for piece in pieces], axis=0)
    weight = jnp.concatenate([weight[...] for weight in weights], axis=1)
    total[...] += dot(rows, weight, 1, 0)

    @pl.when(step == pl.num_programs(0) - 1)
    def _():
        size, units = rows.shape[0], total.shape[1] // n_weights
        for i in range(n_weights):
            out[i * size : (i + 1) * size] = narrow(total[:, i * units : (i + 1) * units])


def contract(pieces, weights):
    width = pieces[0].shape[1]
    units = weights[0].shape[1]
    block = min(1024, width)
    weight_spec = pl.BlockSpec((block, units), lambda k: (k, 0))
    rows = sum(piece.shape[0] for piece in pieces)
    shape = (rows * len(weights), units)
    return pl.pallas_call(
        functools.partial(contract_kernel, len(pieces), len(weights)),
        grid=(width // block,),
        in_specs=[pl.BlockSpec((piece.shape[0], block), lambda k: (0, k)) for piece in pieces]
        + [weight_spec] * len(weights),
        out_specs=pl.BlockSpec(shape, lambda k: (0, 0)),
        out_shape=jax.ShapeDtypeStruct(shape, jnp.bfloat16),
        scratch_shapes=[pltpu.VMEM((rows, units * len(weights)), jnp.float32)],
        compiler_params=pltpu.CompilerParams(vmem_limit_bytes=VMEM_BYTES),
        cost_estimate=cost(2 * len(weights) * rows * width * units, *pieces, *weights),
    )(*pieces, *weights)


def store_parts(total, outs):
    size = total.shape[0] // 8
    for i, out in enumerate(outs):
        for block in range(2):
            first = (4 * block + i) * size
            out[block * size : (block + 1) * size] = narrow(total[first : first + size])


def expand_kernel(n, *refs):
    lefts, weights, outs = refs[: 2 * n], refs[2 * n : 3 * n], refs[3 * n :]
    left = [
        jnp.concatenate([block[...] for block in lefts[2 * i : 2 * i + 2]], axis=0)
        for i in range(n)
    ]
    weight = jnp.concatenate([weight[...] for weight in weights], axis=1)
    store_parts(dot(jnp.concatenate(left, axis=1), weight, 1, 1), outs)


def expand(lefts, weights):
    blocks = sum(lefts, [])
    rows, units = blocks[0].shape
    width = weights[0].shape[0]
    block = min(512, width)
    out = jax.ShapeDtypeStruct((rows // 2, width), jnp.bfloat16)
    return pl.pallas_call(
        functools.partial(expand_kernel, len(lefts)),
        grid=(width // block,),
        in_specs=[pl.BlockSpec((rows, units), lambda j: (0, 0))] * len(blocks)
        + [pl.BlockSpec((block, units), lambda j: (j, 0))] * len(weights),
        out_specs=[pl.BlockSpec(out.shape[:1] + (block,), lambda j: (0, j))] * 4,
        out_shape=[out] * 4,
        compiler_params=pltpu.CompilerParams(vmem_limit_bytes=VMEM_BYTES),
        cost_estimate=cost(4 * len(lefts) * rows * width * units, *blocks, *weights, *[out] * 4),
    )(*blocks, *weights)


def down_kernel(n_pieces, *refs):
    pieces, (first, second, weight, grad, *outs, total) = refs[:n_pieces], refs[n_pieces:]
    step = pl.program_id(0)

    @pl.when(step == 0)
    def _():
        total[...] = jnp.zeros_like(total)

    rows = jnp.concatenate([piece[...] for piece in pieces], axis=0)
    total[...] += dot(rows, weight[...], 1, 1)
    hidden = jnp.concatenate([first[...], second[...]], axis=0)
    store_parts(dot(hidden, weight[...], 1, 0), outs)

    @pl.when(step == pl.num_programs(0) - 1)
    def _():
        grad[...] = narrow(total[...])


def down_products(pieces, hiddens, weight):
    units, width = weight.shape
    block = min(512, width)
    rows = sum(piece.shape[0] for piece in pieces)
    half = hiddens[0].shape[0]
    grad = jax.ShapeDtypeStruct((rows, units), jnp.bfloat16)
    out = jax.ShapeDtypeStruct((half // 2, width), jnp.bfloat16)
    return pl.pallas_call(
        functools.partial(down_kernel, len(pieces)),
        grid=(width // block,),
        in_specs=[pl.BlockSpec((piece.shape[0], block), lambda j: (0, j)) for piece in pieces]
        + [pl.BlockSpec((half, units), lambda j: (0, 0))] * 2
        + [pl.BlockSpec((units, block), lambda j: (0, j))],
        out_specs=[pl.BlockSpec(grad.shape, lambda j: (0, 0))]
        + [pl.BlockSpec((half // 2, block), lambda j: (0, j))] * 4,
        out_shape=[grad] + [out] * 4,
        scratch_shapes=[pltpu.VMEM(grad.shape, jnp.float32)],
        compiler_params=pltpu.CompilerParams(vmem_limit_bytes=VMEM_BYTES),
        cost_estimate=cost(4 * rows * width * units, *pieces, *hiddens, weight, *[out] * 4),
    )(*pieces, *hiddens, weight)


def wide_grad_kernel(n_pieces, *refs):
    pieces, grads, outs = refs[:n_pieces], refs[n_pieces:-2], refs[-2:]
    rows = jnp.concatenate([piece[...] for piece in pieces], axis=0)
    half = len(grads) // 2
    grad = [
        jnp.concatenate([grad[...] for grad in grads[i * half : (i + 1) * half]], axis=0)
        for i in range(2)
    ]
    both = dot(rows, jnp.concatenate(grad, axis=1), 0, 0)
    units = both.shape[1] // 2
    for i, out in enumerate(outs):
        out[...] = both[:, i * units : (i + 1) * units]


def wide_grads(pieces, gate_grads, up_grads):
    grads = [*gate_grads, *up_grads]
    width, units = pieces[0].shape[1], grads[0].shape[1]
    block = min(512, width)
    rows = sum(piece.shape[0] for piece in pieces)
    out = jax.ShapeDtypeStruct((width, units), jnp.float32)
    return pl.pallas_call(
        functools.partial(wide_grad_kernel, len(pieces)),
        grid=(width // block,),
        in_specs=[pl.BlockSpec((piece.shape[0], block), lambda j: (0, j)) for piece in pieces]
        + [pl.BlockSpec(grad.shape, lambda j: (0, 0)) for grad in grads],
        out_specs=[pl.BlockSpec((block, units), lambda j: (j, 0))] * 2,
        out_shape=[out, out],
        compiler_params=pltpu.CompilerParams(vmem_limit_bytes=VMEM_BYTES),
        cost_estimate=cost(4 * rows * width * units, *pieces, *grads, out, out),
    )(*pieces, *grads)


def tall_grad_kernel(n_pieces, *refs):
    pieces, hiddens, out = refs[:n_pieces], refs[n_pieces:-1], refs[-1]
    rows = jnp.concatenate([piece[...] for piece in pieces], axis=0)
    hidden = jnp.concatenate([hidden[...] for hidden in hiddens], axis=0)
    out[...] = dot(hidden, rows, 0, 0)


def tall_grad(pieces, hiddens):
    width, units = pieces[0].shape[1], hiddens[0].shape[1]
    block = min(512, width)
    rows = sum(piece.shape[0] for piece in pieces)
    out = jax.ShapeDtypeStruct((units, width), jnp.float32)
    return pl.pallas_call(
        functools.partial(tall_grad_kernel, len(pieces)),
        grid=(width // block,),
        in_specs=[pl.BlockSpec((piece.shape[0], block), lambda j: (0, j)) for piece in pieces]
        + [pl.BlockSpec(hidden.shape, lambda j: (0, 0)) for hidden in hiddens],
        out_specs=pl.BlockSpec((units, block), lambda j: (0, j)),
        out_shape=out,
        compiler_params=pltpu.CompilerParams(vmem_limit_bytes=VMEM_BYTES),
        cost_estimate=cost(2 * rows * width * units, *pieces, *hiddens, out),
    )(*pieces, *hiddens)


def shift(block, step):
    n = lax.axis_size("depth")
    return lax.ppermute(block, "depth", [(i, (i + step) % n) for i in range(n)])


def swap(block, bit):
    n = lax.axis_size("col")
    return lax.ppermute(block, "col", [(i, i ^ bit) for i in range(n)])


def row_moves(partial):
    n = lax.axis_size("row")
    return [
        lax.ppermute(partial, "row", [(i, (i + step) % n) for i in range(n)])
        for step in range(1, n)
    ]


def row_sum(partial, moved, *others):
    return sum([wide(after(block, *others)) for block in moved], wide(partial))


def add(*blocks):
    return narrow(sum(wide(block) for block in blocks))


def grads_of(gate, up, hidden_grad):
    sigma = jax.nn.sigmoid(gate)
    gate_grad = narrow(hidden_grad * up * sigma * (1.0 + gate * (1.0 - sigma)))
    return gate_grad, narrow(hidden_grad * (gate * sigma))


def hidden_of(gate, up):
    return narrow(gate * jax.nn.sigmoid(gate) * up)


def sync(*arrays):
    return lax.optimization_barrier(arrays)


def other_cores(blocks):
    return [swap(block, CORE) for block in blocks]


def chip_part(parts):
    near, far, other_near, other_far = parts
    sent = add(far, swap(other_far, CORE))
    return sent, [near, swap(after(other_near, sent), CORE)]


def owner_parts(kept, moved):
    size = moved.shape[0] // 2
    rows = [slice(0, size), slice(size, 2 * size)]
    return [sum(wide(block[at]) for block in (*kept, moved)) for at in rows]


def quad(near, far, moved):
    return [near, far, *moved]


def body(tokens, gate_weight, up_weight, down_weight, cotangent):
    pair = [gate_weight, up_weight]

    def pair_sums(partial, moved):
        half = partial.shape[0] // 2
        total = row_sum(partial, moved)
        return total[:half], total[half:]

    near1, far0, core0 = sync(shift(tokens, 1), swap(tokens, CHIP), swap(tokens, CORE))

    near3, far1 = shift(after(tokens, near1), 3), swap(near1, CHIP)
    core1, far_core0 = other_cores([near1, far0])
    token0 = quad(tokens, far0, [core0, far_core0])
    pair0 = contract(token0, pair)
    near3, far1, core1, pair0 = sync(near3, far1, core1, pair0)

    pair0_moved = row_moves(pair0)
    cot = after(cotangent, pair0)
    near2, cot_near3 = shift(near1, 1), shift(cot, 3)
    far3, cot_far0 = swap(near3, CHIP), swap(cot, CHIP)
    token1 = quad(near1, far1, [core1, swap(far1, CORE)])
    pair1 = contract(token1, pair)
    near2, cot_near3, far3, cot_far0, pair1, *pair0_moved = sync(
        near2, cot_near3, far3, cot_far0, pair1, *pair0_moved
    )

    gate0, up0 = pair_sums(pair0, pair0_moved)
    hidden0 = hidden_of(gate0, up0)
    pair1_moved = row_moves(pair1)
    cot = after(cotangent, pair1)
    cot_near2 = shift(cot, 2)
    far2, cot_far3 = swap(near2, CHIP), swap(cot_near3, CHIP)
    token3 = quad(near3, far3, other_cores([after(near3, pair1), far3]))
    pair3 = contract(token3, pair)
    cot_near2, far2, cot_far3, pair3, *pair1_moved = sync(
        cot_near2, far2, cot_far3, pair3, *pair1_moved
    )

    gate1, up1 = pair_sums(pair1, pair1_moved)
    hidden1 = hidden_of(gate1, up1)
    pair3_moved = row_moves(pair3)
    cot = after(cotangent, pair3)
    cot_near1, cot_far2 = shift(cot, 1), swap(cot_near2, CHIP)
    token2 = quad(near2, far2, other_cores([after(near2, pair3), far2]))
    pair2 = contract(token2, pair)
    cot0 = quad(cot, cot_far0, other_cores([cot, after(cot_far0, pair3)]))
    cot_near1, cot_far2, pair2, cot0[2], cot0[3], *pair3_moved = sync(
        cot_near1, cot_far2, pair2, cot0[2], cot0[3], *pair3_moved
    )

    gate3, up3 = pair_sums(pair3, pair3_moved)
    hidden3 = hidden_of(gate3, up3)
    pair2_moved = row_moves(pair2)
    cot_far1 = swap(cot_near1, CHIP)
    cot3 = quad(cot_near3, cot_far3, other_cores(after(x, pair2) for x in (cot_near3, cot_far3)))
    cot2 = quad(cot_near2, cot_far2, other_cores(after(x, pair2) for x in (cot_near2, cot_far2)))
    products = down_products(cot3 + cot2, [hidden0, hidden1], down_weight)
    cot_far1, grad_b, *rest = sync(cot_far1, *products, *pair2_moved)
    parts, pair2_moved = rest[:4], rest[4:]

    gate2, up2 = pair_sums(pair2, pair2_moved)
    hidden2 = hidden_of(gate2, up2)
    grad_b_moved = row_moves(grad_b)
    sent, mixed_a = chip_part(parts)
    mixed_a_moved = swap(sent, CHIP)
    cot1 = quad(cot_near1, cot_far1, other_cores([after(cot_near1, grad_b), cot_far1]))
    products = down_products(cot0 + cot1, [hidden3, hidden2], down_weight)
    mixed_a_moved, mixed_a[1], grad_a, *rest = sync(
        mixed_a_moved, mixed_a[1], *products, *grad_b_moved
    )
    parts, grad_b_moved = rest[:4], rest[4:]

    grad_b = row_sum(grad_b, grad_b_moved)
    grad_a_moved = row_moves(grad_a)
    sent, mixed_b = chip_part(parts)
    mixed_b_moved = swap(sent, CHIP)
    half = grad_b.shape[0] // 2
    grads3 = grads_of(gate3, up3, grad_b[:half])
    grads2 = grads_of(gate2, up2, grad_b[half:])
    parts = expand([[x, y] for x, y in zip(grads3, grads2)], pair)
    mixed_b_moved, mixed_b[1], *rest = sync(mixed_b_moved, mixed_b[1], *parts, *grad_a_moved)
    parts, grad_a_moved = rest[:4], rest[4:]

    sent, token_grad_b = chip_part(parts)
    token_b_moved = swap(sent, CHIP)
    grad_a = row_sum(grad_a, grad_a_moved)
    mixed_b = owner_parts(mixed_b, after(mixed_b_moved, sent))
    part3, part2 = shift(narrow(mixed_b[0]), 1), shift(narrow(mixed_b[1]), -1)
    grads0 = grads_of(gate0, up0, grad_a[:half])
    grads1 = grads_of(gate1, up1, grad_a[half:])
    parts = expand([[x, y] for x, y in zip(grads0, grads1)], pair)
    token_b_moved, token_grad_b[1], mixed_part3, mixed_part2, *parts = sync(
        token_b_moved, token_grad_b[1], part3, part2, *parts
    )

    sent, token_grad_a = chip_part(parts)
    token_a_moved = swap(sent, CHIP)
    mixed_a = owner_parts(mixed_a, mixed_a_moved)
    token_grad_b = owner_parts(token_grad_b, after(token_b_moved, sent))
    part3, part2 = shift(narrow(token_grad_b[0]), 1), shift(narrow(token_grad_b[1]), -1)
    down_total = tall_grad(
        cot0 + cot1 + cot3 + cot2, [after(hidden0, sent), hidden1, hidden3, hidden2]
    )
    token_a_moved, token_grad_a[1], part2, part3, down_total = sync(
        token_a_moved, token_grad_a[1], part2, part3, down_total
    )

    token_grad_a = owner_parts(token_grad_a, token_a_moved)
    back = [mixed_a[1] + wide(mixed_part2), token_grad_a[1] + wide(part2)]
    back = shift(narrow(jnp.concatenate(back, axis=0)), -1)
    gate_total, up_total = wide_grads(
        [after(tokens, down_total), *token0[1:], *token1, *token3, *token2],
        [grads0[0], grads1[0], grads3[0], grads2[0]],
        [grads0[1], grads1[1], grads3[1], grads2[1]],
    )
    back, mixed_part3, part3, gate_total = sync(back, mixed_part3, part3, gate_total)
    size = back.shape[0] // 2
    mixed = mixed_a[0] + wide(mixed_part3) + wide(back[:size])
    token_grad = token_grad_a[0] + wide(part3) + wide(back[size:])
    return (mixed, token_grad, gate_total, up_total, down_total)


def solution(mesh):
    activations = P(("depth", "col"), "row")
    wide_weight = P("row", ("col", "depth"))
    tall_weight = P(("col", "depth"), "row")
    return jax.shard_map(
        body,
        mesh=mesh,
        in_specs=(activations, wide_weight, wide_weight, tall_weight, activations),
        out_specs=(activations, activations, wide_weight, wide_weight, tall_weight),
        check_vma=False,
    )
```

```python
import functools

import jax
import jax.numpy as jnp
from jax import lax
from jax.experimental import pallas as pl
from jax.experimental.pallas import tpu as pltpu
from jax.sharding import PartitionSpec as P

CORE, CHIP = 1, 2
VMEM_BYTES = 56 * 1024 * 1024


def dot(left, right, left_dim, right_dim):
    return lax.dot_general(
        left, right, (((left_dim,), (right_dim,)), ((), ())), preferred_element_type=jnp.float32
    )


def after(array, *others):
    return lax.optimization_barrier((array, *others))[0]


def wide(block):
    return block.astype(jnp.float32)


def narrow(block):
    return block.astype(jnp.bfloat16)


def cost(flops, *arrays):
    moved = sum(array.size * array.dtype.itemsize for array in arrays)
    return pl.CostEstimate(flops=flops, bytes_accessed=moved, transcendentals=0)


def contract_kernel(n_pieces, n_weights, *refs):
    pieces, weights = refs[:n_pieces], refs[n_pieces : n_pieces + n_weights]
    out, total = refs[-2:]
    step = pl.program_id(0)

    @pl.when(step == 0)
    def _():
        total[...] = jnp.zeros_like(total)

    rows = jnp.concatenate([piece[...] for piece in pieces], axis=0)
    weight = jnp.concatenate([weight[...] for weight in weights], axis=1)
    total[...] += dot(rows, weight, 1, 0)

    @pl.when(step == pl.num_programs(0) - 1)
    def _():
        size, units = rows.shape[0], total.shape[1] // n_weights
        for i in range(n_weights):
            out[i * size : (i + 1) * size] = narrow(total[:, i * units : (i + 1) * units])


def contract(pieces, weights):
    width = pieces[0].shape[1]
    units = weights[0].shape[1]
    block = min(1024, width)
    weight_spec = pl.BlockSpec((block, units), lambda k: (k, 0))
    rows = sum(piece.shape[0] for piece in pieces)
    shape = (rows * len(weights), units)
    return pl.pallas_call(
        functools.partial(contract_kernel, len(pieces), len(weights)),
        grid=(width // block,),
        in_specs=[pl.BlockSpec((piece.shape[0], block), lambda k: (0, k)) for piece in pieces]
        + [weight_spec] * len(weights),
        out_specs=pl.BlockSpec(shape, lambda k: (0, 0)),
        out_shape=jax.ShapeDtypeStruct(shape, jnp.bfloat16),
        scratch_shapes=[pltpu.VMEM((rows, units * len(weights)), jnp.float32)],
        compiler_params=pltpu.CompilerParams(vmem_limit_bytes=VMEM_BYTES),
        cost_estimate=cost(2 * len(weights) * rows * width * units, *pieces, *weights),
    )(*pieces, *weights)


def store_parts(total, outs):
    size = total.shape[0] // 8
    for i, out in enumerate(outs):
        for block in range(2):
            first = (4 * block + i) * size
            out[block * size : (block + 1) * size] = narrow(total[first : first + size])


def expand_kernel(n, *refs):
    lefts, weights, outs = refs[: 2 * n], refs[2 * n : 3 * n], refs[3 * n :]
    left = [
        jnp.concatenate([block[...] for block in lefts[2 * i : 2 * i + 2]], axis=0)
        for i in range(n)
    ]
    weight = jnp.concatenate([weight[...] for weight in weights], axis=1)
    store_parts(dot(jnp.concatenate(left, axis=1), weight, 1, 1), outs)


def expand(lefts, weights):
    blocks = sum(lefts, [])
    rows, units = blocks[0].shape
    width = weights[0].shape[0]
    block = min(512, width)
    out = jax.ShapeDtypeStruct((rows // 2, width), jnp.bfloat16)
    return pl.pallas_call(
        functools.partial(expand_kernel, len(lefts)),
        grid=(width // block,),
        in_specs=[pl.BlockSpec((rows, units), lambda j: (0, 0))] * len(blocks)
        + [pl.BlockSpec((block, units), lambda j: (j, 0))] * len(weights),
        out_specs=[pl.BlockSpec(out.shape[:1] + (block,), lambda j: (0, j))] * 4,
        out_shape=[out] * 4,
        compiler_params=pltpu.CompilerParams(vmem_limit_bytes=VMEM_BYTES),
        cost_estimate=cost(4 * len(lefts) * rows * width * units, *blocks, *weights, *[out] * 4),
    )(*blocks, *weights)


def down_kernel(n_pieces, *refs):
    pieces, (first, second, weight, grad, *outs, total) = refs[:n_pieces], refs[n_pieces:]
    step = pl.program_id(0)

    @pl.when(step == 0)
    def _():
        total[...] = jnp.zeros_like(total)

    rows = jnp.concatenate([piece[...] for piece in pieces], axis=0)
    total[...] += dot(rows, weight[...], 1, 1)
    hidden = jnp.concatenate([first[...], second[...]], axis=0)
    store_parts(dot(hidden, weight[...], 1, 0), outs)

    @pl.when(step == pl.num_programs(0) - 1)
    def _():
        grad[...] = narrow(total[...])


def down_products(pieces, hiddens, weight):
    units, width = weight.shape
    block = min(512, width)
    rows = sum(piece.shape[0] for piece in pieces)
    half = hiddens[0].shape[0]
    grad = jax.ShapeDtypeStruct((rows, units), jnp.bfloat16)
    out = jax.ShapeDtypeStruct((half // 2, width), jnp.bfloat16)
    return pl.pallas_call(
        functools.partial(down_kernel, len(pieces)),
        grid=(width // block,),
        in_specs=[pl.BlockSpec((piece.shape[0], block), lambda j: (0, j)) for piece in pieces]
        + [pl.BlockSpec((half, units), lambda j: (0, 0))] * 2
        + [pl.BlockSpec((units, block), lambda j: (0, j))],
        out_specs=[pl.BlockSpec(grad.shape, lambda j: (0, 0))]
        + [pl.BlockSpec((half // 2, block), lambda j: (0, j))] * 4,
        out_shape=[grad] + [out] * 4,
        scratch_shapes=[pltpu.VMEM(grad.shape, jnp.float32)],
        compiler_params=pltpu.CompilerParams(vmem_limit_bytes=VMEM_BYTES),
        cost_estimate=cost(4 * rows * width * units, *pieces, *hiddens, weight, *[out] * 4),
    )(*pieces, *hiddens, weight)


def wide_grad_kernel(n_pieces, *refs):
    pieces, grads, outs = refs[:n_pieces], refs[n_pieces:-2], refs[-2:]
    rows = jnp.concatenate([piece[...] for piece in pieces], axis=0)
    half = len(grads) // 2
    grad = [
        jnp.concatenate([grad[...] for grad in grads[i * half : (i + 1) * half]], axis=0)
        for i in range(2)
    ]
    both = dot(rows, jnp.concatenate(grad, axis=1), 0, 0)
    units = both.shape[1] // 2
    for i, out in enumerate(outs):
        out[...] = both[:, i * units : (i + 1) * units]


def wide_grads(pieces, gate_grads, up_grads):
    grads = [*gate_grads, *up_grads]
    width, units = pieces[0].shape[1], grads[0].shape[1]
    block = min(512, width)
    rows = sum(piece.shape[0] for piece in pieces)
    out = jax.ShapeDtypeStruct((width, units), jnp.float32)
    return pl.pallas_call(
        functools.partial(wide_grad_kernel, len(pieces)),
        grid=(width // block,),
        in_specs=[pl.BlockSpec((piece.shape[0], block), lambda j: (0, j)) for piece in pieces]
        + [pl.BlockSpec(grad.shape, lambda j: (0, 0)) for grad in grads],
        out_specs=[pl.BlockSpec((block, units), lambda j: (j, 0))] * 2,
        out_shape=[out, out],
        compiler_params=pltpu.CompilerParams(vmem_limit_bytes=VMEM_BYTES),
        cost_estimate=cost(4 * rows * width * units, *pieces, *grads, out, out),
    )(*pieces, *grads)


def tall_grad_kernel(n_pieces, *refs):
    pieces, hiddens, out = refs[:n_pieces], refs[n_pieces:-1], refs[-1]
    rows = jnp.concatenate([piece[...] for piece in pieces], axis=0)
    hidden = jnp.concatenate([hidden[...] for hidden in hiddens], axis=0)
    out[...] = dot(hidden, rows, 0, 0)


def tall_grad(pieces, hiddens):
    width, units = pieces[0].shape[1], hiddens[0].shape[1]
    block = min(512, width)
    rows = sum(piece.shape[0] for piece in pieces)
    out = jax.ShapeDtypeStruct((units, width), jnp.float32)
    return pl.pallas_call(
        functools.partial(tall_grad_kernel, len(pieces)),
        grid=(width // block,),
        in_specs=[pl.BlockSpec((piece.shape[0], block), lambda j: (0, j)) for piece in pieces]
        + [pl.BlockSpec(hidden.shape, lambda j: (0, 0)) for hidden in hiddens],
        out_specs=pl.BlockSpec((units, block), lambda j: (0, j)),
        out_shape=out,
        compiler_params=pltpu.CompilerParams(vmem_limit_bytes=VMEM_BYTES),
        cost_estimate=cost(2 * rows * width * units, *pieces, *hiddens, out),
    )(*pieces, *hiddens)


def shift(block, step):
    n = lax.axis_size("depth")
    return lax.ppermute(block, "depth", [(i, (i + step) % n) for i in range(n)])


def swap(block, bit):
    n = lax.axis_size("col")
    return lax.ppermute(block, "col", [(i, i ^ bit) for i in range(n)])


def row_moves(partial):
    n = lax.axis_size("row")
    return [
        lax.ppermute(partial, "row", [(i, (i + step) % n) for i in range(n)])
        for step in range(1, n)
    ]


def row_sum(partial, moved, *others):
    return sum([wide(after(block, *others)) for block in moved], wide(partial))


def add(*blocks):
    return narrow(sum(wide(block) for block in blocks))


def grads_of(gate, up, hidden_grad):
    sigma = jax.nn.sigmoid(gate)
    gate_grad = narrow(hidden_grad * up * sigma * (1.0 + gate * (1.0 - sigma)))
    return gate_grad, narrow(hidden_grad * (gate * sigma))


def hidden_of(gate, up):
    return narrow(gate * jax.nn.sigmoid(gate) * up)


def sync(*arrays):
    return lax.optimization_barrier(arrays)


def other_cores(blocks):
    return [swap(block, CORE) for block in blocks]


def chip_part(parts):
    near, far, other_near, other_far = parts
    moved = swap(other_far, CORE)
    size = far.shape[0] // 2
    sent = [add(x, y) for x, y in ((far[:size], moved[:size]), (far[size:], moved[size:]))]
    return sent, [near, swap(after(other_near, *sent), CORE)]


def block_sum(kept, block, *moved):
    size = kept[0].shape[0] // 2
    rows = slice(block * size, (block + 1) * size)
    return sum(wide(x) for x in (*(x[rows] for x in kept), *moved))


def quad(near, far, moved):
    return [*near, *far, *moved]


def body(tokens, gate_weight, up_weight, down_weight, cotangent):
    pair = [gate_weight, up_weight]

    def pair_sums(partial, moved):
        half = partial.shape[0] // 2
        total = row_sum(partial, moved)
        return total[:half], total[half:]

    far0, near1, cot_core0 = sync(
        swap(tokens, CHIP), shift(tokens, 1), swap(cotangent, CORE)
    )
    head = 16 * (cotangent.shape[0] // 48)
    cot_head, cot_tail = cotangent[:head], cotangent[head:]

    far1, near3 = swap(near1, CHIP), shift(after(tokens, near1), 3)
    head3 = shift(after(cot_head, near1), 3)
    core0, far_core0, core1 = other_cores([after(tokens, near1), far0, near1])
    token0 = quad([tokens], [far0], [core0, far_core0])
    pair0 = contract(token0, pair)
    far1, near3, head3, core1, pair0 = sync(far1, near3, head3, core1, pair0)

    pair0_moved = row_moves(pair0)
    near2, tail3 = (shift(after(x, pair0), k) for x, k in ((near1, 1), (cot_tail, 3)))
    far3, far_head0 = swap(near3, CHIP), swap(after(cot_head, pair0), CHIP)
    token1 = quad([near1], [far1], [core1, swap(far1, CORE)])
    pair1 = contract(token1, pair)
    near2, tail3, far3, far_head0, pair1, *pair0_moved = sync(
        near2, tail3, far3, far_head0, pair1, *pair0_moved
    )

    gate0, up0 = pair_sums(pair0, pair0_moved)
    hidden0 = hidden_of(gate0, up0)
    pair1_moved = row_moves(pair1)
    cot_near3 = jnp.concatenate([head3, tail3], axis=0)
    cot_near2 = shift(cot_near3, 3)
    far2, far_head3 = swap(near2, CHIP), swap(after(head3, pair1), CHIP)
    token3 = quad([near3], [far3], other_cores([after(near3, pair1), far3]))
    pair3 = contract(token3, pair)
    cot_near2, far2, far_head3, pair3, *pair1_moved = sync(
        cot_near2, far2, far_head3, pair3, *pair1_moved
    )

    gate1, up1 = pair_sums(pair1, pair1_moved)
    hidden1 = hidden_of(gate1, up1)
    pair3_moved = row_moves(pair3)
    cot = after(cotangent, pair3)
    cot_near1 = shift(cot, 1)
    cot_far2, far_tail3 = swap(cot_near2, CHIP), swap(after(tail3, pair3), CHIP)
    token2 = quad([near2], [far2], other_cores([after(near2, pair3), far2]))
    pair2 = contract(token2, pair)
    far_head0_core = swap(after(far_head0, pair3), CORE)
    cot_near1, cot_far2, far_tail3, pair2, far_head0_core, *pair3_moved = sync(
        cot_near1, cot_far2, far_tail3, pair2, far_head0_core, *pair3_moved
    )

    gate3, up3 = pair_sums(pair3, pair3_moved)
    hidden3 = hidden_of(gate3, up3)
    pair2_moved = row_moves(pair2)
    cot_far1, far_tail0 = swap(cot_near1, CHIP), swap(after(cot_tail, pair2), CHIP)
    cot_far3 = [after(far_head3, pair2), far_tail3]
    cot3 = quad([cot_near3], cot_far3, other_cores([after(cot_near3, pair2), *cot_far3]))
    cot2 = quad([cot_near2], [cot_far2], other_cores([after(cot_near2, pair2), cot_far2]))
    products = down_products(cot3 + cot2, [hidden0, hidden1], down_weight)
    cot_far1, far_tail0, grad_b, *rest = sync(cot_far1, far_tail0, *products, *pair2_moved)
    parts, pair2_moved = rest[:4], rest[4:]

    gate2, up2 = pair_sums(pair2, pair2_moved)
    hidden2 = hidden_of(gate2, up2)
    grad_b_moved = row_moves(grad_b)
    (mixed_sent0, sent), mixed_a = chip_part(parts)
    mixed_a_moved = swap(sent, CHIP)
    cot_far0 = [far_head0, far_tail0]
    cot0 = quad([cotangent], cot_far0, [cot_core0, far_head0_core, swap(far_tail0, CORE)])
    cot1 = quad([cot_near1], [cot_far1], other_cores([after(cot_near1, grad_b), cot_far1]))
    products = down_products(cot0 + cot1, [hidden3, hidden2], down_weight)
    mixed_a_moved, mixed_a[1], mixed_sent0, grad_a, *rest = sync(
        mixed_a_moved, mixed_a[1], mixed_sent0, *products, *grad_b_moved
    )
    parts, grad_b_moved = rest[:4], rest[4:]

    grad_a_moved = row_moves(grad_a)
    sent, mixed_b = chip_part(parts)
    mixed_b_moved = swap(jnp.concatenate(sent, axis=0), CHIP)
    grad_b = row_sum(grad_b, grad_b_moved)
    half = grad_b.shape[0] // 2
    grads3 = grads_of(gate3, up3, grad_b[:half])
    grads2 = grads_of(gate2, up2, grad_b[half:])
    parts = expand([[x, y] for x, y in zip(grads3, grads2)], pair)
    mixed_b_moved, mixed_b[1], *rest = sync(mixed_b_moved, mixed_b[1], *parts, *grad_a_moved)
    parts, grad_a_moved = rest[:4], rest[4:]

    sent, token_grad_b = chip_part(parts)
    token_b_moved = swap(jnp.concatenate(sent, axis=0), CHIP)
    grad_a = row_sum(grad_a, grad_a_moved)
    size = tokens.shape[0]
    moved = after(mixed_b_moved, *sent)
    mixed_part3 = shift(narrow(block_sum(mixed_b, 0, moved[:size])), 1)
    mixed_part2 = shift(narrow(block_sum(mixed_b, 1, moved[size:])), -1)
    grads0 = grads_of(gate0, up0, grad_a[:half])
    grads1 = grads_of(gate1, up1, grad_a[half:])
    parts = expand([[x, y] for x, y in zip(grads0, grads1)], pair)
    token_b_moved, token_grad_b[1], mixed_part3, mixed_part2, *parts = sync(
        token_b_moved, token_grad_b[1], mixed_part3, mixed_part2, *parts
    )

    (token_sent0, sent), token_grad_a = chip_part(parts)
    token_a_moved = swap(sent, CHIP)
    moved = after(token_b_moved, sent)
    part3 = shift(narrow(block_sum(token_grad_b, 0, moved[:size])), 1)
    part2 = shift(narrow(block_sum(token_grad_b, 1, moved[size:])), -1)
    down_total = tall_grad(
        cot0 + cot1 + cot3 + cot2, [after(hidden0, sent), hidden1, hidden3, hidden2]
    )
    token_a_moved, token_grad_a[1], token_sent0, part2, part3, down_total = sync(
        token_a_moved, token_grad_a[1], token_sent0, part2, part3, down_total
    )

    moved0 = swap(jnp.concatenate([mixed_sent0, token_sent0], axis=0), CHIP)
    back = [
        block_sum(mixed_a, 1, mixed_a_moved, mixed_part2),
        block_sum(token_grad_a, 1, token_a_moved, part2),
    ]
    back = shift(narrow(jnp.concatenate(back, axis=0)), -1)
    gate_total, up_total = wide_grads(
        [after(tokens, down_total), *token0[1:], *token1, *token3, *token2],
        [grads0[0], grads1[0], grads3[0], grads2[0]],
        [grads0[1], grads1[1], grads3[1], grads2[1]],
    )
    moved0, back, mixed_part3, part3, gate_total = sync(
        moved0, back, mixed_part3, part3, gate_total
    )
    mixed = block_sum(mixed_a, 0, moved0[:size], mixed_part3, back[:size])
    token_grad = block_sum(token_grad_a, 0, moved0[size:], part3, back[size:])
    return (mixed, token_grad, gate_total, up_total, down_total)


def solution(mesh):
    activations = P(("depth", "col"), "row")
    wide_weight = P("row", ("col", "depth"))
    tall_weight = P(("col", "depth"), "row")
    return jax.shard_map(
        body,
        mesh=mesh,
        in_specs=(activations, wide_weight, wide_weight, tall_weight, activations),
        out_specs=(activations, activations, wide_weight, wide_weight, tall_weight),
        check_vma=False,
    )
```

```python
import functools

import jax
import jax.numpy as jnp
from jax import lax
from jax.experimental import pallas as pl
from jax.experimental.pallas import tpu as pltpu
from jax.sharding import PartitionSpec as P

CORE, CHIP = 1, 2
VMEM_BYTES = 56 * 1024 * 1024


def dot(left, right, left_dim, right_dim):
    return lax.dot_general(
        left, right, (((left_dim,), (right_dim,)), ((), ())), preferred_element_type=jnp.float32
    )


def after(array, *others):
    return lax.optimization_barrier((array, *others))[0]


def wide(block):
    return block.astype(jnp.float32)


def narrow(block):
    return block.astype(jnp.bfloat16)


def cost(flops, *arrays):
    moved = sum(array.size * array.dtype.itemsize for array in arrays)
    return pl.CostEstimate(flops=flops, bytes_accessed=moved, transcendentals=0)


def contract_kernel(n_pieces, n_weights, *refs):
    pieces, weights = refs[:n_pieces], refs[n_pieces : n_pieces + n_weights]
    out, total = refs[-2:]
    step = pl.program_id(0)

    @pl.when(step == 0)
    def _():
        total[...] = jnp.zeros_like(total)

    rows = jnp.concatenate([piece[...] for piece in pieces], axis=0)
    weight = jnp.concatenate([weight[...] for weight in weights], axis=1)
    total[...] += dot(rows, weight, 1, 0)

    @pl.when(step == pl.num_programs(0) - 1)
    def _():
        size, units = rows.shape[0], total.shape[1] // n_weights
        for i in range(n_weights):
            out[i * size : (i + 1) * size] = narrow(total[:, i * units : (i + 1) * units])


def contract(pieces, weights):
    width = pieces[0].shape[1]
    units = weights[0].shape[1]
    block = min(1024, width)
    weight_spec = pl.BlockSpec((block, units), lambda k: (k, 0))
    rows = sum(piece.shape[0] for piece in pieces)
    shape = (rows * len(weights), units)
    return pl.pallas_call(
        functools.partial(contract_kernel, len(pieces), len(weights)),
        grid=(width // block,),
        in_specs=[pl.BlockSpec((piece.shape[0], block), lambda k: (0, k)) for piece in pieces]
        + [weight_spec] * len(weights),
        out_specs=pl.BlockSpec(shape, lambda k: (0, 0)),
        out_shape=jax.ShapeDtypeStruct(shape, jnp.bfloat16),
        scratch_shapes=[pltpu.VMEM((rows, units * len(weights)), jnp.float32)],
        compiler_params=pltpu.CompilerParams(vmem_limit_bytes=VMEM_BYTES),
        cost_estimate=cost(2 * len(weights) * rows * width * units, *pieces, *weights),
    )(*pieces, *weights)


def store_parts(total, outs):
    size = total.shape[0] // 8
    for i, out in enumerate(outs):
        for block in range(2):
            first = (4 * block + i) * size
            out[block * size : (block + 1) * size] = narrow(total[first : first + size])


def expand_kernel(n, *refs):
    lefts, weights, outs = refs[: 2 * n], refs[2 * n : 3 * n], refs[3 * n :]
    left = [
        jnp.concatenate([block[...] for block in lefts[2 * i : 2 * i + 2]], axis=0)
        for i in range(n)
    ]
    weight = jnp.concatenate([weight[...] for weight in weights], axis=1)
    store_parts(dot(jnp.concatenate(left, axis=1), weight, 1, 1), outs)


def expand(lefts, weights):
    blocks = sum(lefts, [])
    rows, units = blocks[0].shape
    width = weights[0].shape[0]
    block = min(512, width)
    out = jax.ShapeDtypeStruct((rows // 2, width), jnp.bfloat16)
    return pl.pallas_call(
        functools.partial(expand_kernel, len(lefts)),
        grid=(width // block,),
        in_specs=[pl.BlockSpec((rows, units), lambda j: (0, 0))] * len(blocks)
        + [pl.BlockSpec((block, units), lambda j: (j, 0))] * len(weights),
        out_specs=[pl.BlockSpec(out.shape[:1] + (block,), lambda j: (0, j))] * 4,
        out_shape=[out] * 4,
        compiler_params=pltpu.CompilerParams(vmem_limit_bytes=VMEM_BYTES),
        cost_estimate=cost(4 * len(lefts) * rows * width * units, *blocks, *weights, *[out] * 4),
    )(*blocks, *weights)


def down_kernel(n_pieces, *refs):
    pieces, (first, second, weight, grad, *outs, total) = refs[:n_pieces], refs[n_pieces:]
    step = pl.program_id(0)

    @pl.when(step == 0)
    def _():
        total[...] = jnp.zeros_like(total)

    rows = jnp.concatenate([piece[...] for piece in pieces], axis=0)
    total[...] += dot(rows, weight[...], 1, 1)
    hidden = jnp.concatenate([first[...], second[...]], axis=0)
    store_parts(dot(hidden, weight[...], 1, 0), outs)

    @pl.when(step == pl.num_programs(0) - 1)
    def _():
        grad[...] = narrow(total[...])


def down_products(pieces, hiddens, weight):
    units, width = weight.shape
    block = min(512, width)
    rows = sum(piece.shape[0] for piece in pieces)
    half = hiddens[0].shape[0]
    grad = jax.ShapeDtypeStruct((rows, units), jnp.bfloat16)
    out = jax.ShapeDtypeStruct((half // 2, width), jnp.bfloat16)
    return pl.pallas_call(
        functools.partial(down_kernel, len(pieces)),
        grid=(width // block,),
        in_specs=[pl.BlockSpec((piece.shape[0], block), lambda j: (0, j)) for piece in pieces]
        + [pl.BlockSpec((half, units), lambda j: (0, 0))] * 2
        + [pl.BlockSpec((units, block), lambda j: (0, j))],
        out_specs=[pl.BlockSpec(grad.shape, lambda j: (0, 0))]
        + [pl.BlockSpec((half // 2, block), lambda j: (0, j))] * 4,
        out_shape=[grad] + [out] * 4,
        scratch_shapes=[pltpu.VMEM(grad.shape, jnp.float32)],
        compiler_params=pltpu.CompilerParams(vmem_limit_bytes=VMEM_BYTES),
        cost_estimate=cost(4 * rows * width * units, *pieces, *hiddens, weight, *[out] * 4),
    )(*pieces, *hiddens, weight)


def wide_grad_kernel(n_pieces, *refs):
    pieces, grads, outs = refs[:n_pieces], refs[n_pieces:-2], refs[-2:]
    rows = jnp.concatenate([piece[...] for piece in pieces], axis=0)
    half = len(grads) // 2
    grad = [
        jnp.concatenate([grad[...] for grad in grads[i * half : (i + 1) * half]], axis=0)
        for i in range(2)
    ]
    both = dot(rows, jnp.concatenate(grad, axis=1), 0, 0)
    units = both.shape[1] // 2
    for i, out in enumerate(outs):
        out[...] = both[:, i * units : (i + 1) * units]


def wide_grads(pieces, gate_grads, up_grads):
    grads = [*gate_grads, *up_grads]
    width, units = pieces[0].shape[1], grads[0].shape[1]
    block = min(512, width)
    rows = sum(piece.shape[0] for piece in pieces)
    out = jax.ShapeDtypeStruct((width, units), jnp.float32)
    return pl.pallas_call(
        functools.partial(wide_grad_kernel, len(pieces)),
        grid=(width // block,),
        in_specs=[pl.BlockSpec((piece.shape[0], block), lambda j: (0, j)) for piece in pieces]
        + [pl.BlockSpec(grad.shape, lambda j: (0, 0)) for grad in grads],
        out_specs=[pl.BlockSpec((block, units), lambda j: (j, 0))] * 2,
        out_shape=[out, out],
        compiler_params=pltpu.CompilerParams(vmem_limit_bytes=VMEM_BYTES),
        cost_estimate=cost(4 * rows * width * units, *pieces, *grads, out, out),
    )(*pieces, *grads)


def tall_grad_kernel(n_pieces, *refs):
    pieces, hiddens, out = refs[:n_pieces], refs[n_pieces:-1], refs[-1]
    rows = jnp.concatenate([piece[...] for piece in pieces], axis=0)
    hidden = jnp.concatenate([hidden[...] for hidden in hiddens], axis=0)
    out[...] = dot(hidden, rows, 0, 0)


def tall_grad(pieces, hiddens):
    width, units = pieces[0].shape[1], hiddens[0].shape[1]
    block = min(512, width)
    rows = sum(piece.shape[0] for piece in pieces)
    out = jax.ShapeDtypeStruct((units, width), jnp.float32)
    return pl.pallas_call(
        functools.partial(tall_grad_kernel, len(pieces)),
        grid=(width // block,),
        in_specs=[pl.BlockSpec((piece.shape[0], block), lambda j: (0, j)) for piece in pieces]
        + [pl.BlockSpec(hidden.shape, lambda j: (0, 0)) for hidden in hiddens],
        out_specs=pl.BlockSpec((units, block), lambda j: (0, j)),
        out_shape=out,
        compiler_params=pltpu.CompilerParams(vmem_limit_bytes=VMEM_BYTES),
        cost_estimate=cost(2 * rows * width * units, *pieces, *hiddens, out),
    )(*pieces, *hiddens)


def shift(block, step):
    n = lax.axis_size("depth")
    return lax.ppermute(block, "depth", [(i, (i + step) % n) for i in range(n)])


def swap(block, bit):
    n = lax.axis_size("col")
    return lax.ppermute(block, "col", [(i, i ^ bit) for i in range(n)])


def row_moves(partial):
    n = lax.axis_size("row")
    return [
        lax.ppermute(partial, "row", [(i, (i + step) % n) for i in range(n)])
        for step in range(1, n)
    ]


def row_sum(partial, moved, *others):
    return sum([wide(after(block, *others)) for block in moved], wide(partial))


def add(*blocks):
    return narrow(sum(wide(block) for block in blocks))


def grads_of(gate, up, hidden_grad):
    sigma = jax.nn.sigmoid(gate)
    gate_grad = narrow(hidden_grad * up * sigma * (1.0 + gate * (1.0 - sigma)))
    return gate_grad, narrow(hidden_grad * (gate * sigma))


def hidden_of(gate, up):
    return narrow(gate * jax.nn.sigmoid(gate) * up)


def sync(*arrays):
    return lax.optimization_barrier(arrays)


def other_cores(blocks):
    return [swap(block, CORE) for block in blocks]


def chip_part(parts):
    near, far, other_near, other_far = parts
    moved = swap(other_far, CORE)
    size = far.shape[0] // 2
    sent = [add(x, y) for x, y in ((far[:size], moved[:size]), (far[size:], moved[size:]))]
    return sent, [near, swap(after(other_near, *sent), CORE)]


def block_sum(kept, block, *moved):
    size = kept[0].shape[0] // 2
    rows = slice(block * size, (block + 1) * size)
    return sum(wide(x) for x in (*(x[rows] for x in kept), *moved))


def quad(near, far, moved):
    return [*near, *far, *moved]


def body(tokens, gate_weight, up_weight, down_weight, cotangent):
    pair = [gate_weight, up_weight]

    def pair_sums(partial, moved):
        half = partial.shape[0] // 2
        total = row_sum(partial, moved)
        return total[:half], total[half:]

    head = 16 * (cotangent.shape[0] // 48)
    far0, near1, cot_core0, cot_head, cot_tail = sync(
        swap(tokens, CHIP),
        shift(tokens, 1),
        swap(cotangent, CORE),
        cotangent[:head],
        cotangent[head:],
    )

    far1, near3 = swap(near1, CHIP), shift(after(tokens, near1), 3)
    head3 = shift(after(cot_head, near1), 3)
    core0, far_core0, core1 = other_cores([after(tokens, near1), far0, near1])
    token0 = quad([tokens], [far0], [core0, far_core0])
    pair0 = contract(token0, pair)
    far1, near3, head3, core1, pair0 = sync(far1, near3, head3, core1, pair0)

    pair0_moved = row_moves(pair0)
    near2, tail3 = (shift(after(x, pair0), k) for x, k in ((near1, 1), (cot_tail, 3)))
    far3, far_head0 = swap(near3, CHIP), swap(after(cot_head, pair0), CHIP)
    token1 = quad([near1], [far1], [core1, swap(far1, CORE)])
    pair1 = contract(token1, pair)
    near2, tail3, far3, far_head0, pair1, *pair0_moved = sync(
        near2, tail3, far3, far_head0, pair1, *pair0_moved
    )

    gate0, up0 = pair_sums(pair0, pair0_moved)
    hidden0 = hidden_of(gate0, up0)
    pair1_moved = row_moves(pair1)
    cot_near3 = jnp.concatenate([head3, tail3], axis=0)
    cot_near2 = shift(cot_near3, 3)
    far2, far_head3 = swap(near2, CHIP), swap(after(head3, pair1), CHIP)
    token3 = quad([near3], [far3], other_cores([after(near3, pair1), far3]))
    pair3 = contract(token3, pair)
    far_head0_core = swap(after(far_head0, pair1), CORE)
    cot_near2, far2, far_head3, pair3, far_head0_core, *pair1_moved = sync(
        cot_near2, far2, far_head3, pair3, far_head0_core, *pair1_moved
    )

    gate1, up1 = pair_sums(pair1, pair1_moved)
    hidden1 = hidden_of(gate1, up1)
    pair3_moved = row_moves(pair3)
    cot = after(cotangent, pair3)
    cot_near1 = shift(cot, 1)
    cot_far2, far_tail3 = swap(cot_near2, CHIP), swap(after(tail3, pair3), CHIP)
    token2 = quad([near2], [far2], other_cores([after(near2, pair3), far2]))
    pair2 = contract(token2, pair)
    core3, far_head3_core = other_cores(after(x, pair3) for x in (cot_near3, far_head3))
    cot_near1, cot_far2, far_tail3, pair2, core3, far_head3_core, hidden0, hidden1, *rest = sync(
        cot_near1, cot_far2, far_tail3, pair2, core3, far_head3_core, hidden0, hidden1, *pair3_moved
    )
    pair3_moved = rest

    gate3, up3 = pair_sums(pair3, pair3_moved)
    hidden3 = hidden_of(gate3, up3)
    pair2_moved = row_moves(pair2)
    cot_far1, far_tail0 = swap(cot_near1, CHIP), swap(after(cot_tail, pair2), CHIP)
    cot_far3 = [after(far_head3, pair2), far_tail3]
    cot3 = quad([cot_near3], cot_far3, [core3, far_head3_core, swap(far_tail3, CORE)])
    cot2 = quad([cot_near2], [cot_far2], other_cores([after(cot_near2, pair2), cot_far2]))
    products = down_products(cot3 + cot2, [hidden0, hidden1], down_weight)
    cot_far1, far_tail0, grad_b, *rest = sync(cot_far1, far_tail0, *products, *pair2_moved)
    parts, pair2_moved = rest[:4], rest[4:]

    gate2, up2 = pair_sums(pair2, pair2_moved)
    hidden2 = hidden_of(gate2, up2)
    grad_b_moved = row_moves(grad_b)
    (mixed_sent0, sent), mixed_a = chip_part(parts)
    mixed_a_moved = swap(sent, CHIP)
    cot_far0 = [far_head0, far_tail0]
    cot0 = quad([cotangent], cot_far0, [cot_core0, far_head0_core, swap(far_tail0, CORE)])
    cot1 = quad([cot_near1], [cot_far1], other_cores([after(cot_near1, grad_b), cot_far1]))
    products = down_products(cot0 + cot1, [hidden3, hidden2], down_weight)
    mixed_a_moved, mixed_a[1], mixed_sent0, grad_a, *rest = sync(
        mixed_a_moved, mixed_a[1], mixed_sent0, *products, *grad_b_moved
    )
    parts, grad_b_moved = rest[:4], rest[4:]

    grad_a_moved = row_moves(grad_a)
    sent, mixed_b = chip_part(parts)
    mixed_b_moved = swap(jnp.concatenate(sent, axis=0), CHIP)
    grad_b = row_sum(grad_b, grad_b_moved)
    half = grad_b.shape[0] // 2
    grads3 = grads_of(gate3, up3, grad_b[:half])
    grads2 = grads_of(gate2, up2, grad_b[half:])
    parts = expand([[x, y] for x, y in zip(grads3, grads2)], pair)
    mixed_b_moved, mixed_b[1], *rest = sync(mixed_b_moved, mixed_b[1], *parts, *grad_a_moved)
    parts, grad_a_moved = rest[:4], rest[4:]

    sent, token_grad_b = chip_part(parts)
    token_b_moved = swap(jnp.concatenate(sent, axis=0), CHIP)
    grad_a = row_sum(grad_a, grad_a_moved, *sent)
    size = tokens.shape[0]
    mixed_part3 = shift(narrow(block_sum(mixed_b, 0, mixed_b_moved[:size])), 1)
    mixed_part2 = shift(narrow(block_sum(mixed_b, 1, mixed_b_moved[size:])), -1)
    grads0 = grads_of(gate0, up0, grad_a[:half])
    grads1 = grads_of(gate1, up1, grad_a[half:])
    parts = expand([[x, y] for x, y in zip(grads0, grads1)], pair)
    token_b_moved, token_grad_b[1], mixed_part3, mixed_part2, *parts = sync(
        token_b_moved, token_grad_b[1], mixed_part3, mixed_part2, *parts
    )

    (token_sent0, sent), token_grad_a = chip_part(parts)
    token_a_moved = swap(sent, CHIP)
    part3 = shift(narrow(block_sum(token_grad_b, 0, token_b_moved[:size])), 1)
    part2 = shift(narrow(block_sum(token_grad_b, 1, token_b_moved[size:])), -1)
    down_total = tall_grad(
        cot0 + cot1 + cot3 + cot2, [after(hidden0, sent), hidden1, hidden3, hidden2]
    )
    token_a_moved, token_grad_a[1], token_sent0, part2, part3, down_total = sync(
        token_a_moved, token_grad_a[1], token_sent0, part2, part3, down_total
    )

    moved0 = swap(jnp.concatenate([mixed_sent0, token_sent0], axis=0), CHIP)
    back = [
        block_sum(mixed_a, 1, mixed_a_moved, mixed_part2),
        block_sum(token_grad_a, 1, token_a_moved, part2),
    ]
    back = shift(narrow(jnp.concatenate(back, axis=0)), -1)
    gate_total, up_total = wide_grads(
        [after(tokens, down_total), *token0[1:], *token1, *token3, *token2],
        [grads0[0], grads1[0], grads3[0], grads2[0]],
        [grads0[1], grads1[1], grads3[1], grads2[1]],
    )
    moved0, back, mixed_part3, part3, gate_total = sync(
        moved0, back, mixed_part3, part3, gate_total
    )
    mixed = block_sum(mixed_a, 0, moved0[:size], mixed_part3, back[:size])
    token_grad = block_sum(token_grad_a, 0, moved0[size:], part3, back[size:])
    return (mixed, token_grad, gate_total, up_total, down_total)


def solution(mesh):
    activations = P(("depth", "col"), "row")
    wide_weight = P("row", ("col", "depth"))
    tall_weight = P(("col", "depth"), "row")
    return jax.shard_map(
        body,
        mesh=mesh,
        in_specs=(activations, wide_weight, wide_weight, tall_weight, activations),
        out_specs=(activations, activations, wide_weight, wide_weight, tall_weight),
        check_vma=False,
    )
```

```python
import functools

import jax
import jax.numpy as jnp
from jax import lax
from jax.experimental import pallas as pl
from jax.experimental.pallas import tpu as pltpu
from jax.sharding import PartitionSpec as P

CORE, CHIP = 1, 2
VMEM_BYTES = 56 * 1024 * 1024


def dot(left, right, left_dim, right_dim):
    return lax.dot_general(
        left, right, (((left_dim,), (right_dim,)), ((), ())), preferred_element_type=jnp.float32
    )


def after(array, *others):
    return lax.optimization_barrier((array, *others))[0]


def wide(block):
    return block.astype(jnp.float32)


def narrow(block):
    return block.astype(jnp.bfloat16)


def cost(flops, *arrays):
    moved = sum(array.size * array.dtype.itemsize for array in arrays)
    return pl.CostEstimate(flops=flops, bytes_accessed=moved, transcendentals=0)


def contract_kernel(n_pieces, n_weights, *refs):
    pieces, weights = refs[:n_pieces], refs[n_pieces : n_pieces + n_weights]
    out, total = refs[-2:]
    step = pl.program_id(0)

    @pl.when(step == 0)
    def _():
        total[...] = jnp.zeros_like(total)

    rows = jnp.concatenate([piece[...] for piece in pieces], axis=0)
    weight = jnp.concatenate([weight[...] for weight in weights], axis=1)
    total[...] += dot(rows, weight, 1, 0)

    @pl.when(step == pl.num_programs(0) - 1)
    def _():
        size, units = rows.shape[0], total.shape[1] // n_weights
        for i in range(n_weights):
            out[i * size : (i + 1) * size] = narrow(total[:, i * units : (i + 1) * units])


def contract(pieces, weights):
    width = pieces[0].shape[1]
    units = weights[0].shape[1]
    block = min(512, width)
    deep = pl.Buffered(4)
    rows = sum(piece.shape[0] for piece in pieces)
    out = jax.ShapeDtypeStruct((rows * len(weights), units), jnp.bfloat16)
    n_ins = len(pieces) + len(weights)

    def kernel(*refs):
        pltpu.emit_pipeline(
            lambda *blocks: contract_kernel(len(pieces), len(weights), *blocks, refs[-1]),
            grid=(width // block,),
            in_specs=[
                pl.BlockSpec((piece.shape[0], block), lambda k: (0, k), pipeline_mode=deep)
                for piece in pieces
            ]
            + [pl.BlockSpec((block, units), lambda k: (k, 0), pipeline_mode=deep)] * len(weights),
            out_specs=[pl.BlockSpec(out.shape, lambda k: (0, 0))],
        )(*refs[:-1])

    return pl.pallas_call(
        kernel,
        in_specs=[pl.BlockSpec(memory_space=pl.ANY)] * n_ins,
        out_specs=pl.BlockSpec(memory_space=pl.ANY),
        out_shape=out,
        scratch_shapes=[pltpu.VMEM((rows, units * len(weights)), jnp.float32)],
        compiler_params=pltpu.CompilerParams(vmem_limit_bytes=VMEM_BYTES),
        cost_estimate=cost(2 * len(weights) * rows * width * units, *pieces, *weights),
    )(*pieces, *weights)


def store_parts(total, outs):
    size = total.shape[0] // 8
    for i, out in enumerate(outs):
        for block in range(2):
            first = (4 * block + i) * size
            out[block * size : (block + 1) * size] = narrow(total[first : first + size])


def expand_kernel(n, *refs):
    lefts, weights, outs = refs[: 2 * n], refs[2 * n : 3 * n], refs[3 * n :]
    left = [
        jnp.concatenate([block[...] for block in lefts[2 * i : 2 * i + 2]], axis=0)
        for i in range(n)
    ]
    weight = jnp.concatenate([weight[...] for weight in weights], axis=1)
    store_parts(dot(jnp.concatenate(left, axis=1), weight, 1, 1), outs)


def expand(lefts, weights):
    blocks = sum(lefts, [])
    rows, units = blocks[0].shape
    width = weights[0].shape[0]
    block = min(512, width)
    out = jax.ShapeDtypeStruct((rows // 2, width), jnp.bfloat16)
    return pl.pallas_call(
        functools.partial(expand_kernel, len(lefts)),
        grid=(width // block,),
        in_specs=[pl.BlockSpec((rows, units), lambda j: (0, 0))] * len(blocks)
        + [pl.BlockSpec((block, units), lambda j: (j, 0))] * len(weights),
        out_specs=[pl.BlockSpec(out.shape[:1] + (block,), lambda j: (0, j))] * 4,
        out_shape=[out] * 4,
        compiler_params=pltpu.CompilerParams(vmem_limit_bytes=VMEM_BYTES),
        cost_estimate=cost(4 * len(lefts) * rows * width * units, *blocks, *weights, *[out] * 4),
    )(*blocks, *weights)


def down_kernel(n_pieces, *refs):
    pieces, (first, second, weight, grad, *outs, total) = refs[:n_pieces], refs[n_pieces:]
    step = pl.program_id(0)

    @pl.when(step == 0)
    def _():
        total[...] = jnp.zeros_like(total)

    rows = jnp.concatenate([piece[...] for piece in pieces], axis=0)
    total[...] += dot(rows, weight[...], 1, 1)
    hidden = jnp.concatenate([first[...], second[...]], axis=0)
    store_parts(dot(hidden, weight[...], 1, 0), outs)

    @pl.when(step == pl.num_programs(0) - 1)
    def _():
        grad[...] = narrow(total[...])


def down_products(pieces, hiddens, weight):
    units, width = weight.shape
    block = min(1024, width)
    rows = sum(piece.shape[0] for piece in pieces)
    half = hiddens[0].shape[0]
    grad = jax.ShapeDtypeStruct((rows, units), jnp.bfloat16)
    out = jax.ShapeDtypeStruct((half // 2, width), jnp.bfloat16)
    return pl.pallas_call(
        functools.partial(down_kernel, len(pieces)),
        grid=(width // block,),
        in_specs=[pl.BlockSpec((piece.shape[0], block), lambda j: (0, j)) for piece in pieces]
        + [pl.BlockSpec((half, units), lambda j: (0, 0))] * 2
        + [pl.BlockSpec((units, block), lambda j: (0, j))],
        out_specs=[pl.BlockSpec(grad.shape, lambda j: (0, 0))]
        + [pl.BlockSpec((half // 2, block), lambda j: (0, j))] * 4,
        out_shape=[grad] + [out] * 4,
        scratch_shapes=[pltpu.VMEM(grad.shape, jnp.float32)],
        compiler_params=pltpu.CompilerParams(vmem_limit_bytes=VMEM_BYTES),
        cost_estimate=cost(4 * rows * width * units, *pieces, *hiddens, weight, *[out] * 4),
    )(*pieces, *hiddens, weight)


def wide_grad_kernel(n_pieces, *refs):
    pieces, grads, outs = refs[:n_pieces], refs[n_pieces:-2], refs[-2:]
    rows = jnp.concatenate([piece[...] for piece in pieces], axis=0)
    half = len(grads) // 2
    grad = [
        jnp.concatenate([grad[...] for grad in grads[i * half : (i + 1) * half]], axis=0)
        for i in range(2)
    ]
    both = dot(rows, jnp.concatenate(grad, axis=1), 0, 0)
    units = both.shape[1] // 2
    for i, out in enumerate(outs):
        out[...] = both[:, i * units : (i + 1) * units]


def wide_grads(pieces, gate_grads, up_grads):
    grads = [*gate_grads, *up_grads]
    width, units = pieces[0].shape[1], grads[0].shape[1]
    block = min(512, width)
    rows = sum(piece.shape[0] for piece in pieces)
    out = jax.ShapeDtypeStruct((width, units), jnp.float32)
    return pl.pallas_call(
        functools.partial(wide_grad_kernel, len(pieces)),
        grid=(width // block,),
        in_specs=[pl.BlockSpec((piece.shape[0], block), lambda j: (0, j)) for piece in pieces]
        + [pl.BlockSpec(grad.shape, lambda j: (0, 0)) for grad in grads],
        out_specs=[pl.BlockSpec((block, units), lambda j: (j, 0))] * 2,
        out_shape=[out, out],
        compiler_params=pltpu.CompilerParams(vmem_limit_bytes=VMEM_BYTES),
        cost_estimate=cost(4 * rows * width * units, *pieces, *grads, out, out),
    )(*pieces, *grads)


def tall_grad_kernel(n_pieces, *refs):
    pieces, hiddens, out = refs[:n_pieces], refs[n_pieces:-1], refs[-1]
    rows = jnp.concatenate([piece[...] for piece in pieces], axis=0)
    hidden = jnp.concatenate([hidden[...] for hidden in hiddens], axis=0)
    out[...] = dot(hidden, rows, 0, 0)


def tall_grad(pieces, hiddens):
    width, units = pieces[0].shape[1], hiddens[0].shape[1]
    block = min(512, width)
    rows = sum(piece.shape[0] for piece in pieces)
    out = jax.ShapeDtypeStruct((units, width), jnp.float32)
    return pl.pallas_call(
        functools.partial(tall_grad_kernel, len(pieces)),
        grid=(width // block,),
        in_specs=[pl.BlockSpec((piece.shape[0], block), lambda j: (0, j)) for piece in pieces]
        + [pl.BlockSpec(hidden.shape, lambda j: (0, 0)) for hidden in hiddens],
        out_specs=pl.BlockSpec((units, block), lambda j: (0, j)),
        out_shape=out,
        compiler_params=pltpu.CompilerParams(vmem_limit_bytes=VMEM_BYTES),
        cost_estimate=cost(2 * rows * width * units, *pieces, *hiddens, out),
    )(*pieces, *hiddens)


def shift(block, step):
    n = lax.axis_size("depth")
    return lax.ppermute(block, "depth", [(i, (i + step) % n) for i in range(n)])


def swap(block, bit):
    n = lax.axis_size("col")
    return lax.ppermute(block, "col", [(i, i ^ bit) for i in range(n)])


def row_moves(partial):
    n = lax.axis_size("row")
    return [
        lax.ppermute(partial, "row", [(i, (i + step) % n) for i in range(n)])
        for step in range(1, n)
    ]


def row_sum(partial, moved):
    return sum([wide(block) for block in moved], wide(partial))


def add(*blocks):
    return narrow(sum(wide(block) for block in blocks))


def grads_of(gate, up, hidden_grad):
    sigma = jax.nn.sigmoid(gate)
    gate_grad = narrow(hidden_grad * up * sigma * (1.0 + gate * (1.0 - sigma)))
    return gate_grad, narrow(hidden_grad * (gate * sigma))


def hidden_of(gate, up):
    return narrow(gate * jax.nn.sigmoid(gate) * up)


def sync(*arrays):
    return lax.optimization_barrier(arrays)


def other_cores(blocks):
    return [swap(block, CORE) for block in blocks]


def chip_part(parts):
    near, far, other_near, other_far = parts
    moved = swap(other_far, CORE)
    size = far.shape[0] // 2
    sent = [add(x, y) for x, y in ((far[:size], moved[:size]), (far[size:], moved[size:]))]
    return sent, [near, swap(after(other_near, *sent), CORE)]


def block_sum(kept, block, *moved):
    size = kept[0].shape[0] // 2
    rows = slice(block * size, (block + 1) * size)
    return sum(wide(x) for x in (*(x[rows] for x in kept), *moved))


def quad(near, far, moved):
    return [*near, *far, *moved]


def body(tokens, gate_weight, up_weight, down_weight, cotangent):
    pair = [gate_weight, up_weight]

    def half_sums(partial, moved, *others):
        half = partial.shape[0] // 2
        moved = [after(block, *others) for block in moved]
        return [
            row_sum(partial[at], [block[at] for block in moved])
            for at in (slice(0, half), slice(half, 2 * half))
        ]

    def pair_sums(partial, moved):
        half = partial.shape[0] // 2
        total = row_sum(partial, moved)
        return total[:half], total[half:]

    head = 16 * (cotangent.shape[0] // 48)
    far0, near1, cot_core0, cot_head, cot_tail = sync(
        swap(tokens, CHIP),
        shift(tokens, 1),
        swap(cotangent, CORE),
        cotangent[:head],
        cotangent[head:],
    )

    far1, near3 = swap(near1, CHIP), shift(after(tokens, near1), 3)
    head3 = shift(after(cot_head, near1), 3)
    core0, far_core0, core1 = other_cores([after(tokens, near1), far0, near1])
    token0 = quad([tokens], [far0], [core0, far_core0])
    pair0 = contract(token0, pair)
    far1, near3, head3, core1, pair0 = sync(far1, near3, head3, core1, pair0)

    pair0_moved = row_moves(pair0)
    near2, tail3 = (shift(after(x, pair0), k) for x, k in ((near1, 1), (cot_tail, 3)))
    far3, far_head0 = swap(near3, CHIP), swap(after(cot_head, pair0), CHIP)
    token1 = quad([near1], [far1], [core1, swap(far1, CORE)])
    pair1 = contract(token1, pair)
    near2, tail3, far3, far_head0, pair1, *pair0_moved = sync(
        near2, tail3, far3, far_head0, pair1, *pair0_moved
    )

    gate0, up0 = half_sums(pair0, pair0_moved)
    hidden0 = hidden_of(gate0, up0)
    pair1_moved = row_moves(pair1)
    cot_near3 = jnp.concatenate([head3, tail3], axis=0)
    cot_near2 = shift(cot_near3, 3)
    far2, far_tail3 = swap(near2, CHIP), swap(after(tail3, pair1), CHIP)
    token3 = quad([near3], [far3], other_cores([after(near3, pair1), far3]))
    pair3 = contract(token3, pair)
    far_head0_core = swap(after(far_head0, pair1), CORE)
    cot_near2, far2, far_tail3, pair3, far_head0_core, *pair1_moved = sync(
        cot_near2, far2, far_tail3, pair3, far_head0_core, *pair1_moved
    )

    gate1, up1 = half_sums(pair1, pair1_moved)
    hidden1 = hidden_of(gate1, up1)
    pair3_moved = row_moves(pair3)
    cot = after(cotangent, pair3)
    cot_near1 = shift(cot, 1)
    cot_far2, far_head3 = swap(cot_near2, CHIP), swap(after(head3, pair3), CHIP)
    token2 = quad([near2], [far2], other_cores([after(near2, pair3), far2]))
    pair2 = contract(token2, pair)
    core3, far_tail3_core = other_cores(after(x, pair3) for x in (cot_near3, far_tail3))
    cot_near1, cot_far2, far_head3, pair2, core3, far_tail3_core, hidden0, hidden1, *rest = sync(
        cot_near1, cot_far2, far_head3, pair2, core3, far_tail3_core, hidden0, hidden1, *pair3_moved
    )
    pair3_moved = rest

    gate3, up3 = pair_sums(pair3, pair3_moved)
    hidden3 = hidden_of(gate3, up3)
    pair2_moved = row_moves(pair2)
    cot_far1, far_tail0 = swap(cot_near1, CHIP), swap(after(cot_tail, pair2), CHIP)
    cot_far3 = [far_head3, far_tail3]
    cot3 = quad([cot_near3], cot_far3, [core3, swap(far_head3, CORE), far_tail3_core])
    cot2 = quad([cot_near2], [cot_far2], other_cores([after(cot_near2, pair2), cot_far2]))
    products = down_products(cot3 + cot2, [hidden0, hidden1], down_weight)
    cot_far1, far_tail0, grad_b, *rest = sync(cot_far1, far_tail0, *products, *pair2_moved)
    parts, pair2_moved = rest[:4], rest[4:]

    gate2, up2 = pair_sums(pair2, pair2_moved)
    hidden2 = hidden_of(gate2, up2)
    grad_b_moved = row_moves(grad_b)
    (mixed_sent0, sent), mixed_a = chip_part(parts)
    mixed_a_moved = swap(sent, CHIP)
    cot_far0 = [far_head0, far_tail0]
    cot0 = quad([cotangent], cot_far0, [cot_core0, far_head0_core, swap(far_tail0, CORE)])
    cot1 = quad([cot_near1], [cot_far1], other_cores([after(cot_near1, grad_b), cot_far1]))
    products = down_products(cot0 + cot1, [hidden3, hidden2], down_weight)
    mixed_a_moved, mixed_a[1], mixed_sent0, grad_a, *rest = sync(
        mixed_a_moved, mixed_a[1], mixed_sent0, *products, *grad_b_moved
    )
    parts, grad_b_moved = rest[:4], rest[4:]

    grad_a_moved = row_moves(grad_a)
    sent, mixed_b = chip_part(parts)
    mixed_b_moved = swap(jnp.concatenate(sent, axis=0), CHIP)
    grad3, grad2 = half_sums(grad_b, grad_b_moved)
    grads3, grads2 = grads_of(gate3, up3, grad3), grads_of(gate2, up2, grad2)
    parts = expand([[x, y] for x, y in zip(grads3, grads2)], pair)
    mixed_b_moved, mixed_b[1], *rest = sync(mixed_b_moved, mixed_b[1], *parts, *grad_a_moved)
    parts, grad_a_moved = rest[:4], rest[4:]

    sent, token_grad_b = chip_part(parts)
    token_b_moved = swap(jnp.concatenate(sent, axis=0), CHIP)
    grad0, grad1 = half_sums(grad_a, grad_a_moved, *sent)
    size = tokens.shape[0]
    mixed_part3 = shift(narrow(block_sum(mixed_b, 0, mixed_b_moved[:size])), 1)
    mixed_part2 = shift(narrow(block_sum(mixed_b, 1, mixed_b_moved[size:])), -1)
    grads0, grads1 = grads_of(gate0, up0, grad0), grads_of(gate1, up1, grad1)
    parts = expand([[x, y] for x, y in zip(grads0, grads1)], pair)
    token_b_moved, token_grad_b[1], mixed_part3, mixed_part2, *parts = sync(
        token_b_moved, token_grad_b[1], mixed_part3, mixed_part2, *parts
    )

    (token_sent0, sent), token_grad_a = chip_part(parts)
    token_a_moved = swap(sent, CHIP)
    part3 = shift(narrow(block_sum(token_grad_b, 0, token_b_moved[:size])), 1)
    part2 = shift(narrow(block_sum(token_grad_b, 1, token_b_moved[size:])), -1)
    down_total = tall_grad(
        cot0 + cot1 + cot3 + cot2, [after(hidden0, sent), hidden1, hidden3, hidden2]
    )
    token_a_moved, token_grad_a[1], token_sent0, part2, part3, down_total = sync(
        token_a_moved, token_grad_a[1], token_sent0, part2, part3, down_total
    )

    moved0 = swap(jnp.concatenate([mixed_sent0, token_sent0], axis=0), CHIP)
    back = [
        block_sum(mixed_a, 1, mixed_a_moved, mixed_part2),
        block_sum(token_grad_a, 1, token_a_moved, part2),
    ]
    back = shift(narrow(jnp.concatenate(back, axis=0)), -1)
    gate_total, up_total = wide_grads(
        [after(tokens, down_total), *token0[1:], *token1, *token3, *token2],
        [grads0[0], grads1[0], grads3[0], grads2[0]],
        [grads0[1], grads1[1], grads3[1], grads2[1]],
    )
    moved0, back, mixed_part3, part3, gate_total = sync(
        moved0, back, mixed_part3, part3, gate_total
    )
    mixed = block_sum(mixed_a, 0, moved0[:size], mixed_part3, back[:size])
    token_grad = block_sum(token_grad_a, 0, moved0[size:], part3, back[size:])
    return (mixed, token_grad, gate_total, up_total, down_total)


def solution(mesh):
    activations = P(("depth", "col"), "row")
    wide_weight = P("row", ("col", "depth"))
    tall_weight = P(("col", "depth"), "row")
    return jax.shard_map(
        body,
        mesh=mesh,
        in_specs=(activations, wide_weight, wide_weight, tall_weight, activations),
        out_specs=(activations, activations, wide_weight, wide_weight, tall_weight),
        check_vma=False,
    )
```

```python
import functools

import jax
import jax.numpy as jnp
from jax import lax
from jax.experimental import pallas as pl
from jax.experimental.pallas import tpu as pltpu
from jax.sharding import PartitionSpec as P

CORE, CHIP = 1, 2
VMEM_BYTES = 56 * 1024 * 1024


def dot(left, right, left_dim, right_dim):
    return lax.dot_general(
        left, right, (((left_dim,), (right_dim,)), ((), ())), preferred_element_type=jnp.float32
    )


def after(array, *others):
    return lax.optimization_barrier((array, *others))[0]


def wide(block):
    return block.astype(jnp.float32)


def narrow(block):
    return block.astype(jnp.bfloat16)


def cost(flops, *arrays):
    moved = sum(array.size * array.dtype.itemsize for array in arrays)
    return pl.CostEstimate(flops=flops, bytes_accessed=moved, transcendentals=0)


def contract_kernel(n_pieces, n_weights, *refs):
    pieces, weights = refs[:n_pieces], refs[n_pieces : n_pieces + n_weights]
    out, total = refs[-2:]
    step = pl.program_id(0)

    @pl.when(step == 0)
    def _():
        total[...] = jnp.zeros_like(total)

    rows = jnp.concatenate([piece[...] for piece in pieces], axis=0)
    weight = jnp.concatenate([weight[...] for weight in weights], axis=1)
    total[...] += dot(rows, weight, 1, 0)

    @pl.when(step == pl.num_programs(0) - 1)
    def _():
        size, units = rows.shape[0], total.shape[1] // n_weights
        for i in range(n_weights):
            out[i * size : (i + 1) * size] = narrow(total[:, i * units : (i + 1) * units])


def contract(pieces, weights):
    width = pieces[0].shape[1]
    units = weights[0].shape[1]
    block = min(512, width)
    deep = pl.Buffered(4)
    rows = sum(piece.shape[0] for piece in pieces)
    out = jax.ShapeDtypeStruct((rows * len(weights), units), jnp.bfloat16)
    n_ins = len(pieces) + len(weights)

    def kernel(*refs):
        pltpu.emit_pipeline(
            lambda *blocks: contract_kernel(len(pieces), len(weights), *blocks, refs[-1]),
            grid=(width // block,),
            in_specs=[
                pl.BlockSpec((piece.shape[0], block), lambda k: (0, k), pipeline_mode=deep)
                for piece in pieces
            ]
            + [pl.BlockSpec((block, units), lambda k: (k, 0), pipeline_mode=deep)] * len(weights),
            out_specs=[pl.BlockSpec(out.shape, lambda k: (0, 0))],
        )(*refs[:-1])

    return pl.pallas_call(
        kernel,
        in_specs=[pl.BlockSpec(memory_space=pl.ANY)] * n_ins,
        out_specs=pl.BlockSpec(memory_space=pl.ANY),
        out_shape=out,
        scratch_shapes=[pltpu.VMEM((rows, units * len(weights)), jnp.float32)],
        compiler_params=pltpu.CompilerParams(vmem_limit_bytes=VMEM_BYTES),
        cost_estimate=cost(2 * len(weights) * rows * width * units, *pieces, *weights),
    )(*pieces, *weights)


def store_parts(total, outs):
    size = total.shape[0] // 8
    for i, out in enumerate(outs):
        for block in range(2):
            first = (4 * block + i) * size
            out[block * size : (block + 1) * size] = narrow(total[first : first + size])


def expand_kernel(n, *refs):
    lefts, weights, outs = refs[: 2 * n], refs[2 * n : 3 * n], refs[3 * n :]
    left = [
        jnp.concatenate([block[...] for block in lefts[2 * i : 2 * i + 2]], axis=0)
        for i in range(n)
    ]
    weight = jnp.concatenate([weight[...] for weight in weights], axis=1)
    store_parts(dot(jnp.concatenate(left, axis=1), weight, 1, 1), outs)


def expand(lefts, weights):
    blocks = sum(lefts, [])
    rows, units = blocks[0].shape
    width = weights[0].shape[0]
    block = min(1024, width)
    out = jax.ShapeDtypeStruct((rows // 2, width), jnp.bfloat16)
    return pl.pallas_call(
        functools.partial(expand_kernel, len(lefts)),
        grid=(width // block,),
        in_specs=[pl.BlockSpec((rows, units), lambda j: (0, 0))] * len(blocks)
        + [pl.BlockSpec((block, units), lambda j: (j, 0))] * len(weights),
        out_specs=[pl.BlockSpec(out.shape[:1] + (block,), lambda j: (0, j))] * 4,
        out_shape=[out] * 4,
        compiler_params=pltpu.CompilerParams(vmem_limit_bytes=VMEM_BYTES),
        cost_estimate=cost(4 * len(lefts) * rows * width * units, *blocks, *weights, *[out] * 4),
    )(*blocks, *weights)


def down_kernel(n_pieces, *refs):
    pieces, (first, second, weight, grad, *outs, total) = refs[:n_pieces], refs[n_pieces:]
    step = pl.program_id(0)

    @pl.when(step == 0)
    def _():
        total[...] = jnp.zeros_like(total)

    rows = jnp.concatenate([piece[...] for piece in pieces], axis=0)
    total[...] += dot(rows, weight[...], 1, 1)
    hidden = jnp.concatenate([first[...], second[...]], axis=0)
    store_parts(dot(hidden, weight[...], 1, 0), outs)

    @pl.when(step == pl.num_programs(0) - 1)
    def _():
        grad[...] = narrow(total[...])


def down_products(pieces, hiddens, weight):
    units, width = weight.shape
    block = min(1024, width)
    rows = sum(piece.shape[0] for piece in pieces)
    half = hiddens[0].shape[0]
    grad = jax.ShapeDtypeStruct((rows, units), jnp.bfloat16)
    out = jax.ShapeDtypeStruct((half // 2, width), jnp.bfloat16)
    return pl.pallas_call(
        functools.partial(down_kernel, len(pieces)),
        grid=(width // block,),
        in_specs=[pl.BlockSpec((piece.shape[0], block), lambda j: (0, j)) for piece in pieces]
        + [pl.BlockSpec((half, units), lambda j: (0, 0))] * 2
        + [pl.BlockSpec((units, block), lambda j: (0, j))],
        out_specs=[pl.BlockSpec(grad.shape, lambda j: (0, 0))]
        + [pl.BlockSpec((half // 2, block), lambda j: (0, j))] * 4,
        out_shape=[grad] + [out] * 4,
        scratch_shapes=[pltpu.VMEM(grad.shape, jnp.float32)],
        compiler_params=pltpu.CompilerParams(vmem_limit_bytes=VMEM_BYTES),
        cost_estimate=cost(4 * rows * width * units, *pieces, *hiddens, weight, *[out] * 4),
    )(*pieces, *hiddens, weight)


def wide_grad_kernel(n_pieces, *refs):
    pieces, grads, outs = refs[:n_pieces], refs[n_pieces:-2], refs[-2:]
    rows = jnp.concatenate([piece[...] for piece in pieces], axis=0)
    half = len(grads) // 2
    grad = [
        jnp.concatenate([grad[...] for grad in grads[i * half : (i + 1) * half]], axis=0)
        for i in range(2)
    ]
    both = dot(rows, jnp.concatenate(grad, axis=1), 0, 0)
    units = both.shape[1] // 2
    for i, out in enumerate(outs):
        out[...] = both[:, i * units : (i + 1) * units]


def wide_grads(pieces, gate_grads, up_grads):
    grads = [*gate_grads, *up_grads]
    width, units = pieces[0].shape[1], grads[0].shape[1]
    block = min(512, width)
    rows = sum(piece.shape[0] for piece in pieces)
    out = jax.ShapeDtypeStruct((width, units), jnp.float32)
    return pl.pallas_call(
        functools.partial(wide_grad_kernel, len(pieces)),
        grid=(width // block,),
        in_specs=[pl.BlockSpec((piece.shape[0], block), lambda j: (0, j)) for piece in pieces]
        + [pl.BlockSpec(grad.shape, lambda j: (0, 0)) for grad in grads],
        out_specs=[pl.BlockSpec((block, units), lambda j: (j, 0))] * 2,
        out_shape=[out, out],
        compiler_params=pltpu.CompilerParams(vmem_limit_bytes=VMEM_BYTES),
        cost_estimate=cost(4 * rows * width * units, *pieces, *grads, out, out),
    )(*pieces, *grads)


def tall_grad_kernel(n_pieces, *refs):
    pieces, hiddens, out = refs[:n_pieces], refs[n_pieces:-1], refs[-1]
    rows = jnp.concatenate([piece[...] for piece in pieces], axis=0)
    hidden = jnp.concatenate([hidden[...] for hidden in hiddens], axis=0)
    out[...] = dot(hidden, rows, 0, 0)


def tall_grad(pieces, hiddens):
    width, units = pieces[0].shape[1], hiddens[0].shape[1]
    block = min(512, width)
    rows = sum(piece.shape[0] for piece in pieces)
    out = jax.ShapeDtypeStruct((units, width), jnp.float32)
    return pl.pallas_call(
        functools.partial(tall_grad_kernel, len(pieces)),
        grid=(width // block,),
        in_specs=[pl.BlockSpec((piece.shape[0], block), lambda j: (0, j)) for piece in pieces]
        + [pl.BlockSpec(hidden.shape, lambda j: (0, 0)) for hidden in hiddens],
        out_specs=pl.BlockSpec((units, block), lambda j: (0, j)),
        out_shape=out,
        compiler_params=pltpu.CompilerParams(vmem_limit_bytes=VMEM_BYTES),
        cost_estimate=cost(2 * rows * width * units, *pieces, *hiddens, out),
    )(*pieces, *hiddens)


def shift(block, step):
    n = lax.axis_size("depth")
    return lax.ppermute(block, "depth", [(i, (i + step) % n) for i in range(n)])


def swap(block, bit):
    n = lax.axis_size("col")
    return lax.ppermute(block, "col", [(i, i ^ bit) for i in range(n)])


def row_moves(partial):
    n = lax.axis_size("row")
    return [
        lax.ppermute(partial, "row", [(i, (i + step) % n) for i in range(n)])
        for step in range(1, n)
    ]


def row_sum(partial, moved):
    return sum([wide(block) for block in moved], wide(partial))


def add(*blocks):
    return narrow(sum(wide(block) for block in blocks))


def grads_of(gate, up, hidden_grad):
    sigma = jax.nn.sigmoid(gate)
    gate_grad = narrow(hidden_grad * up * sigma * (1.0 + gate * (1.0 - sigma)))
    return gate_grad, narrow(hidden_grad * (gate * sigma))


def hidden_of(gate, up):
    return narrow(gate * jax.nn.sigmoid(gate) * up)


def sync(*arrays):
    return lax.optimization_barrier(arrays)


def other_cores(blocks):
    return [swap(block, CORE) for block in blocks]


def chip_part(parts):
    near, far, other_near, other_far = parts
    moved = swap(other_far, CORE)
    size = far.shape[0] // 2
    sent = [add(x, y) for x, y in ((far[:size], moved[:size]), (far[size:], moved[size:]))]
    return sent, [near, swap(after(other_near, *sent), CORE)]


def block_sum(kept, block, *moved):
    size = kept[0].shape[0] // 2
    rows = slice(block * size, (block + 1) * size)
    return sum(wide(x) for x in (*(x[rows] for x in kept), *moved))


def quad(near, far, moved):
    return [*near, *far, *moved]


def body(tokens, gate_weight, up_weight, down_weight, cotangent):
    pair = [gate_weight, up_weight]

    def half_sums(partial, moved):
        half = partial.shape[0] // 2
        return [
            row_sum(partial[at], [block[at] for block in moved])
            for at in (slice(0, half), slice(half, 2 * half))
        ]

    def pair_sums(partial, moved):
        half = partial.shape[0] // 2
        total = row_sum(partial, moved)
        return total[:half], total[half:]

    head = 16 * (cotangent.shape[0] // 48)
    far0, near1, cot_core0, cot_head, cot_tail = sync(
        swap(tokens, CHIP),
        shift(tokens, 1),
        swap(cotangent, CORE),
        cotangent[:head],
        cotangent[head:],
    )

    far1, near3 = swap(near1, CHIP), shift(after(tokens, near1), 3)
    head3 = shift(after(cot_head, near1), 3)
    core0, far_core0, core1 = other_cores([after(tokens, near1), far0, near1])
    token0 = quad([tokens], [far0], [core0, far_core0])
    pair0 = contract(token0, pair)
    far1, near3, head3, core1, pair0 = sync(far1, near3, head3, core1, pair0)

    pair0_moved = row_moves(pair0)
    near2, tail3 = (shift(after(x, pair0), k) for x, k in ((near1, 1), (cot_tail, 3)))
    far3, far_tail0 = swap(near3, CHIP), swap(after(cot_tail, pair0), CHIP)
    token1 = quad([near1], [far1], [core1, swap(far1, CORE)])
    pair1 = contract(token1, pair)
    near2, tail3, far3, far_tail0, pair1, *pair0_moved = sync(
        near2, tail3, far3, far_tail0, pair1, *pair0_moved
    )

    gate0, up0 = half_sums(pair0, pair0_moved)
    hidden0 = hidden_of(gate0, up0)
    pair1_moved = row_moves(pair1)
    cot_near3 = jnp.concatenate([head3, tail3], axis=0)
    cot_near2 = shift(cot_near3, 3)
    far2, far_tail3 = swap(near2, CHIP), swap(after(tail3, pair1), CHIP)
    token3 = quad([near3], [far3], other_cores([after(near3, pair1), far3]))
    pair3 = contract(token3, pair)
    far_tail0_core = swap(after(far_tail0, pair1), CORE)
    cot_near2, far2, far_tail3, pair3, far_tail0_core, *pair1_moved = sync(
        cot_near2, far2, far_tail3, pair3, far_tail0_core, *pair1_moved
    )

    gate1, up1 = half_sums(pair1, pair1_moved)
    hidden1 = hidden_of(gate1, up1)
    pair3_moved = row_moves(pair3)
    cot = after(cotangent, pair3)
    cot_near1 = shift(cot, 1)
    cot_far2, far_head3 = swap(cot_near2, CHIP), swap(after(head3, pair3), CHIP)
    token2 = quad([near2], [far2], other_cores([after(near2, pair3), far2]))
    pair2 = contract(token2, pair)
    core3, far_tail3_core = other_cores(after(x, pair3) for x in (cot_near3, far_tail3))
    cot_near1, cot_far2, far_head3, pair2, core3, far_tail3_core, hidden0, hidden1, *rest = sync(
        cot_near1, cot_far2, far_head3, pair2, core3, far_tail3_core, hidden0, hidden1, *pair3_moved
    )
    pair3_moved = rest

    gate3, up3 = pair_sums(pair3, pair3_moved)
    hidden3 = hidden_of(gate3, up3)
    pair2_moved = row_moves(pair2)
    cot_far1, far_head0 = swap(cot_near1, CHIP), swap(after(cot_head, pair2), CHIP)
    cot_far3 = [far_head3, far_tail3]
    cot3 = quad([cot_near3], cot_far3, [core3, swap(far_head3, CORE), far_tail3_core])
    cot2 = quad([cot_near2], [cot_far2], other_cores([after(cot_near2, pair2), cot_far2]))
    products = down_products(cot3 + cot2, [hidden0, hidden1], down_weight)
    cot_far1, far_head0, grad_b, *rest = sync(cot_far1, far_head0, *products, *pair2_moved)
    parts, pair2_moved = rest[:4], rest[4:]

    gate2, up2 = pair_sums(pair2, pair2_moved)
    hidden2 = hidden_of(gate2, up2)
    grad_b_moved = row_moves(grad_b)
    (mixed_sent0, sent), mixed_a = chip_part(parts)
    mixed_a_moved = swap(sent, CHIP)
    cot_far0 = [far_head0, far_tail0]
    cot0 = quad([cotangent], cot_far0, [cot_core0, swap(far_head0, CORE), far_tail0_core])
    cot1 = quad([cot_near1], [cot_far1], other_cores([after(cot_near1, grad_b), cot_far1]))
    products = down_products(cot0 + cot1, [hidden3, hidden2], down_weight)
    mixed_a_moved, mixed_a[1], mixed_sent0, grad_a, *rest = sync(
        mixed_a_moved, mixed_a[1], mixed_sent0, *products, *grad_b_moved
    )
    parts, grad_b_moved = rest[:4], rest[4:]

    grad_a_moved = row_moves(grad_a)
    sent, mixed_b = chip_part(parts)
    mixed_b_moved = swap(jnp.concatenate(sent, axis=0), CHIP)
    grad3, grad2 = pair_sums(grad_b, grad_b_moved)
    grads3, grads2 = grads_of(gate3, up3, grad3), grads_of(gate2, up2, grad2)
    parts = expand([[x, y] for x, y in zip(grads3, grads2)], pair)
    mixed_b_moved, mixed_b[1], *rest = sync(mixed_b_moved, mixed_b[1], *parts, *grad_a_moved)
    parts, grad_a_moved = rest[:4], rest[4:]

    sent, token_grad_b = chip_part(parts)
    token_b_moved = swap(jnp.concatenate(sent, axis=0), CHIP)
    grad0, grad1 = pair_sums(grad_a, grad_a_moved)
    size = tokens.shape[0]
    mixed_part3 = shift(narrow(block_sum(mixed_b, 0, mixed_b_moved[:size])), 1)
    mixed_part2 = shift(narrow(block_sum(mixed_b, 1, mixed_b_moved[size:])), -1)
    grads0, grads1 = grads_of(gate0, up0, grad0), grads_of(gate1, up1, grad1)
    parts = expand([[x, y] for x, y in zip(grads0, grads1)], pair)
    token_b_moved, token_grad_b[1], mixed_part3, mixed_part2, *parts = sync(
        token_b_moved, token_grad_b[1], mixed_part3, mixed_part2, *parts
    )

    (token_sent0, sent), token_grad_a = chip_part(parts)
    token_a_moved = swap(sent, CHIP)
    part3 = shift(narrow(block_sum(token_grad_b, 0, token_b_moved[:size])), 1)
    part2 = shift(narrow(block_sum(token_grad_b, 1, token_b_moved[size:])), -1)
    down_total = tall_grad(
        cot0 + cot1 + cot3 + cot2, [after(hidden0, sent), hidden1, hidden3, hidden2]
    )
    token_a_moved, token_grad_a[1], token_sent0, part2, part3, down_total = sync(
        token_a_moved, token_grad_a[1], token_sent0, part2, part3, down_total
    )

    moved0 = swap(jnp.concatenate([mixed_sent0, token_sent0], axis=0), CHIP)
    back = [
        block_sum(mixed_a, 1, mixed_a_moved, mixed_part2),
        block_sum(token_grad_a, 1, token_a_moved, part2),
    ]
    back = shift(narrow(jnp.concatenate(back, axis=0)), -1)
    gate_total, up_total = wide_grads(
        [after(tokens, down_total), *token0[1:], *token1, *token3, *token2],
        [grads0[0], grads1[0], grads3[0], grads2[0]],
        [grads0[1], grads1[1], grads3[1], grads2[1]],
    )
    moved0, back, mixed_part3, part3, gate_total = sync(
        moved0, back, mixed_part3, part3, gate_total
    )
    mixed = block_sum(mixed_a, 0, moved0[:size], mixed_part3, back[:size])
    token_grad = block_sum(token_grad_a, 0, moved0[size:], part3, back[size:])
    return (mixed, token_grad, gate_total, up_total, down_total)


def solution(mesh):
    activations = P(("depth", "col"), "row")
    wide_weight = P("row", ("col", "depth"))
    tall_weight = P(("col", "depth"), "row")
    return jax.shard_map(
        body,
        mesh=mesh,
        in_specs=(activations, wide_weight, wide_weight, tall_weight, activations),
        out_specs=(activations, activations, wide_weight, wide_weight, tall_weight),
        check_vma=False,
    )
```

```python
import functools

import jax
import jax.numpy as jnp
from jax import lax
from jax.experimental import pallas as pl
from jax.experimental.pallas import tpu as pltpu
from jax.sharding import PartitionSpec as P

CORE, CHIP = 1, 2
VMEM_BYTES = 56 * 1024 * 1024


def dot(left, right, left_dim, right_dim):
    return lax.dot_general(
        left, right, (((left_dim,), (right_dim,)), ((), ())), preferred_element_type=jnp.float32
    )


def after(array, *others):
    return lax.optimization_barrier((array, *others))[0]


def wide(block):
    return block.astype(jnp.float32)


def narrow(block):
    return block.astype(jnp.bfloat16)


def cost(flops, *arrays):
    moved = sum(array.size * array.dtype.itemsize for array in arrays)
    return pl.CostEstimate(flops=flops, bytes_accessed=moved, transcendentals=0)


def contract_kernel(n_pieces, n_weights, *refs):
    pieces, weights = refs[:n_pieces], refs[n_pieces : n_pieces + n_weights]
    out, total = refs[-2:]
    step = pl.program_id(0)

    @pl.when(step == 0)
    def _():
        total[...] = jnp.zeros_like(total)

    rows = jnp.concatenate([piece[...] for piece in pieces], axis=0)
    weight = jnp.concatenate([weight[...] for weight in weights], axis=1)
    total[...] += dot(rows, weight, 1, 0)

    @pl.when(step == pl.num_programs(0) - 1)
    def _():
        size, units = rows.shape[0], total.shape[1] // n_weights
        for i in range(n_weights):
            out[i * size : (i + 1) * size] = narrow(total[:, i * units : (i + 1) * units])


def contract(pieces, weights):
    width = pieces[0].shape[1]
    units = weights[0].shape[1]
    block = min(512, width)
    deep = pl.Buffered(4)
    rows = sum(piece.shape[0] for piece in pieces)
    out = jax.ShapeDtypeStruct((rows * len(weights), units), jnp.bfloat16)
    n_ins = len(pieces) + len(weights)

    def kernel(*refs):
        pltpu.emit_pipeline(
            lambda *blocks: contract_kernel(len(pieces), len(weights), *blocks, refs[-1]),
            grid=(width // block,),
            in_specs=[
                pl.BlockSpec((piece.shape[0], block), lambda k: (0, k), pipeline_mode=deep)
                for piece in pieces
            ]
            + [pl.BlockSpec((block, units), lambda k: (k, 0), pipeline_mode=deep)] * len(weights),
            out_specs=[pl.BlockSpec(out.shape, lambda k: (0, 0))],
        )(*refs[:-1])

    return pl.pallas_call(
        kernel,
        in_specs=[pl.BlockSpec(memory_space=pl.ANY)] * n_ins,
        out_specs=pl.BlockSpec(memory_space=pl.ANY),
        out_shape=out,
        scratch_shapes=[pltpu.VMEM((rows, units * len(weights)), jnp.float32)],
        compiler_params=pltpu.CompilerParams(vmem_limit_bytes=VMEM_BYTES),
        cost_estimate=cost(2 * len(weights) * rows * width * units, *pieces, *weights),
    )(*pieces, *weights)


def store_parts(total, outs):
    size = total.shape[0] // 8
    for i, out in enumerate(outs):
        for block in range(2):
            first = (4 * block + i) * size
            out[block * size : (block + 1) * size] = narrow(total[first : first + size])


def expand_kernel(n, *refs):
    lefts, weights, outs = refs[: 2 * n], refs[2 * n : 3 * n], refs[3 * n :]
    left = [
        jnp.concatenate([block[...] for block in lefts[2 * i : 2 * i + 2]], axis=0)
        for i in range(n)
    ]
    weight = jnp.concatenate([weight[...] for weight in weights], axis=1)
    store_parts(dot(jnp.concatenate(left, axis=1), weight, 1, 1), outs)


def expand(lefts, weights):
    blocks = sum(lefts, [])
    rows, units = blocks[0].shape
    width = weights[0].shape[0]
    block = min(1024, width)
    out = jax.ShapeDtypeStruct((rows // 2, width), jnp.bfloat16)
    return pl.pallas_call(
        functools.partial(expand_kernel, len(lefts)),
        grid=(width // block,),
        in_specs=[pl.BlockSpec((rows, units), lambda j: (0, 0))] * len(blocks)
        + [pl.BlockSpec((block, units), lambda j: (j, 0))] * len(weights),
        out_specs=[pl.BlockSpec(out.shape[:1] + (block,), lambda j: (0, j))] * 4,
        out_shape=[out] * 4,
        compiler_params=pltpu.CompilerParams(vmem_limit_bytes=VMEM_BYTES),
        cost_estimate=cost(4 * len(lefts) * rows * width * units, *blocks, *weights, *[out] * 4),
    )(*blocks, *weights)


def down_kernel(n_pieces, *refs):
    pieces, (first, second, weight, grad, *outs, total) = refs[:n_pieces], refs[n_pieces:]
    step = pl.program_id(0)

    @pl.when(step == 0)
    def _():
        total[...] = jnp.zeros_like(total)

    rows = jnp.concatenate([piece[...] for piece in pieces], axis=0)
    total[...] += dot(rows, weight[...], 1, 1)
    hidden = jnp.concatenate([first[...], second[...]], axis=0)
    store_parts(dot(hidden, weight[...], 1, 0), outs)

    @pl.when(step == pl.num_programs(0) - 1)
    def _():
        grad[...] = narrow(total[...])


def down_products(pieces, hiddens, weight):
    units, width = weight.shape
    block = min(1024, width)
    rows = sum(piece.shape[0] for piece in pieces)
    half = hiddens[0].shape[0]
    grad = jax.ShapeDtypeStruct((rows, units), jnp.bfloat16)
    out = jax.ShapeDtypeStruct((half // 2, width), jnp.bfloat16)
    return pl.pallas_call(
        functools.partial(down_kernel, len(pieces)),
        grid=(width // block,),
        in_specs=[pl.BlockSpec((piece.shape[0], block), lambda j: (0, j)) for piece in pieces]
        + [pl.BlockSpec((half, units), lambda j: (0, 0))] * 2
        + [pl.BlockSpec((units, block), lambda j: (0, j))],
        out_specs=[pl.BlockSpec(grad.shape, lambda j: (0, 0))]
        + [pl.BlockSpec((half // 2, block), lambda j: (0, j))] * 4,
        out_shape=[grad] + [out] * 4,
        scratch_shapes=[pltpu.VMEM(grad.shape, jnp.float32)],
        compiler_params=pltpu.CompilerParams(vmem_limit_bytes=VMEM_BYTES),
        cost_estimate=cost(4 * rows * width * units, *pieces, *hiddens, weight, *[out] * 4),
    )(*pieces, *hiddens, weight)


def wide_grad_kernel(n_pieces, *refs):
    pieces, grads, outs = refs[:n_pieces], refs[n_pieces:-2], refs[-2:]
    rows = jnp.concatenate([piece[...] for piece in pieces], axis=0)
    half = len(grads) // 2
    grad = [
        jnp.concatenate([grad[...] for grad in grads[i * half : (i + 1) * half]], axis=0)
        for i in range(2)
    ]
    both = dot(rows, jnp.concatenate(grad, axis=1), 0, 0)
    units = both.shape[1] // 2
    for i, out in enumerate(outs):
        out[...] = both[:, i * units : (i + 1) * units]


def wide_grads(pieces, gate_grads, up_grads):
    grads = [*gate_grads, *up_grads]
    width, units = pieces[0].shape[1], grads[0].shape[1]
    block = min(1024, width)
    rows = sum(piece.shape[0] for piece in pieces)
    out = jax.ShapeDtypeStruct((width, units), jnp.float32)
    return pl.pallas_call(
        functools.partial(wide_grad_kernel, len(pieces)),
        grid=(width // block,),
        in_specs=[pl.BlockSpec((piece.shape[0], block), lambda j: (0, j)) for piece in pieces]
        + [pl.BlockSpec(grad.shape, lambda j: (0, 0)) for grad in grads],
        out_specs=[pl.BlockSpec((block, units), lambda j: (j, 0))] * 2,
        out_shape=[out, out],
        compiler_params=pltpu.CompilerParams(vmem_limit_bytes=VMEM_BYTES),
        cost_estimate=cost(4 * rows * width * units, *pieces, *grads, out, out),
    )(*pieces, *grads)


def tall_grad_kernel(n_pieces, *refs):
    pieces, hiddens, out = refs[:n_pieces], refs[n_pieces:-1], refs[-1]
    rows = jnp.concatenate([piece[...] for piece in pieces], axis=0)
    hidden = jnp.concatenate([hidden[...] for hidden in hiddens], axis=0)
    out[...] = dot(hidden, rows, 0, 0)


def tall_grad(pieces, hiddens):
    width, units = pieces[0].shape[1], hiddens[0].shape[1]
    block = min(512, width)
    rows = sum(piece.shape[0] for piece in pieces)
    out = jax.ShapeDtypeStruct((units, width), jnp.float32)
    return pl.pallas_call(
        functools.partial(tall_grad_kernel, len(pieces)),
        grid=(width // block,),
        in_specs=[pl.BlockSpec((piece.shape[0], block), lambda j: (0, j)) for piece in pieces]
        + [pl.BlockSpec(hidden.shape, lambda j: (0, 0)) for hidden in hiddens],
        out_specs=pl.BlockSpec((units, block), lambda j: (0, j)),
        out_shape=out,
        compiler_params=pltpu.CompilerParams(vmem_limit_bytes=VMEM_BYTES),
        cost_estimate=cost(2 * rows * width * units, *pieces, *hiddens, out),
    )(*pieces, *hiddens)


def shift(block, step):
    n = lax.axis_size("depth")
    return lax.ppermute(block, "depth", [(i, (i + step) % n) for i in range(n)])


def swap(block, bit):
    n = lax.axis_size("col")
    return lax.ppermute(block, "col", [(i, i ^ bit) for i in range(n)])


def row_moves(partial):
    n = lax.axis_size("row")
    return [
        lax.ppermute(partial, "row", [(i, (i + step) % n) for i in range(n)])
        for step in range(1, n)
    ]


def row_sum(partial, moved):
    return sum([wide(block) for block in moved], wide(partial))


def add(*blocks):
    return narrow(sum(wide(block) for block in blocks))


def grads_of(gate, up, hidden_grad):
    sigma = jax.nn.sigmoid(gate)
    gate_grad = narrow(hidden_grad * up * sigma * (1.0 + gate * (1.0 - sigma)))
    return gate_grad, narrow(hidden_grad * (gate * sigma))


def hidden_of(gate, up):
    return narrow(gate * jax.nn.sigmoid(gate) * up)


def sync(*arrays):
    return lax.optimization_barrier(arrays)


def other_cores(blocks):
    return [swap(block, CORE) for block in blocks]


def chip_part(parts):
    near, far, other_near, other_far = parts
    moved = swap(other_far, CORE)
    size = far.shape[0] // 2
    sent = [add(x, y) for x, y in ((far[:size], moved[:size]), (far[size:], moved[size:]))]
    return sent, [near, swap(after(other_near, *sent), CORE)]


def block_sum(kept, block, *moved):
    size = kept[0].shape[0] // 2
    rows = slice(block * size, (block + 1) * size)
    return sum(wide(x) for x in (*(x[rows] for x in kept), *moved))


def quad(near, far, moved):
    return [*near, *far, *moved]


def body(tokens, gate_weight, up_weight, down_weight, cotangent):
    pair = [gate_weight, up_weight]

    def half_sums(partial, moved):
        half = partial.shape[0] // 2
        return [
            row_sum(partial[at], [block[at] for block in moved])
            for at in (slice(0, half), slice(half, 2 * half))
        ]

    def pair_sums(partial, moved):
        half = partial.shape[0] // 2
        total = row_sum(partial, moved)
        return total[:half], total[half:]

    head = 16 * (cotangent.shape[0] // 48)
    far0, near1, cot_core0, cot_head, cot_tail = sync(
        swap(tokens, CHIP),
        shift(tokens, 1),
        swap(cotangent, CORE),
        cotangent[:head],
        cotangent[head:],
    )

    far1, near3 = swap(near1, CHIP), shift(after(tokens, near1), 3)
    head3 = shift(after(cot_head, near1), 3)
    core0, far_core0, core1 = other_cores([after(tokens, near1), far0, near1])
    token0 = quad([tokens], [far0], [core0, far_core0])
    pair0 = contract(token0, pair)
    far1, near3, head3, core1, pair0 = sync(far1, near3, head3, core1, pair0)

    pair0_moved = row_moves(pair0)
    near2, tail3 = (shift(after(x, pair0), k) for x, k in ((near1, 1), (cot_tail, 3)))
    far3, far_tail0 = swap(near3, CHIP), swap(after(cot_tail, pair0), CHIP)
    token1 = quad([near1], [far1], [core1, swap(far1, CORE)])
    pair1 = contract(token1, pair)
    near2, tail3, far3, far_tail0, pair1, *pair0_moved = sync(
        near2, tail3, far3, far_tail0, pair1, *pair0_moved
    )

    gate0, up0 = half_sums(pair0, pair0_moved)
    hidden0 = hidden_of(gate0, up0)
    pair1_moved = row_moves(pair1)
    cot_near3 = jnp.concatenate([head3, tail3], axis=0)
    cot_near2 = shift(cot_near3, 3)
    far2, far_tail3 = swap(near2, CHIP), swap(after(tail3, pair1), CHIP)
    token3 = quad([near3], [far3], other_cores([after(near3, pair1), far3]))
    pair3 = contract(token3, pair)
    far_tail0_core = swap(after(far_tail0, pair1), CORE)
    cot_near2, far2, far_tail3, pair3, far_tail0_core, *pair1_moved = sync(
        cot_near2, far2, far_tail3, pair3, far_tail0_core, *pair1_moved
    )

    gate1, up1 = half_sums(pair1, pair1_moved)
    hidden1 = hidden_of(gate1, up1)
    pair3_moved = row_moves(pair3)
    cot = after(cotangent, pair3)
    cot_near1 = shift(cot, 1)
    cot_far2, far_head3 = swap(cot_near2, CHIP), swap(after(head3, pair3), CHIP)
    token2 = quad([near2], [far2], other_cores([after(near2, pair3), far2]))
    pair2 = contract(token2, pair)
    core3, far_tail3_core = other_cores(after(x, pair3) for x in (cot_near3, far_tail3))
    cot_near1, cot_far2, far_head3, pair2, core3, far_tail3_core, hidden0, hidden1, *rest = sync(
        cot_near1, cot_far2, far_head3, pair2, core3, far_tail3_core, hidden0, hidden1, *pair3_moved
    )
    pair3_moved = rest

    gate3, up3 = pair_sums(pair3, pair3_moved)
    hidden3 = hidden_of(gate3, up3)
    pair2_moved = row_moves(pair2)
    cot_far1, far_head0 = swap(cot_near1, CHIP), swap(after(cot_head, pair2), CHIP)
    cot_far3 = [far_head3, far_tail3]
    cot3 = quad([cot_near3], cot_far3, [core3, swap(far_head3, CORE), far_tail3_core])
    cot2 = quad([cot_near2], [cot_far2], other_cores([after(cot_near2, pair2), cot_far2]))
    products = down_products(cot3 + cot2, [hidden0, hidden1], down_weight)
    cot_far1, far_head0, grad_b, *rest = sync(cot_far1, far_head0, *products, *pair2_moved)
    parts, pair2_moved = rest[:4], rest[4:]

    gate2, up2 = pair_sums(pair2, pair2_moved)
    hidden2 = hidden_of(gate2, up2)
    grad_b_moved = row_moves(grad_b)
    (mixed_sent0, sent), mixed_a = chip_part(parts)
    mixed_a_moved = swap(sent, CHIP)
    cot_far0 = [far_head0, far_tail0]
    cot0 = quad([cotangent], cot_far0, [cot_core0, swap(far_head0, CORE), far_tail0_core])
    cot1 = quad([cot_near1], [cot_far1], other_cores([after(cot_near1, grad_b), cot_far1]))
    products = down_products(cot0 + cot1, [hidden3, hidden2], down_weight)
    mixed_a_moved, mixed_a[1], mixed_sent0, grad_a, *rest = sync(
        mixed_a_moved, mixed_a[1], mixed_sent0, *products, *grad_b_moved
    )
    parts, grad_b_moved = rest[:4], rest[4:]

    grad_a_moved = row_moves(grad_a)
    sent, mixed_b = chip_part(parts)
    mixed_b_moved = swap(jnp.concatenate(sent, axis=0), CHIP)
    grad3, grad2 = pair_sums(grad_b, grad_b_moved)
    grads3, grads2 = grads_of(gate3, up3, grad3), grads_of(gate2, up2, grad2)
    parts = expand([[x, y] for x, y in zip(grads3, grads2)], pair)
    mixed_b_moved, mixed_b[1], *rest = sync(mixed_b_moved, mixed_b[1], *parts, *grad_a_moved)
    parts, grad_a_moved = rest[:4], rest[4:]

    sent, token_grad_b = chip_part(parts)
    token_b_moved = swap(jnp.concatenate(sent, axis=0), CHIP)
    grad0, grad1 = pair_sums(grad_a, grad_a_moved)
    size = tokens.shape[0]
    mixed_part3 = shift(narrow(block_sum(mixed_b, 0, mixed_b_moved[:size])), 1)
    mixed_part2 = shift(narrow(block_sum(mixed_b, 1, mixed_b_moved[size:])), -1)
    grads0, grads1 = grads_of(gate0, up0, grad0), grads_of(gate1, up1, grad1)
    parts = expand([[x, y] for x, y in zip(grads0, grads1)], pair)
    token_b_moved, token_grad_b[1], mixed_part3, mixed_part2, *parts = sync(
        token_b_moved, token_grad_b[1], mixed_part3, mixed_part2, *parts
    )

    (token_sent0, sent), token_grad_a = chip_part(parts)
    token_a_moved = swap(sent, CHIP)
    part3 = shift(narrow(block_sum(token_grad_b, 0, token_b_moved[:size])), 1)
    part2 = shift(narrow(block_sum(token_grad_b, 1, token_b_moved[size:])), -1)
    down_total = tall_grad(
        cot0 + cot1 + cot3 + cot2, [after(hidden0, sent), hidden1, hidden3, hidden2]
    )
    token_a_moved, token_grad_a[1], token_sent0, part2, part3, down_total = sync(
        token_a_moved, token_grad_a[1], token_sent0, part2, part3, down_total
    )

    moved0 = swap(jnp.concatenate([mixed_sent0, token_sent0], axis=0), CHIP)
    back = [
        block_sum(mixed_a, 1, mixed_a_moved, mixed_part2),
        block_sum(token_grad_a, 1, token_a_moved, part2),
    ]
    back = shift(narrow(jnp.concatenate(back, axis=0)), -1)
    gate_total, up_total = wide_grads(
        [after(tokens, down_total), *token0[1:], *token1, *token3, *token2],
        [grads0[0], grads1[0], grads3[0], grads2[0]],
        [grads0[1], grads1[1], grads3[1], grads2[1]],
    )
    moved0, back, mixed_part3, part3, gate_total = sync(
        moved0, back, mixed_part3, part3, gate_total
    )
    mixed = block_sum(mixed_a, 0, moved0[:size], mixed_part3, back[:size])
    token_grad = block_sum(token_grad_a, 0, moved0[size:], part3, back[size:])
    return (mixed, token_grad, gate_total, up_total, down_total)


def solution(mesh):
    activations = P(("depth", "col"), "row")
    wide_weight = P("row", ("col", "depth"))
    tall_weight = P(("col", "depth"), "row")
    return jax.shard_map(
        body,
        mesh=mesh,
        in_specs=(activations, wide_weight, wide_weight, tall_weight, activations),
        out_specs=(activations, activations, wide_weight, wide_weight, tall_weight),
        check_vma=False,
    )
```

```python
import functools

import jax
import jax.numpy as jnp
from jax import lax
from jax.experimental import pallas as pl
from jax.experimental.pallas import tpu as pltpu
from jax.sharding import PartitionSpec as P

CORE, CHIP = 1, 2
VMEM_BYTES = 56 * 1024 * 1024


def dot(left, right, left_dim, right_dim):
    return lax.dot_general(
        left, right, (((left_dim,), (right_dim,)), ((), ())), preferred_element_type=jnp.float32
    )


def after(array, *others):
    return lax.optimization_barrier((array, *others))[0]


def wide(block):
    return block.astype(jnp.float32)


def narrow(block):
    return block.astype(jnp.bfloat16)


def cost(flops, *arrays):
    moved = sum(array.size * array.dtype.itemsize for array in arrays)
    return pl.CostEstimate(flops=flops, bytes_accessed=moved, transcendentals=0)


def contract_kernel(n_pieces, n_weights, *refs):
    pieces, weights = refs[:n_pieces], refs[n_pieces : n_pieces + n_weights]
    out, total = refs[-2:]
    step = pl.program_id(0)

    @pl.when(step == 0)
    def _():
        total[...] = jnp.zeros_like(total)

    rows = jnp.concatenate([piece[...] for piece in pieces], axis=0)
    weight = jnp.concatenate([weight[...] for weight in weights], axis=1)
    total[...] += dot(rows, weight, 1, 0)

    @pl.when(step == pl.num_programs(0) - 1)
    def _():
        size, units = rows.shape[0], total.shape[1] // n_weights
        for i in range(n_weights):
            out[i * size : (i + 1) * size] = narrow(total[:, i * units : (i + 1) * units])


def contract(pieces, weights):
    width = pieces[0].shape[1]
    units = weights[0].shape[1]
    block = min(1024, width)
    deep = pl.Buffered(4)
    rows = sum(piece.shape[0] for piece in pieces)
    out = jax.ShapeDtypeStruct((rows * len(weights), units), jnp.bfloat16)
    n_ins = len(pieces) + len(weights)

    def kernel(*refs):
        pltpu.emit_pipeline(
            lambda *blocks: contract_kernel(len(pieces), len(weights), *blocks, refs[-1]),
            grid=(width // block,),
            in_specs=[
                pl.BlockSpec((piece.shape[0], block), lambda k: (0, k), pipeline_mode=deep)
                for piece in pieces
            ]
            + [pl.BlockSpec((block, units), lambda k: (k, 0), pipeline_mode=deep)] * len(weights),
            out_specs=[pl.BlockSpec(out.shape, lambda k: (0, 0))],
        )(*refs[:-1])

    return pl.pallas_call(
        kernel,
        in_specs=[pl.BlockSpec(memory_space=pl.ANY)] * n_ins,
        out_specs=pl.BlockSpec(memory_space=pl.ANY),
        out_shape=out,
        scratch_shapes=[pltpu.VMEM((rows, units * len(weights)), jnp.float32)],
        compiler_params=pltpu.CompilerParams(vmem_limit_bytes=VMEM_BYTES),
        cost_estimate=cost(2 * len(weights) * rows * width * units, *pieces, *weights),
    )(*pieces, *weights)


def store_parts(total, outs):
    size = total.shape[0] // 8
    for i, out in enumerate(outs):
        for block in range(2):
            first = (4 * block + i) * size
            out[block * size : (block + 1) * size] = narrow(total[first : first + size])


def expand_kernel(n, *refs):
    lefts, weights, outs = refs[: 2 * n], refs[2 * n : 3 * n], refs[3 * n :]
    left = [
        jnp.concatenate([block[...] for block in lefts[2 * i : 2 * i + 2]], axis=0)
        for i in range(n)
    ]
    weight = jnp.concatenate([weight[...] for weight in weights], axis=1)
    store_parts(dot(jnp.concatenate(left, axis=1), weight, 1, 1), outs)


def expand(lefts, weights):
    blocks = sum(lefts, [])
    rows, units = blocks[0].shape
    width = weights[0].shape[0]
    block = min(1024, width)
    out = jax.ShapeDtypeStruct((rows // 2, width), jnp.bfloat16)
    return pl.pallas_call(
        functools.partial(expand_kernel, len(lefts)),
        grid=(width // block,),
        in_specs=[pl.BlockSpec((rows, units), lambda j: (0, 0))] * len(blocks)
        + [pl.BlockSpec((block, units), lambda j: (j, 0))] * len(weights),
        out_specs=[pl.BlockSpec(out.shape[:1] + (block,), lambda j: (0, j))] * 4,
        out_shape=[out] * 4,
        compiler_params=pltpu.CompilerParams(vmem_limit_bytes=VMEM_BYTES),
        cost_estimate=cost(4 * len(lefts) * rows * width * units, *blocks, *weights, *[out] * 4),
    )(*blocks, *weights)


def down_kernel(n_pieces, *refs):
    pieces, (first, second, weight, grad, *outs, total) = refs[:n_pieces], refs[n_pieces:]
    step = pl.program_id(0)

    @pl.when(step == 0)
    def _():
        total[...] = jnp.zeros_like(total)

    rows = jnp.concatenate([piece[...] for piece in pieces], axis=0)
    total[...] += dot(rows, weight[...], 1, 1)
    hidden = jnp.concatenate([first[...], second[...]], axis=0)
    store_parts(dot(hidden, weight[...], 1, 0), outs)

    @pl.when(step == pl.num_programs(0) - 1)
    def _():
        grad[...] = narrow(total[...])


def down_products(pieces, hiddens, weight):
    units, width = weight.shape
    block = min(1024, width)
    rows = sum(piece.shape[0] for piece in pieces)
    half = hiddens[0].shape[0]
    grad = jax.ShapeDtypeStruct((rows, units), jnp.bfloat16)
    out = jax.ShapeDtypeStruct((half // 2, width), jnp.bfloat16)
    return pl.pallas_call(
        functools.partial(down_kernel, len(pieces)),
        grid=(width // block,),
        in_specs=[pl.BlockSpec((piece.shape[0], block), lambda j: (0, j)) for piece in pieces]
        + [pl.BlockSpec((half, units), lambda j: (0, 0))] * 2
        + [pl.BlockSpec((units, block), lambda j: (0, j))],
        out_specs=[pl.BlockSpec(grad.shape, lambda j: (0, 0))]
        + [pl.BlockSpec((half // 2, block), lambda j: (0, j))] * 4,
        out_shape=[grad] + [out] * 4,
        scratch_shapes=[pltpu.VMEM(grad.shape, jnp.float32)],
        compiler_params=pltpu.CompilerParams(vmem_limit_bytes=VMEM_BYTES),
        cost_estimate=cost(4 * rows * width * units, *pieces, *hiddens, weight, *[out] * 4),
    )(*pieces, *hiddens, weight)


def wide_grad_kernel(n_pieces, *refs):
    pieces, grads, outs = refs[:n_pieces], refs[n_pieces:-2], refs[-2:]
    rows = jnp.concatenate([piece[...] for piece in pieces], axis=0)
    half = len(grads) // 2
    grad = [
        jnp.concatenate([grad[...] for grad in grads[i * half : (i + 1) * half]], axis=0)
        for i in range(2)
    ]
    both = dot(rows, jnp.concatenate(grad, axis=1), 0, 0)
    units = both.shape[1] // 2
    for i, out in enumerate(outs):
        out[...] = both[:, i * units : (i + 1) * units]


def wide_grads(pieces, gate_grads, up_grads):
    grads = [*gate_grads, *up_grads]
    width, units = pieces[0].shape[1], grads[0].shape[1]
    block = min(1024, width)
    rows = sum(piece.shape[0] for piece in pieces)
    out = jax.ShapeDtypeStruct((width, units), jnp.float32)
    return pl.pallas_call(
        functools.partial(wide_grad_kernel, len(pieces)),
        grid=(width // block,),
        in_specs=[pl.BlockSpec((piece.shape[0], block), lambda j: (0, j)) for piece in pieces]
        + [pl.BlockSpec(grad.shape, lambda j: (0, 0)) for grad in grads],
        out_specs=[pl.BlockSpec((block, units), lambda j: (j, 0))] * 2,
        out_shape=[out, out],
        compiler_params=pltpu.CompilerParams(vmem_limit_bytes=VMEM_BYTES),
        cost_estimate=cost(4 * rows * width * units, *pieces, *grads, out, out),
    )(*pieces, *grads)


def tall_grad_kernel(n_pieces, *refs):
    pieces, hiddens, out = refs[:n_pieces], refs[n_pieces:-1], refs[-1]
    rows = jnp.concatenate([piece[...] for piece in pieces], axis=0)
    hidden = jnp.concatenate([hidden[...] for hidden in hiddens], axis=0)
    out[...] = dot(hidden, rows, 0, 0)


def tall_grad(pieces, hiddens):
    width, units = pieces[0].shape[1], hiddens[0].shape[1]
    block = min(1024, width)
    rows = sum(piece.shape[0] for piece in pieces)
    out = jax.ShapeDtypeStruct((units, width), jnp.float32)
    return pl.pallas_call(
        functools.partial(tall_grad_kernel, len(pieces)),
        grid=(width // block,),
        in_specs=[pl.BlockSpec((piece.shape[0], block), lambda j: (0, j)) for piece in pieces]
        + [pl.BlockSpec(hidden.shape, lambda j: (0, 0)) for hidden in hiddens],
        out_specs=pl.BlockSpec((units, block), lambda j: (0, j)),
        out_shape=out,
        compiler_params=pltpu.CompilerParams(vmem_limit_bytes=VMEM_BYTES),
        cost_estimate=cost(2 * rows * width * units, *pieces, *hiddens, out),
    )(*pieces, *hiddens)


def shift(block, step):
    n = lax.axis_size("depth")
    return lax.ppermute(block, "depth", [(i, (i + step) % n) for i in range(n)])


def swap(block, bit):
    n = lax.axis_size("col")
    return lax.ppermute(block, "col", [(i, i ^ bit) for i in range(n)])


def row_moves(partial):
    n = lax.axis_size("row")
    return [
        lax.ppermute(partial, "row", [(i, (i + step) % n) for i in range(n)])
        for step in range(1, n)
    ]


def row_sum(partial, moved):
    return sum([wide(block) for block in moved], wide(partial))


def add(*blocks):
    return narrow(sum(wide(block) for block in blocks))


def grads_of(gate, up, hidden_grad):
    sigma = jax.nn.sigmoid(gate)
    gate_grad = narrow(hidden_grad * up * sigma * (1.0 + gate * (1.0 - sigma)))
    return gate_grad, narrow(hidden_grad * (gate * sigma))


def hidden_of(gate, up):
    return narrow(gate * jax.nn.sigmoid(gate) * up)


def sync(*arrays):
    return lax.optimization_barrier(arrays)


def other_cores(blocks):
    return [swap(block, CORE) for block in blocks]


def chip_part(parts):
    near, far, other_near, other_far = parts
    moved = swap(other_far, CORE)
    size = far.shape[0] // 2
    sent = [add(x, y) for x, y in ((far[:size], moved[:size]), (far[size:], moved[size:]))]
    return sent, [near, swap(after(other_near, *sent), CORE)]


def block_sum(kept, block, *moved):
    size = kept[0].shape[0] // 2
    rows = slice(block * size, (block + 1) * size)
    return sum(wide(x) for x in (*(x[rows] for x in kept), *moved))


def quad(near, far, moved):
    return [*near, *far, *moved]


def body(tokens, gate_weight, up_weight, down_weight, cotangent):
    pair = [gate_weight, up_weight]

    def half_sums(partial, moved):
        half = partial.shape[0] // 2
        return [
            row_sum(partial[at], [block[at] for block in moved])
            for at in (slice(0, half), slice(half, 2 * half))
        ]

    def pair_sums(partial, moved):
        half = partial.shape[0] // 2
        total = row_sum(partial, moved)
        return total[:half], total[half:]

    head = 16 * (cotangent.shape[0] // 48)
    far0, near1, cot_core0, cot_head, cot_tail = sync(
        swap(tokens, CHIP),
        shift(tokens, 1),
        swap(cotangent, CORE),
        cotangent[:head],
        cotangent[head:],
    )

    far1, near3 = swap(near1, CHIP), shift(after(tokens, near1), 3)
    head3 = shift(after(cot_head, near1), 3)
    core0, far_core0, core1 = other_cores([after(tokens, near1), far0, near1])
    token0 = quad([tokens], [far0], [core0, far_core0])
    pair0 = contract(token0, pair)
    far1, near3, head3, core1, pair0 = sync(far1, near3, head3, core1, pair0)

    pair0_moved = row_moves(pair0)
    near2, tail3 = (shift(after(x, pair0), k) for x, k in ((near1, 1), (cot_tail, 3)))
    far3, far_tail0 = swap(near3, CHIP), swap(after(cot_tail, pair0), CHIP)
    token1 = quad([near1], [far1], [core1, swap(far1, CORE)])
    pair1 = contract(token1, pair)
    near2, tail3, far3, far_tail0, pair1, *pair0_moved = sync(
        near2, tail3, far3, far_tail0, pair1, *pair0_moved
    )

    gate0, up0 = half_sums(pair0, pair0_moved)
    hidden0 = hidden_of(gate0, up0)
    pair1_moved = row_moves(pair1)
    cot_near3 = jnp.concatenate([head3, tail3], axis=0)
    cot_near2 = shift(cot_near3, 3)
    far2, far_tail3 = swap(near2, CHIP), swap(after(tail3, pair1), CHIP)
    token3 = quad([near3], [far3], other_cores([after(near3, pair1), far3]))
    pair3 = contract(token3, pair)
    far_tail0_core = swap(after(far_tail0, pair1), CORE)
    cot_near2, far2, far_tail3, pair3, far_tail0_core, *pair1_moved = sync(
        cot_near2, far2, far_tail3, pair3, far_tail0_core, *pair1_moved
    )

    gate1, up1 = half_sums(pair1, pair1_moved)
    hidden1 = hidden_of(gate1, up1)
    pair3_moved = row_moves(pair3)
    cot = after(cotangent, pair3)
    cot_near1 = shift(cot, 1)
    cot_far2, far_head3 = swap(cot_near2, CHIP), swap(after(head3, pair3), CHIP)
    token2 = quad([near2], [far2], other_cores([after(near2, pair3), far2]))
    pair2 = contract(token2, pair)
    core3, far_tail3_core = other_cores(after(x, pair3) for x in (cot_near3, far_tail3))
    cot_near1, cot_far2, far_head3, pair2, core3, far_tail3_core, hidden0, hidden1, *rest = sync(
        cot_near1, cot_far2, far_head3, pair2, core3, far_tail3_core, hidden0, hidden1, *pair3_moved
    )
    pair3_moved = rest

    gate3, up3 = pair_sums(pair3, pair3_moved)
    hidden3 = hidden_of(gate3, up3)
    pair2_moved = row_moves(pair2)
    cot_far1, far_head0 = swap(cot_near1, CHIP), swap(after(cot_head, pair2), CHIP)
    cot_far3 = [far_head3, far_tail3]
    cot3 = quad([cot_near3], cot_far3, [core3, swap(far_head3, CORE), far_tail3_core])
    cot2 = quad([cot_near2], [cot_far2], other_cores([after(cot_near2, pair2), cot_far2]))
    products = down_products(cot3 + cot2, [hidden0, hidden1], down_weight)
    cot_far1, far_head0, grad_b, *rest = sync(cot_far1, far_head0, *products, *pair2_moved)
    parts, pair2_moved = rest[:4], rest[4:]

    gate2, up2 = pair_sums(pair2, pair2_moved)
    hidden2 = hidden_of(gate2, up2)
    grad_b_moved = row_moves(grad_b)
    (mixed_sent0, sent), mixed_a = chip_part(parts)
    mixed_a_moved = swap(sent, CHIP)
    cot_far0 = [far_head0, far_tail0]
    cot0 = quad([cotangent], cot_far0, [cot_core0, swap(far_head0, CORE), far_tail0_core])
    cot1 = quad([cot_near1], [cot_far1], other_cores([after(cot_near1, grad_b), cot_far1]))
    products = down_products(cot0 + cot1, [hidden3, hidden2], down_weight)
    mixed_a_moved, mixed_a[1], mixed_sent0, grad_a, *rest = sync(
        mixed_a_moved, mixed_a[1], mixed_sent0, *products, *grad_b_moved
    )
    parts, grad_b_moved = rest[:4], rest[4:]

    grad_a_moved = row_moves(grad_a)
    sent, mixed_b = chip_part(parts)
    mixed_b_moved = swap(jnp.concatenate(sent, axis=0), CHIP)
    grad3, grad2 = pair_sums(grad_b, grad_b_moved)
    grads3, grads2 = grads_of(gate3, up3, grad3), grads_of(gate2, up2, grad2)
    parts = expand([[x, y] for x, y in zip(grads3, grads2)], pair)
    mixed_b_moved, mixed_b[1], *rest = sync(mixed_b_moved, mixed_b[1], *parts, *grad_a_moved)
    parts, grad_a_moved = rest[:4], rest[4:]

    sent, token_grad_b = chip_part(parts)
    token_b_moved = swap(jnp.concatenate(sent, axis=0), CHIP)
    grad0, grad1 = pair_sums(grad_a, grad_a_moved)
    size = tokens.shape[0]
    mixed_part3 = shift(narrow(block_sum(mixed_b, 0, mixed_b_moved[:size])), 1)
    mixed_part2 = shift(narrow(block_sum(mixed_b, 1, mixed_b_moved[size:])), -1)
    grads0, grads1 = grads_of(gate0, up0, grad0), grads_of(gate1, up1, grad1)
    parts = expand([[x, y] for x, y in zip(grads0, grads1)], pair)
    token_b_moved, token_grad_b[1], mixed_part3, mixed_part2, *parts = sync(
        token_b_moved, token_grad_b[1], mixed_part3, mixed_part2, *parts
    )

    (token_sent0, sent), token_grad_a = chip_part(parts)
    token_a_moved = swap(sent, CHIP)
    part3 = shift(narrow(block_sum(token_grad_b, 0, token_b_moved[:size])), 1)
    part2 = shift(narrow(block_sum(token_grad_b, 1, token_b_moved[size:])), -1)
    down_total = tall_grad(
        cot0 + cot1 + cot3 + cot2, [after(hidden0, sent), hidden1, hidden3, hidden2]
    )
    token_a_moved, token_grad_a[1], token_sent0, part2, part3, down_total = sync(
        token_a_moved, token_grad_a[1], token_sent0, part2, part3, down_total
    )

    moved0 = swap(jnp.concatenate([mixed_sent0, token_sent0], axis=0), CHIP)
    back = [
        block_sum(mixed_a, 1, mixed_a_moved, mixed_part2),
        block_sum(token_grad_a, 1, token_a_moved, part2),
    ]
    back = shift(narrow(jnp.concatenate(back, axis=0)), -1)
    gate_total, up_total = wide_grads(
        [after(tokens, down_total), *token0[1:], *token1, *token3, *token2],
        [grads0[0], grads1[0], grads3[0], grads2[0]],
        [grads0[1], grads1[1], grads3[1], grads2[1]],
    )
    moved0, back, mixed_part3, part3, gate_total = sync(
        moved0, back, mixed_part3, part3, gate_total
    )
    mixed = block_sum(mixed_a, 0, moved0[:size], mixed_part3, back[:size])
    token_grad = block_sum(token_grad_a, 0, moved0[size:], part3, back[size:])
    return (mixed, token_grad, gate_total, up_total, down_total)


def solution(mesh):
    activations = P(("depth", "col"), "row")
    wide_weight = P("row", ("col", "depth"))
    tall_weight = P(("col", "depth"), "row")
    return jax.shard_map(
        body,
        mesh=mesh,
        in_specs=(activations, wide_weight, wide_weight, tall_weight, activations),
        out_specs=(activations, activations, wide_weight, wide_weight, tall_weight),
        check_vma=False,
    )
```
